32 devices in a mesh: node: 4 (over y, x), local: 4 (over z), edata: 2 (over core).
Axes of the slice: x: 2, y: 2, z: 4, core: 2. Of those that a mesh axis runs over, the one named last changes fastest.
Arguments:
- tokens: bfloat16 [8192, 2048], P(('node', 'local', 'edata')), may hold values from -6 to 6
- out_grad: bfloat16 [8192, 2048], P(('node', 'local', 'edata')), may hold values from -6 to 6
- expert_ids: int32 [8192, 8], P(('node', 'local', 'edata')), may hold values from 0 to 63, as said below
- gates: float32 [8192, 8], P(('node', 'local', 'edata')), may hold values from 0.05 to 0.45
- w_gate_up: bfloat16 [16, 2048, 1536], P(('node', 'local'), 'edata'), may hold values from -0.125 to 0.125
- w_down: bfloat16 [16, 2048, 768], P(('node', 'local'), 'edata'), may hold values from -0.21875 to 0.21875
Outputs:
- mixed: bfloat16 [8192, 2048], P(('node', 'local', 'edata'))
- token_grad: bfloat16 [8192, 2048], P(('node', 'local', 'edata'))
- gate_grad: float32 [8192, 8], P(('node', 'local', 'edata'))
- grad_gate_up: float32 [16, 2048, 1536], P(('node', 'local'), 'edata')
- grad_down: float32 [16, 2048, 768], P(('node', 'local'), 'edata')
The draws below stay inside these ranges and needn't reach their ends.
Inputs may be any that keep to these rules, and one draw needn't show every extreme that they name: `expert_ids`: each row names 8 different experts. Expert e is held by node (e mod 16) // 4, and the experts of one row lie on at most 2 nodes.
All inputs are finite; a program needn't handle non-finite values.
Results may differ from the reference program's by a relative error of at most 0.0064.
Values may be sent and summed in bfloat16 or wider, within the bound.
No kernel may reach another device: no remote copies, remote signals or barrier semaphores. Data moves between devices by JAX's collectives and lax.ppermute only.
A program may use at most 128 MiB of HBM per device.

```python
import jax
import jax.numpy as jnp
from jax import lax

D = 2048
H = 768
TOP = 8
EXP_DEV = 4
NODE_LIMIT = 2
TOK_DEV = 256
EXPERTS = 64
GROUPS = 16
CAPACITY = 32
TOKENS = 8192
N_NODE = 4
N_LOCAL = 4
N_EDATA = 2


def draw_expert_ids(key, part):
    key = jax.random.fold_in(key, 7)
    key_hot, key_node, key_level, key_pick = jax.random.split(key, 4)
    per_node = EXP_DEV * N_LOCAL
    hot_expert = jax.random.randint(key_hot, (), 0, GROUPS)
    hot_node = hot_expert // N_LOCAL
    node_ids = jnp.arange(N_NODE, dtype=jnp.int32)
    node_score = jax.random.randint(key_node, (TOKENS, N_NODE), 0, 1 << 20) * N_NODE + node_ids[None, :]
    forced = (jnp.arange(TOKENS) % TOK_DEV % 2 == 0)[:, None] & (node_ids[None, :] == hot_node)
    node_score = jnp.where(forced, 1 << 26, node_score)
    chosen_nodes = lax.top_k(node_score, NODE_LIMIT)[1].astype(jnp.int32)
    candidate = jnp.arange(per_node, dtype=jnp.int32)
    node_table = candidate[None, :] // N_LOCAL * GROUPS + node_ids[:, None] * N_LOCAL + candidate[None, :] % N_LOCAL
    load_level = jax.random.randint(key_level, (EXPERTS,), 0, 4)
    load_bias = load_level * (1 << 14) + jnp.where(jnp.arange(EXPERTS) == hot_expert, 1 << 20, 0)
    options = node_table[chosen_nodes]
    pick_score = (jax.random.randint(key_pick, (TOKENS, NODE_LIMIT, per_node), 0, 1 << 16) + load_bias[options]) * per_node + candidate
    picked = lax.top_k(pick_score, TOP // NODE_LIMIT)[1]
    selected = jnp.take_along_axis(options, picked, axis=2)
    return selected.reshape(TOKENS, TOP).astype(jnp.int32)


def steps_of(own_key, extent, cuts, low, high):
    def one(axis_at, blocks):
        steps = jax.random.uniform(jax.random.fold_in(jax.random.fold_in(own_key, 6), axis_at), (blocks,), jnp.float32, low / len(cuts), high / len(cuts))
        return jnp.repeat(jnp.exp(steps), extent[axis_at] // blocks).reshape((-1,) + (1,) * (len(extent) - axis_at - 1))

    gain = one(*cuts[0])
    for cut in cuts[1:]:
        gain = gain * one(*cut)
    return gain


def noise(rng, dims, spread, bound, cuts=(), kind=jnp.bfloat16):
    array = jax.random.normal(rng, dims, jnp.float32) * spread
    if len(cuts) > 0:
        array = steps_of(rng, dims, cuts, -0.22, 0.18) * array
    return jnp.clip(array, min=-bound, max=bound).astype(kind)


def setup_inputs(seed: int = 0) -> dict:
    splits = jax.random.split(jax.random.key(seed), 7)
    return {
        "tokens": noise(splits[0], (TOKENS, D), 1.0, 6.0, ((0, 32),)),
        "out_grad": noise(splits[1], (TOKENS, D), 1.0, 6.0, ((0, 32),)),
        "expert_ids": draw_expert_ids(jax.random.fold_in(splits[6], 71), 0),
        "gates": jnp.clip(0.05 + 0.39999999 * jax.random.uniform(splits[3], (TOKENS, TOP), jnp.float32) ** steps_of(splits[3], (TOKENS, TOP), ((0, 32),), -0.2, 0.2), 0.05, 0.45),
        "w_gate_up": noise(splits[4], (GROUPS, D, 2 * H), D ** -0.5, 0.125, ((0, 16), (1, 2))),
        "w_down": noise(splits[5], (GROUPS, D, H), H ** -0.5, 0.21875, ((0, 16), (1, 2))),
    }


def expert_rows(x_rows, dy_rows, w_in, w_out):
    hidden = w_out.shape[1]
    activation = jnp.dot(x_rows, w_in, preferred_element_type=jnp.float32)
    act_gate = activation[:, :hidden]
    act_up = activation[:, hidden:]
    sigmoid_gate = jax.nn.sigmoid(act_gate)
    swished = act_gate * sigmoid_gate
    inner_act = (swished * act_up).astype(jnp.bfloat16)
    expert_out = lax.dot_general(inner_act, w_out, (((1,), (1,)), ((), ())), preferred_element_type=jnp.float32).astype(jnp.bfloat16)
    inner_grad = jnp.dot(dy_rows, w_out, preferred_element_type=jnp.float32)
    grad_gate_part = inner_grad * act_up * sigmoid_gate * (1.0 + act_gate * (1.0 - sigmoid_gate))
    grad_up_part = inner_grad * swished
    act_grad = jnp.concatenate([grad_gate_part, grad_up_part], axis=1).astype(jnp.bfloat16)
    copy_grad = lax.dot_general(act_grad, w_in, (((1,), (1,)), ((), ())), preferred_element_type=jnp.float32).astype(jnp.bfloat16)
    return inner_act, expert_out, act_grad, copy_grad


def by_replica(values):
    shaped = values.reshape(GROUPS, N_EDATA, CAPACITY, values.shape[-1])
    return jnp.transpose(shaped, (1, 0, 2, 3)).reshape(N_EDATA, GROUPS * CAPACITY, values.shape[-1])


def replica_part(operands):
    x_part, act_part, dy_part, inner_part = operands
    grad_first = jnp.dot(x_part.T, act_part, preferred_element_type=jnp.float32).astype(jnp.bfloat16)
    second = jnp.dot(dy_part.T, inner_part, preferred_element_type=jnp.float32).astype(jnp.bfloat16)
    return grad_first, second


def reference(tokens, out_grad, expert_ids, gates, w_gate_up, w_down):
    device_total = N_NODE * N_LOCAL * N_EDATA
    numbers = jnp.arange(GROUPS, dtype=jnp.int32)
    chosen = expert_ids[:, :, None] == numbers[None, None, :]
    routed = jnp.sum(chosen.astype(jnp.int32), axis=1).astype(jnp.int32)
    block_route = routed.reshape(device_total, TOK_DEV, GROUPS)
    order_in = (jnp.cumsum(block_route, axis=1) - block_route).astype(jnp.int32)
    retained = (block_route > 0) & (order_in < CAPACITY)
    retained_flat = retained.reshape(TOKENS, GROUPS)
    weight = jnp.sum(jnp.where(chosen, gates[:, :, None], jnp.zeros((), jnp.float32)), axis=1)
    weight = jnp.where(retained_flat, weight, jnp.zeros((), jnp.float32))
    device_index = jnp.broadcast_to(jnp.arange(device_total, dtype=jnp.int32)[:, None, None], retained.shape)
    group_index = jnp.broadcast_to(numbers[None, None, :], retained.shape)
    token_numbers = (jnp.arange(device_total, dtype=jnp.int32)[:, None] * TOK_DEV + jnp.arange(TOK_DEV, dtype=jnp.int32)[None, :]).astype(jnp.int32)
    token_index = jnp.broadcast_to(token_numbers[:, :, None], retained.shape)
    slot_index = jnp.where(retained, order_in, CAPACITY).astype(jnp.int32)
    slot_token = jnp.zeros((device_total, GROUPS, CAPACITY), jnp.int32).at[device_index, group_index, slot_index].set(token_index, mode="drop")
    slot_live = jnp.zeros((device_total, GROUPS, CAPACITY), jnp.int32).at[device_index, group_index, slot_index].set(jnp.ones_like(token_index), mode="drop")

    def per_expert(totals, expert):
        mixed_sum, grad_sum, gate_sum = totals
        row_index = slot_token[:, expert, :].reshape(-1)
        live_rows = slot_live[:, expert, :].reshape(-1) > 0
        x_rows = jnp.where(live_rows[:, None], tokens[row_index], jnp.zeros((), jnp.bfloat16))
        row_weight = jnp.where(live_rows, weight[row_index, expert], jnp.zeros((), jnp.float32))
        grad_rows = out_grad[row_index]
        dy_rows = (row_weight[:, None] * grad_rows.astype(jnp.float32)).astype(jnp.bfloat16)
        inner_act, expert_out, act_grad, copy_grad = expert_rows(x_rows, dy_rows, w_gate_up[expert], w_down[expert])
        out_wide = expert_out.astype(jnp.float32)
        mixed_sum = mixed_sum.at[row_index].add(row_weight[:, None] * out_wide)
        grad_sum = grad_sum.at[row_index].add(jnp.where(live_rows[:, None], copy_grad.astype(jnp.float32), jnp.zeros((), jnp.float32)))
        slot_dots = jnp.where(live_rows, jnp.sum(out_wide * grad_rows.astype(jnp.float32), axis=1), jnp.zeros((), jnp.float32))
        token_dots = jnp.zeros((TOKENS,), jnp.float32).at[row_index].add(slot_dots)
        gate_sum = gate_sum + jnp.where(expert_ids == expert, token_dots[:, None], jnp.zeros((), jnp.float32))
        replica_parts = lax.map(replica_part, (by_replica(x_rows), by_replica(act_grad), by_replica(dy_rows), by_replica(inner_act)))
        grad_in = jnp.sum(replica_parts[0].astype(jnp.float32), axis=0)
        grad_out = jnp.sum(replica_parts[1].astype(jnp.float32), axis=0)
        return (mixed_sum, grad_sum, gate_sum), (grad_in, grad_out)

    start_totals = (jnp.zeros((TOKENS, D), jnp.float32), jnp.zeros((TOKENS, D), jnp.float32), jnp.zeros((TOKENS, TOP), jnp.float32))
    totals, grads = lax.scan(per_expert, start_totals, numbers)
    mixed_sum, grad_sum, gate_sum = totals
    return mixed_sum.astype(jnp.bfloat16), grad_sum.astype(jnp.bfloat16), gate_sum, grads[0], grads[1]
```

```python
import jax
import jax.numpy as jnp
from jax import lax
from jax.sharding import PartitionSpec as P

EXP_DEV = 4
BF = jnp.bfloat16
F32 = jnp.float32


def slot_tables(expert_ids, gates, groups, capacity):
    tok_rows = expert_ids.shape[0]
    ids_t = expert_ids.T
    numbers = jnp.arange(groups, dtype=jnp.int32)
    chosen = ids_t[None, :, :] == numbers[:, None, None]
    routed = jnp.any(chosen, axis=1)
    earlier = jnp.arange(tok_rows)[:, None] < jnp.arange(tok_rows)[None, :]
    order_in = jnp.dot(
        routed.astype(BF), earlier.astype(BF), preferred_element_type=F32
    ).astype(jnp.int32)
    weight = jnp.sum(jnp.where(chosen, gates.T[None, :, :], 0.0), axis=1)
    slot_ids = jnp.arange(capacity, dtype=jnp.int32)
    hits = routed[:, None, :] & (order_in[:, None, :] == slot_ids[None, :, None])
    slot_weight = jnp.sum(jnp.where(hits, weight[:, None, :], 0.0), axis=2)
    return chosen, hits.reshape(groups * capacity, tok_rows), slot_weight.reshape(-1)


def exchange(rows, groups):
    shaped = rows.reshape(groups, rows.shape[0] // groups, rows.shape[1])
    out = lax.all_to_all(shaped, ("node", "local"), split_axis=0, concat_axis=0, tiled=True)
    return out.reshape(rows.shape)


def shards(tokens, out_grad, expert_ids, gates, w_gate_up, w_down):
    groups = lax.axis_size("node") * lax.axis_size("local")
    tok_rows, model_width = tokens.shape
    hidden = w_down.shape[2]
    capacity = tok_rows * expert_ids.shape[1] // (EXP_DEV * groups)
    chosen, hits, slot_weight = slot_tables(expert_ids, gates, groups, capacity)
    pick = hits.astype(BF)
    x_send = jnp.dot(pick, tokens, preferred_element_type=F32).astype(BF)
    x_recv = exchange(x_send, groups)
    grad_rows = jnp.dot(pick, out_grad, preferred_element_type=F32)
    dy_send = (slot_weight[:, None] * grad_rows).astype(BF)
    dy_recv = exchange(dy_send, groups)
    w_in = lax.all_gather(w_gate_up, "edata", axis=1, tiled=True)[0]
    w_out = lax.all_gather(w_down, "edata", axis=1, tiled=True)[0]

    activation = jnp.dot(x_recv, w_in, preferred_element_type=F32)
    act_gate = activation[:, :hidden]
    act_up = activation[:, hidden:]
    sigmoid_gate = jax.nn.sigmoid(act_gate)
    swished = act_gate * sigmoid_gate
    inner_act = (swished * act_up).astype(BF)
    expert_out = lax.dot_general(
        inner_act, w_out, (((1,), (1,)), ((), ())), preferred_element_type=F32
    ).astype(BF)
    y_back = exchange(expert_out, groups)

    inner_grad = jnp.dot(dy_recv, w_out, preferred_element_type=F32)
    grad_gate_part = inner_grad * act_up * sigmoid_gate * (1.0 + act_gate * (1.0 - sigmoid_gate))
    grad_up_part = inner_grad * swished
    act_grad = jnp.concatenate([grad_gate_part, grad_up_part], axis=1).astype(BF)
    copy_grad = lax.dot_general(
        act_grad, w_in, (((1,), (1,)), ((), ())), preferred_element_type=F32
    ).astype(BF)
    dx_back = exchange(copy_grad, groups)

    part_down = lax.dot_general(
        dy_recv, inner_act, (((0,), (0,)), ((), ())), preferred_element_type=F32
    ).astype(BF)
    grad_down = lax.psum_scatter(part_down, "edata", scatter_dimension=0, tiled=True).astype(F32)
    part_in = lax.dot_general(
        x_recv, act_grad, (((0,), (0,)), ((), ())), preferred_element_type=F32
    ).astype(BF)
    grad_in = lax.psum_scatter(part_in, "edata", scatter_dimension=0, tiled=True).astype(F32)

    spread = jnp.where(hits, slot_weight[:, None], 0.0)
    high = spread.astype(BF)
    rest = spread - high.astype(F32)
    middle = rest.astype(BF)
    low = (rest - middle.astype(F32)).astype(BF)
    over_slots = (((0,), (0,)), ((), ()))
    mixed = (
        lax.dot_general(high, y_back, over_slots, preferred_element_type=F32)
        + lax.dot_general(middle, y_back, over_slots, preferred_element_type=F32)
        + lax.dot_general(low, y_back, over_slots, preferred_element_type=F32)
    )
    slot_dots = jnp.sum(y_back.astype(F32) * grad_rows, axis=1)
    token_dots = jnp.sum(
        jnp.where(hits, slot_dots[:, None], 0.0).reshape(groups, capacity, tok_rows), axis=1
    )
    gate_grad = jnp.sum(jnp.where(chosen, token_dots[:, None, :], 0.0), axis=0).T
    token_grad = lax.dot_general(pick, dx_back, over_slots, preferred_element_type=F32)
    return (mixed.astype(BF), token_grad.astype(BF), gate_grad, grad_in[None], grad_down[None])


def solution(mesh):
    rows = P(("node", "local", "edata"), None)
    weights = P(("node", "local"), "edata", None)
    return jax.shard_map(
        shards,
        mesh=mesh,
        in_specs=(rows, rows, rows, rows, weights, weights),
        out_specs=(rows, rows, rows, weights, weights),
        check_vma=False,
    )
```

```python
import jax
import jax.numpy as jnp
from jax import lax
from jax.sharding import PartitionSpec as P

EXP_DEV = 4
BF = jnp.bfloat16
F32 = jnp.float32


def slot_tables(expert_ids, gates, groups, capacity):
    tok_rows = expert_ids.shape[0]
    ids_t = expert_ids.T
    numbers = jnp.arange(groups, dtype=jnp.int32)
    chosen = ids_t[None, :, :] == numbers[:, None, None]
    routed = jnp.any(chosen, axis=1)
    earlier = jnp.arange(tok_rows)[:, None] < jnp.arange(tok_rows)[None, :]
    order_in = jnp.dot(
        routed.astype(BF), earlier.astype(BF), preferred_element_type=F32
    ).astype(jnp.int32)
    weight = jnp.sum(jnp.where(chosen, gates.T[None, :, :], 0.0), axis=1)
    slot_ids = jnp.arange(capacity, dtype=jnp.int32)
    hits = routed[:, None, :] & (order_in[:, None, :] == slot_ids[None, :, None])
    slot_weight = jnp.sum(jnp.where(hits, weight[:, None, :], 0.0), axis=2)
    return chosen, hits.reshape(groups * capacity, tok_rows), slot_weight.reshape(-1)


def exchange(rows, groups):
    shaped = rows.reshape(groups, rows.shape[0] // groups, rows.shape[1])
    out = lax.all_to_all(shaped, ("node", "local"), split_axis=0, concat_axis=0, tiled=True)
    return out.reshape(rows.shape)


def shards(tokens, out_grad, expert_ids, gates, w_gate_up, w_down):
    groups = lax.axis_size("node") * lax.axis_size("local")
    tok_rows, model_width = tokens.shape
    hidden = w_down.shape[2]
    capacity = tok_rows * expert_ids.shape[1] // (EXP_DEV * groups)
    chosen, hits, slot_weight = slot_tables(expert_ids, gates, groups, capacity)
    pick = hits.astype(BF)
    x_send = jnp.dot(pick, tokens, preferred_element_type=F32).astype(BF)
    x_recv = exchange(x_send, groups)
    grad_rows = jnp.dot(pick, out_grad, preferred_element_type=F32)
    dy_send = (slot_weight[:, None] * grad_rows).astype(BF)
    dy_recv = exchange(dy_send, groups)
    w_in = lax.all_gather(w_gate_up, "edata", axis=1, tiled=True)[0]
    w_out = lax.all_gather(w_down, "edata", axis=1, tiled=True)[0]

    activation = jnp.dot(x_recv, w_in, preferred_element_type=F32)
    act_gate = activation[:, :hidden]
    act_up = activation[:, hidden:]
    sigmoid_gate = jax.nn.sigmoid(act_gate)
    swished = act_gate * sigmoid_gate
    inner_act = (swished * act_up).astype(BF)
    expert_out = lax.dot_general(
        inner_act, w_out, (((1,), (1,)), ((), ())), preferred_element_type=F32
    ).astype(BF)
    expert_out, dy_recv = lax.optimization_barrier((expert_out, dy_recv))
    y_back = exchange(expert_out, groups)

    inner_grad = jnp.dot(dy_recv, w_out, preferred_element_type=F32)
    grad_gate_part = inner_grad * act_up * sigmoid_gate * (1.0 + act_gate * (1.0 - sigmoid_gate))
    grad_up_part = inner_grad * swished
    act_grad = jnp.concatenate([grad_gate_part, grad_up_part], axis=1).astype(BF)
    copy_grad = lax.dot_general(
        act_grad, w_in, (((1,), (1,)), ((), ())), preferred_element_type=F32
    ).astype(BF)
    copy_grad, y_back = lax.optimization_barrier((copy_grad, y_back))
    dx_back = exchange(copy_grad, groups)

    part_down = lax.dot_general(
        dy_recv, inner_act, (((0,), (0,)), ((), ())), preferred_element_type=F32
    ).astype(BF)
    grad_down = lax.psum_scatter(part_down, "edata", scatter_dimension=0, tiled=True).astype(F32)
    part_in = lax.dot_general(
        x_recv, act_grad, (((0,), (0,)), ((), ())), preferred_element_type=F32
    ).astype(BF)
    grad_in = lax.psum_scatter(part_in, "edata", scatter_dimension=0, tiled=True).astype(F32)

    spread = jnp.where(hits, slot_weight[:, None], 0.0)
    high = lax.reduce_precision(spread, 8, 7)
    middle = lax.reduce_precision(spread - high, 8, 7)
    low = spread - high - middle
    high, middle, low = high.astype(BF), middle.astype(BF), low.astype(BF)
    over_slots = (((0,), (0,)), ((), ()))
    mixed = (
        lax.dot_general(high, y_back, over_slots, preferred_element_type=F32)
        + lax.dot_general(middle, y_back, over_slots, preferred_element_type=F32)
        + lax.dot_general(low, y_back, over_slots, preferred_element_type=F32)
    )
    slot_dots = jnp.sum(y_back.astype(F32) * grad_rows, axis=1)
    token_dots = jnp.sum(
        jnp.where(hits, slot_dots[:, None], 0.0).reshape(groups, capacity, tok_rows), axis=1
    )
    gate_grad = jnp.sum(jnp.where(chosen, token_dots[:, None, :], 0.0), axis=0).T
    dx_back, grad_in, grad_down = lax.optimization_barrier((dx_back, grad_in, grad_down))
    token_grad = lax.dot_general(pick, dx_back, over_slots, preferred_element_type=F32)
    return (mixed.astype(BF), token_grad.astype(BF), gate_grad, grad_in[None], grad_down[None])


def solution(mesh):
    rows = P(("node", "local", "edata"), None)
    weights = P(("node", "local"), "edata", None)
    return jax.shard_map(
        shards,
        mesh=mesh,
        in_specs=(rows, rows, rows, rows, weights, weights),
        out_specs=(rows, rows, rows, weights, weights),
        check_vma=False,
    )
```

```python
import jax
import jax.numpy as jnp
from jax import lax
from jax.sharding import PartitionSpec as P

EXP_DEV = 4
BF = jnp.bfloat16
F32 = jnp.float32
ROWS_IN = (((0,), (0,)), ((), ()))
COLS_IN = (((1,), (1,)), ((), ()))


def slot_tables(expert_ids, gates, numbers, capacity):
    tok_rows = expert_ids.shape[0]
    groups = numbers.shape[0]
    ids_t = expert_ids.T
    chosen = ids_t[None, :, :] == numbers[:, None, None]
    routed = jnp.any(chosen, axis=1)
    earlier = jnp.arange(tok_rows)[:, None] < jnp.arange(tok_rows)[None, :]
    order_in = jnp.dot(
        routed.astype(BF), earlier.astype(BF), preferred_element_type=F32
    ).astype(jnp.int32)
    weight = jnp.sum(jnp.where(chosen, gates.T[None, :, :], 0.0), axis=1)
    slot_ids = jnp.arange(capacity, dtype=jnp.int32)
    hits = routed[:, None, :] & (order_in[:, None, :] == slot_ids[None, :, None])
    slot_weight = jnp.sum(jnp.where(hits, weight[:, None, :], 0.0), axis=2)
    return chosen, hits.reshape(groups * capacity, tok_rows), slot_weight.reshape(-1)


def exchange(rows, groups):
    size = rows.shape[0] // groups
    blocks = [rows[:size]]
    for j in range(1, groups):
        pairs = [(i, i ^ j) for i in range(groups)]
        blocks.append(lax.ppermute(rows[j * size : (j + 1) * size], ("node", "local"), pairs))
    return jnp.concatenate(blocks, axis=0)


def gathered(shard):
    count = lax.axis_size("edata")
    shards = [shard]
    for step in range(1, count):
        pairs = [((i + step) % count, i) for i in range(count)]
        shards.append(lax.ppermute(shard, "edata", pairs))
    return jnp.concatenate(shards, axis=0)


def reduced(part):
    count = lax.axis_size("edata")
    size = part.shape[0] // count
    total = part[:size].astype(F32)
    for step in range(1, count):
        pairs = [(i, (i + step) % count) for i in range(count)]
        piece = lax.ppermute(part[step * size : (step + 1) * size], "edata", pairs)
        total = total + piece.astype(F32)
    return total


def shards(tokens, out_grad, expert_ids, gates, w_gate_up, w_down):
    groups = lax.axis_size("node") * lax.axis_size("local")
    tok_rows, model_width = tokens.shape
    hidden = w_down.shape[2]
    capacity = tok_rows * expert_ids.shape[1] // (EXP_DEV * groups)
    me = lax.axis_index(("node", "local"))
    turn = lax.axis_index("edata") * w_down.shape[1]
    numbers = me ^ jnp.arange(groups, dtype=jnp.int32)
    w_in = gathered(w_gate_up[0])
    w_out = gathered(w_down[0])
    chosen, hits, slot_weight = slot_tables(expert_ids, gates, numbers, capacity)
    pick = hits.astype(BF)
    tokens = jnp.roll(tokens, -turn, axis=1)
    out_grad = jnp.roll(out_grad, -turn, axis=1)
    x_send = jnp.dot(pick, tokens, preferred_element_type=F32).astype(BF)
    x_recv = exchange(x_send, groups)
    grad_rows = jnp.dot(pick, out_grad, preferred_element_type=F32)
    dy_send = (slot_weight[:, None] * grad_rows).astype(BF)
    dy_recv = exchange(dy_send, groups)

    activation = jnp.dot(x_recv, w_in, preferred_element_type=F32)
    act_gate = activation[:, :hidden]
    act_up = activation[:, hidden:]
    sigmoid_gate = jax.nn.sigmoid(act_gate)
    swished = act_gate * sigmoid_gate
    inner_act = (swished * act_up).astype(BF)
    expert_out = lax.dot_general(inner_act, w_out, COLS_IN, preferred_element_type=F32).astype(BF)
    expert_out, dy_recv = lax.optimization_barrier((expert_out, dy_recv))
    y_back = exchange(expert_out, groups)

    inner_grad = jnp.dot(dy_recv, w_out, preferred_element_type=F32)
    grad_gate_part = inner_grad * act_up * sigmoid_gate * (1.0 + act_gate * (1.0 - sigmoid_gate))
    grad_up_part = inner_grad * swished
    act_grad = jnp.concatenate([grad_gate_part, grad_up_part], axis=1).astype(BF)
    copy_grad = lax.dot_general(act_grad, w_in, COLS_IN, preferred_element_type=F32).astype(BF)
    copy_grad, y_back = lax.optimization_barrier((copy_grad, y_back))
    dx_back = exchange(copy_grad, groups)

    part_down = lax.dot_general(dy_recv, inner_act, ROWS_IN, preferred_element_type=F32).astype(BF)
    grad_down = reduced(part_down)
    part_in = lax.dot_general(x_recv, act_grad, ROWS_IN, preferred_element_type=F32).astype(BF)
    grad_in = reduced(part_in)

    spread = jnp.where(hits, slot_weight[:, None], 0.0)
    high = lax.reduce_precision(spread, 8, 7)
    middle = lax.reduce_precision(spread - high, 8, 7)
    low = spread - high - middle
    high, middle, low = high.astype(BF), middle.astype(BF), low.astype(BF)
    mixed = (
        lax.dot_general(high, y_back, ROWS_IN, preferred_element_type=F32)
        + lax.dot_general(middle, y_back, ROWS_IN, preferred_element_type=F32)
        + lax.dot_general(low, y_back, ROWS_IN, preferred_element_type=F32)
    ).astype(BF)
    slot_dots = jnp.sum(y_back.astype(F32) * grad_rows, axis=1)
    token_dots = jnp.sum(
        jnp.where(hits, slot_dots[:, None], 0.0).reshape(groups, capacity, tok_rows), axis=1
    )
    gate_grad = jnp.sum(jnp.where(chosen, token_dots[:, None, :], 0.0), axis=0).T
    dx_back, grad_in, grad_down = lax.optimization_barrier((dx_back, grad_in, grad_down))
    token_grad = lax.dot_general(pick, dx_back, ROWS_IN, preferred_element_type=F32).astype(BF)
    mixed = jnp.roll(mixed, turn, axis=1)
    token_grad = jnp.roll(token_grad, turn, axis=1)
    return (mixed, token_grad, gate_grad, grad_in[None], grad_down[None])


def solution(mesh):
    rows = P(("node", "local", "edata"), None)
    weights = P(("node", "local"), "edata", None)
    return jax.shard_map(
        shards,
        mesh=mesh,
        in_specs=(rows, rows, rows, rows, weights, weights),
        out_specs=(rows, rows, rows, weights, weights),
        check_vma=False,
    )
```

```python
import jax
import jax.numpy as jnp
from jax import lax
from jax.experimental import pallas as pl
from jax.experimental.pallas import tpu as pltpu
from jax.sharding import PartitionSpec as P

EXP_DEV = 4
BF = jnp.bfloat16
F32 = jnp.float32
ROWS_IN = (((0,), (0,)), ((), ()))
COLS_IN = (((1,), (1,)), ((), ()))
LIMIT = 48 * 1024 * 1024
CHEAP = pl.CostEstimate(flops=1, bytes_accessed=1, transcendentals=0)


def slot_tables(expert_ids, gates, groups, capacity):
    tok_rows = expert_ids.shape[0]
    numbers = jnp.arange(groups, dtype=jnp.int32)
    ids_t = expert_ids.T
    chosen = ids_t[None, :, :] == numbers[:, None, None]
    routed = jnp.any(chosen, axis=1)
    earlier = jnp.arange(tok_rows)[:, None] < jnp.arange(tok_rows)[None, :]
    order_in = jnp.dot(
        routed.astype(BF), earlier.astype(BF), preferred_element_type=F32
    ).astype(jnp.int32)
    weight = jnp.sum(jnp.where(chosen, gates.T[None, :, :], 0.0), axis=1)
    slot_ids = jnp.arange(capacity, dtype=jnp.int32)
    hits = routed[:, None, :] & (order_in[:, None, :] == slot_ids[None, :, None])
    slot_weight = jnp.sum(jnp.where(hits, weight[:, None, :], 0.0), axis=2)
    return chosen, hits.reshape(groups * capacity, tok_rows), slot_weight.reshape(-1)


def exchange(rows, groups):
    shaped = rows.reshape(groups, rows.shape[0] // groups, rows.shape[1])
    out = lax.all_to_all(shaped, ("node", "local"), split_axis=0, concat_axis=0, tiled=True)
    return out.reshape(rows.shape)


def gathered(shard):
    count = lax.axis_size("edata")
    shards = [shard]
    for step in range(1, count):
        pairs = [((i + step) % count, i) for i in range(count)]
        shards.append(lax.ppermute(shard, "edata", pairs))
    return shards


def reduced(part):
    count = lax.axis_size("edata")
    size = part.shape[0] // count
    total = part[:size].astype(F32)
    for step in range(1, count):
        pairs = [(i, (i + step) % count) for i in range(count)]
        piece = lax.ppermute(part[step * size : (step + 1) * size], "edata", pairs)
        total = total + piece.astype(F32)
    return total


def backward_kernel(count, act_ref, dy_ref, *refs):
    outs, ins = refs[:count], refs[count : 2 * count]
    act_grad_ref, dx_ref = refs[2 * count :]
    hidden = act_ref.shape[1] // 2
    width = dy_ref.shape[1] // count
    inner_grad = jnp.dot(dy_ref[:, :width], outs[0][...], preferred_element_type=F32)
    for s in range(1, count):
        inner_grad += jnp.dot(
            dy_ref[:, s * width : (s + 1) * width], outs[s][...], preferred_element_type=F32
        )
    act_gate = act_ref[:, :hidden]
    act_up = act_ref[:, hidden:]
    sig = jax.nn.sigmoid(act_gate)
    act_grad_ref[:, :hidden] = (
        inner_grad * act_up * sig * (1.0 + act_gate * (1.0 - sig))
    ).astype(BF)
    act_grad_ref[:, hidden:] = (inner_grad * (act_gate * sig)).astype(BF)
    for s in range(count):
        dx_ref[:, s * width : (s + 1) * width] = lax.dot_general(
            act_grad_ref[...], ins[s][...], COLS_IN, preferred_element_type=F32
        ).astype(BF)


def expert_backward(activation, dy_recv, w_outs, w_ins):
    rows, width = dy_recv.shape
    double = activation.shape[1]
    block = min(rows, 256)

    def whole(shard):
        return pl.BlockSpec(shard.shape, lambda i: (0, 0), pipeline_mode=pl.Buffered(1))

    def band(columns):
        return pl.BlockSpec((block, columns), lambda i: (i, 0))

    return pl.pallas_call(
        lambda *refs: backward_kernel(len(w_ins), *refs),
        grid=(rows // block,),
        in_specs=[band(double), band(width)] + [whole(s) for s in (*w_outs, *w_ins)],
        out_specs=[band(double), band(width)],
        out_shape=[
            jax.ShapeDtypeStruct((rows, double), BF),
            jax.ShapeDtypeStruct((rows, width), BF),
        ],
        compiler_params=pltpu.CompilerParams(vmem_limit_bytes=LIMIT),
        cost_estimate=CHEAP,
        name="expert_backward",
    )(activation, dy_recv, *w_outs, *w_ins)


def combine_kernel(turn_ref, pick_ref, rows_ref, out_ref):
    out_ref[...] = lax.dot_general(
        pick_ref[...], rows_ref[...], ROWS_IN, preferred_element_type=F32
    ).astype(BF)


def combine(pick, rows, position):
    slots, tok_rows = pick.shape
    width = rows.shape[1]
    count = lax.axis_size("edata")
    tile = min(512, width // count)
    steps = width // tile
    per_shard = steps // count
    return pl.pallas_call(
        combine_kernel,
        grid_spec=pltpu.PrefetchScalarGridSpec(
            num_scalar_prefetch=1,
            grid=(steps,),
            in_specs=[
                pl.BlockSpec((slots, tok_rows), lambda i, t: (0, 0)),
                pl.BlockSpec((slots, tile), lambda i, t: (0, i)),
            ],
            out_specs=pl.BlockSpec((tok_rows, tile), lambda i, t: (0, (i + t[0]) % steps)),
        ),
        out_shape=jax.ShapeDtypeStruct((tok_rows, width), BF),
        compiler_params=pltpu.CompilerParams(vmem_limit_bytes=LIMIT),
        cost_estimate=CHEAP,
        name="combine",
    )((position * per_shard).astype(jnp.int32).reshape(1), pick, rows)


def shards(tokens, out_grad, expert_ids, gates, w_gate_up, w_down):
    groups = lax.axis_size("node") * lax.axis_size("local")
    tok_rows, model_width = tokens.shape
    hidden = w_down.shape[2]
    capacity = tok_rows * expert_ids.shape[1] // (EXP_DEV * groups)
    position = lax.axis_index("edata")
    turn = position * w_down.shape[1]
    w_ins = gathered(w_gate_up[0])
    w_outs = gathered(w_down[0])
    chosen, hits, slot_weight = slot_tables(expert_ids, gates, groups, capacity)
    pick = hits.astype(BF)
    x_send = jnp.dot(pick, jnp.roll(tokens, -turn, axis=1), preferred_element_type=F32).astype(BF)
    x_recv = exchange(x_send, groups)
    grad_rows = jnp.dot(pick, jnp.roll(out_grad, -turn, axis=1), preferred_element_type=F32)
    dy_send = (slot_weight[:, None] * grad_rows).astype(BF)
    dy_recv = exchange(dy_send, groups)

    w_in = jnp.concatenate(w_ins, axis=0)
    w_out = jnp.concatenate(w_outs, axis=0)
    activation = jnp.dot(x_recv, w_in, preferred_element_type=F32)
    act_gate = activation[:, :hidden]
    act_up = activation[:, hidden:]
    inner_act = (act_gate * jax.nn.sigmoid(act_gate) * act_up).astype(BF)
    expert_out = lax.dot_general(inner_act, w_out, COLS_IN, preferred_element_type=F32).astype(BF)
    expert_out, dy_recv = lax.optimization_barrier((expert_out, dy_recv))
    y_back = exchange(expert_out, groups)

    act_grad, copy_grad = expert_backward(activation, dy_recv, w_outs, w_ins)
    copy_grad, y_back = lax.optimization_barrier((copy_grad, y_back))
    dx_back = exchange(copy_grad, groups)

    dy_recv, act_grad = lax.optimization_barrier((dy_recv, act_grad))
    part_down = lax.dot_general(dy_recv, inner_act, ROWS_IN, preferred_element_type=F32).astype(BF)
    grad_down = reduced(part_down)
    part_in = lax.dot_general(x_recv, act_grad, ROWS_IN, preferred_element_type=F32).astype(BF)
    grad_in = reduced(part_in)

    spread = jnp.where(hits, slot_weight[:, None], 0.0)
    high = lax.reduce_precision(spread, 8, 7)
    middle = lax.reduce_precision(spread - high, 8, 7)
    low = spread - high - middle
    high, middle, low = high.astype(BF), middle.astype(BF), low.astype(BF)
    mixed = (
        lax.dot_general(high, y_back, ROWS_IN, preferred_element_type=F32)
        + lax.dot_general(middle, y_back, ROWS_IN, preferred_element_type=F32)
        + lax.dot_general(low, y_back, ROWS_IN, preferred_element_type=F32)
    ).astype(BF)
    mixed = jnp.roll(mixed, turn, axis=1)
    slot_dots = jnp.sum(y_back.astype(F32) * grad_rows, axis=1)
    token_dots = jnp.sum(
        jnp.where(hits, slot_dots[:, None], 0.0).reshape(groups, capacity, tok_rows), axis=1
    )
    gate_grad = jnp.sum(jnp.where(chosen, token_dots[:, None, :], 0.0), axis=0).T
    dx_back, grad_in, grad_down, mixed, gate_grad = lax.optimization_barrier(
        (dx_back, grad_in, grad_down, mixed, gate_grad)
    )
    token_grad = combine(pick, dx_back, position)
    return (mixed, token_grad, gate_grad, grad_in[None], grad_down[None])


def solution(mesh):
    rows = P(("node", "local", "edata"), None)
    weights = P(("node", "local"), "edata", None)
    return jax.shard_map(
        shards,
        mesh=mesh,
        in_specs=(rows, rows, rows, rows, weights, weights),
        out_specs=(rows, rows, rows, weights, weights),
        check_vma=False,
    )
```

```python
import jax
import jax.numpy as jnp
from jax import lax
from jax.experimental import pallas as pl
from jax.experimental.pallas import tpu as pltpu
from jax.sharding import PartitionSpec as P

EXP_DEV = 4
BF = jnp.bfloat16
F32 = jnp.float32
ROWS_IN = (((0,), (0,)), ((), ()))
COLS_IN = (((1,), (1,)), ((), ()))
LIMIT = 48 * 1024 * 1024
CHEAP = pl.CostEstimate(flops=1, bytes_accessed=1, transcendentals=0)


def slot_tables(expert_ids, gates, numbers, capacity):
    tok_rows = expert_ids.shape[0]
    ids_t = expert_ids.T
    chosen = ids_t[None, :, :] == numbers[:, None, None]
    routed = jnp.any(chosen, axis=1)
    earlier = jnp.arange(tok_rows)[:, None] < jnp.arange(tok_rows)[None, :]
    order_in = jnp.dot(
        routed.astype(BF), earlier.astype(BF), preferred_element_type=F32
    ).astype(jnp.int32)
    weight = jnp.sum(jnp.where(chosen, gates.T[None, :, :], 0.0), axis=1)
    slot_ids = jnp.arange(capacity, dtype=jnp.int32)
    hits = routed[:, None, :] & (order_in[:, None, :] == slot_ids[None, :, None])
    slot_weight = jnp.sum(jnp.where(hits, weight[:, None, :], 0.0), axis=2)
    return chosen, hits.reshape(numbers.shape[0] * capacity, tok_rows), slot_weight.reshape(-1)


def after(value, *others):
    return lax.optimization_barrier((value, *others))[0]


def to_plane(rows, distance):
    if distance == 0:
        return rows
    pairs = [(i, i ^ distance) for i in range(lax.axis_size("local"))]
    return lax.ppermute(rows, "local", pairs)


def over_nodes(rows):
    nodes = lax.axis_size("node")
    shaped = rows.reshape(nodes, rows.shape[0] // nodes, rows.shape[1])
    out = lax.all_to_all(shaped, "node", split_axis=0, concat_axis=0, tiled=True)
    return out.reshape(rows.shape)


def joined(planes):
    nodes = lax.axis_size("node")
    width = planes[0].shape[1]
    parts = [p.reshape(nodes, -1, width) for p in planes]
    return jnp.concatenate(parts, axis=1).reshape(-1, width)


def parted(rows, count):
    nodes = lax.axis_size("node")
    width = rows.shape[1]
    shaped = rows.reshape(nodes, count, -1, width)
    return [shaped[:, i].reshape(-1, width) for i in range(count)]


def gathered(shard):
    count = lax.axis_size("edata")
    shards = [shard]
    for step in range(1, count):
        pairs = [((i + step) % count, i) for i in range(count)]
        shards.append(lax.ppermute(shard, "edata", pairs))
    return shards


def reduced(part):
    count = lax.axis_size("edata")
    size = part.shape[0] // count
    total = part[:size].astype(F32)
    for step in range(1, count):
        pairs = [(i, (i + step) % count) for i in range(count)]
        piece = lax.ppermute(part[step * size : (step + 1) * size], "edata", pairs)
        total = total + piece.astype(F32)
    return total


def whole(array):
    return pl.BlockSpec(array.shape, lambda i: (0, 0), pipeline_mode=pl.Buffered(1))


def forward_kernel(count, x_ref, *refs):
    ins, outs = refs[:count], refs[count : 2 * count]
    act_ref, inner_ref, y_ref = refs[2 * count :]
    hidden = inner_ref.shape[1]
    width = x_ref.shape[1] // count
    activation = jnp.dot(x_ref[:, :width], ins[0][...], preferred_element_type=F32)
    for s in range(1, count):
        activation += jnp.dot(
            x_ref[:, s * width : (s + 1) * width], ins[s][...], preferred_element_type=F32
        )
    act_ref[...] = activation
    act_gate = act_ref[:, :hidden]
    inner_ref[...] = (act_gate * jax.nn.sigmoid(act_gate) * act_ref[:, hidden:]).astype(BF)
    for s in range(count):
        y_ref[:, s * width : (s + 1) * width] = lax.dot_general(
            inner_ref[...], outs[s][...], COLS_IN, preferred_element_type=F32
        ).astype(BF)


def expert_forward(x_recv, w_ins, w_outs):
    rows, width = x_recv.shape
    double = w_ins[0].shape[1]
    hidden = w_outs[0].shape[1]
    block = min(rows, 256)

    def band(columns):
        return pl.BlockSpec((block, columns), lambda i: (i, 0))

    return pl.pallas_call(
        lambda *refs: forward_kernel(len(w_ins), *refs),
        grid=(rows // block,),
        in_specs=[band(width)] + [whole(s) for s in (*w_ins, *w_outs)],
        out_specs=[band(double), band(hidden), band(width)],
        out_shape=[
            jax.ShapeDtypeStruct((rows, double), F32),
            jax.ShapeDtypeStruct((rows, hidden), BF),
            jax.ShapeDtypeStruct((rows, width), BF),
        ],
        compiler_params=pltpu.CompilerParams(vmem_limit_bytes=LIMIT),
        cost_estimate=CHEAP,
        name="expert_forward",
    )(x_recv, *w_ins, *w_outs)


def backward_kernel(count, act_ref, dy_ref, *refs):
    outs, ins = refs[:count], refs[count : 2 * count]
    act_grad_ref, dx_ref = refs[2 * count :]
    hidden = act_ref.shape[1] // 2
    width = dy_ref.shape[1] // count
    inner_grad = jnp.dot(dy_ref[:, :width], outs[0][...], preferred_element_type=F32)
    for s in range(1, count):
        inner_grad += jnp.dot(
            dy_ref[:, s * width : (s + 1) * width], outs[s][...], preferred_element_type=F32
        )
    act_gate = act_ref[:, :hidden]
    act_up = act_ref[:, hidden:]
    sig = jax.nn.sigmoid(act_gate)
    act_grad_ref[:, :hidden] = (
        inner_grad * act_up * sig * (1.0 + act_gate * (1.0 - sig))
    ).astype(BF)
    act_grad_ref[:, hidden:] = (inner_grad * (act_gate * sig)).astype(BF)
    for s in range(count):
        dx_ref[:, s * width : (s + 1) * width] = lax.dot_general(
            act_grad_ref[...], ins[s][...], COLS_IN, preferred_element_type=F32
        ).astype(BF)


def expert_backward(activation, dy_recv, w_ins, w_outs):
    rows, width = dy_recv.shape
    double = activation.shape[1]
    block = min(rows, 256)

    def band(columns):
        return pl.BlockSpec((block, columns), lambda i: (i, 0))

    return pl.pallas_call(
        lambda *refs: backward_kernel(len(w_ins), *refs),
        grid=(rows // block,),
        in_specs=[band(double), band(width)] + [whole(s) for s in (*w_outs, *w_ins)],
        out_specs=[band(double), band(width)],
        out_shape=[
            jax.ShapeDtypeStruct((rows, double), BF),
            jax.ShapeDtypeStruct((rows, width), BF),
        ],
        compiler_params=pltpu.CompilerParams(vmem_limit_bytes=LIMIT),
        cost_estimate=CHEAP,
        name="expert_backward",
    )(activation, dy_recv, *w_outs, *w_ins)


def combine_kernel(turn_ref, pick_ref, *refs):
    planes, out_ref = refs[:-1], refs[-1]
    size = planes[0].shape[0]
    total = None
    for i, plane in enumerate(planes):
        part = lax.dot_general(
            pick_ref[i * size : (i + 1) * size], plane[...], ROWS_IN, preferred_element_type=F32
        )
        total = part if total is None else total + part
    out_ref[...] = total.astype(BF)


def combine(pick, planes, position):
    slots, tok_rows = pick.shape
    size, width = planes[0].shape
    count = lax.axis_size("edata")
    tile = min(512, width // count)
    steps = width // tile
    per_shard = steps // count
    return pl.pallas_call(
        combine_kernel,
        grid_spec=pltpu.PrefetchScalarGridSpec(
            num_scalar_prefetch=1,
            grid=(steps,),
            in_specs=[pl.BlockSpec((slots, tok_rows), lambda i, t: (0, 0))]
            + [pl.BlockSpec((size, tile), lambda i, t: (0, i)) for _ in planes],
            out_specs=pl.BlockSpec((tok_rows, tile), lambda i, t: (0, (i + t[0]) % steps)),
        ),
        out_shape=jax.ShapeDtypeStruct((tok_rows, width), BF),
        compiler_params=pltpu.CompilerParams(vmem_limit_bytes=LIMIT),
        cost_estimate=CHEAP,
        name="combine",
    )((position * per_shard).astype(jnp.int32).reshape(1), pick, *planes)


def shards(tokens, out_grad, expert_ids, gates, w_gate_up, w_down):
    nodes, planes = lax.axis_size("node"), lax.axis_size("local")
    groups = nodes * planes
    tok_rows, model_width = tokens.shape
    capacity = tok_rows * expert_ids.shape[1] // (EXP_DEV * groups)
    half = planes // 2
    near, far = range(half), range(half, planes)
    size = nodes * capacity
    position = lax.axis_index("edata")
    turn = position * w_down.shape[1]
    w_ins = gathered(w_gate_up[0])
    w_outs = gathered(w_down[0])
    numbers = (
        (lax.axis_index("local") ^ jnp.arange(planes, dtype=jnp.int32))[:, None]
        + planes * jnp.arange(nodes, dtype=jnp.int32)[None, :]
    ).reshape(-1)
    chosen, hits, slot_weight = slot_tables(expert_ids, gates, numbers, capacity)
    pick = hits.astype(BF)

    def cut(rows, d):
        return rows[d * size : (d + 1) * size]

    x_send = jnp.dot(pick, jnp.roll(tokens, -turn, axis=1), preferred_element_type=F32).astype(BF)
    x_far = [to_plane(cut(x_send, d), d) for d in far]
    x_near = [to_plane(cut(x_send, d), d) for d in near]
    grad_rows = jnp.dot(pick, jnp.roll(out_grad, -turn, axis=1), preferred_element_type=F32)
    dy_send = (slot_weight[:, None] * grad_rows).astype(BF)
    dy_near = [to_plane(cut(dy_send, d), d) for d in near]

    x1 = over_nodes(joined(x_near))
    act1, inner1, y1 = expert_forward(x1, w_ins, w_outs)
    dy1 = over_nodes(after(joined(dy_near), x1))
    act_grad1, dx1 = expert_backward(act1, dy1, w_ins, w_outs)

    dy_far = [to_plane(after(cut(dy_send, d), x), d) for d, x in zip(far, x_far)]
    x2 = over_nodes(after(joined(x_far), dx1))
    act2, inner2, y2 = expert_forward(x2, w_ins, w_outs)
    y_parts = parted(over_nodes(y2), len(far))
    y_far = [to_plane(after(y, dy), d) for d, y, dy in zip(far, y_parts, dy_far)]

    dy2 = over_nodes(after(joined(dy_far), *y_parts))
    act_grad2, dx2 = expert_backward(act2, dy2, w_ins, w_outs)
    dx_parts = parted(over_nodes(dx2), len(far))
    dx_far = [to_plane(after(dx, y), d) for d, dx, y in zip(far, dx_parts, y_far)]

    y1 = after(y1, *dx_parts)
    y_near = [to_plane(y, d) for d, y in zip(near, parted(over_nodes(y1), len(near)))]
    dx1 = after(dx1, *y_near)
    dx_near = [to_plane(dx, d) for d, dx in zip(near, parted(over_nodes(dx1), len(near)))]

    dy1, dy2, act_grad1, act_grad2 = lax.optimization_barrier(
        (dy1, dy2, act_grad1, act_grad2, *dx_parts)
    )[:4]
    part_down = (
        lax.dot_general(dy1, inner1, ROWS_IN, preferred_element_type=F32)
        + lax.dot_general(dy2, inner2, ROWS_IN, preferred_element_type=F32)
    ).astype(BF)
    grad_down = reduced(part_down)
    part_in = (
        lax.dot_general(x1, act_grad1, ROWS_IN, preferred_element_type=F32)
        + lax.dot_general(x2, act_grad2, ROWS_IN, preferred_element_type=F32)
    ).astype(BF)
    grad_in = reduced(part_in)

    spread = jnp.where(hits, slot_weight[:, None], 0.0)
    high = lax.reduce_precision(spread, 8, 7)
    middle = lax.reduce_precision(spread - high, 8, 7)
    low = spread - high - middle
    high, middle, low = high.astype(BF), middle.astype(BF), low.astype(BF)
    y_back = jnp.concatenate(y_near + y_far, axis=0)
    mixed = (
        lax.dot_general(high, y_back, ROWS_IN, preferred_element_type=F32)
        + lax.dot_general(middle, y_back, ROWS_IN, preferred_element_type=F32)
        + lax.dot_general(low, y_back, ROWS_IN, preferred_element_type=F32)
    ).astype(BF)
    mixed = jnp.roll(mixed, turn, axis=1)
    slot_dots = jnp.sum(y_back.astype(F32) * grad_rows, axis=1)
    token_dots = jnp.sum(
        jnp.where(hits, slot_dots[:, None], 0.0).reshape(groups, capacity, tok_rows), axis=1
    )
    gate_grad = jnp.sum(jnp.where(chosen, token_dots[:, None, :], 0.0), axis=0).T
    *dx_far, grad_in, grad_down, mixed, gate_grad = lax.optimization_barrier(
        (*dx_far, grad_in, grad_down, mixed, gate_grad)
    )
    token_grad = combine(pick, dx_near + dx_far, position)
    return (mixed, token_grad, gate_grad, grad_in[None], grad_down[None])


def solution(mesh):
    rows = P(("node", "local", "edata"), None)
    weights = P(("node", "local"), "edata", None)
    return jax.shard_map(
        shards,
        mesh=mesh,
        in_specs=(rows, rows, rows, rows, weights, weights),
        out_specs=(rows, rows, rows, weights, weights),
        check_vma=False,
    )
```

```python
import jax
import jax.numpy as jnp
from jax import lax
from jax.experimental import pallas as pl
from jax.experimental.pallas import tpu as pltpu
from jax.sharding import PartitionSpec as P

EXP_DEV = 4
BF = jnp.bfloat16
F32 = jnp.float32
ROWS_IN = (((0,), (0,)), ((), ()))
COLS_IN = (((1,), (1,)), ((), ()))
LIMIT = 56 * 1024 * 1024
CHEAP = pl.CostEstimate(flops=1, bytes_accessed=1, transcendentals=0)


def params():
    return pltpu.CompilerParams(vmem_limit_bytes=LIMIT)


def slot_tables(expert_ids, gates, numbers, capacity):
    tok_rows = expert_ids.shape[0]
    ids_t = expert_ids.T
    chosen = ids_t[None, :, :] == numbers[:, None, None]
    routed = jnp.any(chosen, axis=1)
    earlier = jnp.arange(tok_rows)[:, None] < jnp.arange(tok_rows)[None, :]
    order_in = jnp.dot(
        routed.astype(BF), earlier.astype(BF), preferred_element_type=F32
    ).astype(jnp.int32)
    weight = jnp.sum(jnp.where(chosen, gates.T[None, :, :], 0.0), axis=1)
    slot_ids = jnp.arange(capacity, dtype=jnp.int32)
    hits = routed[:, None, :] & (order_in[:, None, :] == slot_ids[None, :, None])
    slot_weight = jnp.sum(jnp.where(hits, weight[:, None, :], 0.0), axis=2)
    return hits.reshape(numbers.shape[0] * capacity, tok_rows).astype(BF), slot_weight.reshape(-1, 1)


def after(value, *others):
    return lax.optimization_barrier((value, *others))[0]


def to_plane(rows, distance):
    if distance == 0:
        return rows
    pairs = [(i, i ^ distance) for i in range(lax.axis_size("local"))]
    return lax.ppermute(rows, "local", pairs)


def over_nodes(rows):
    return lax.all_to_all(rows, "node", split_axis=0, concat_axis=0, tiled=True)


def to_nodes(blocks):
    count = len(blocks)
    return [blocks[0]] + [
        lax.ppermute(blocks[d], "node", [(i, i ^ d) for i in range(count)]) for d in range(1, count)
    ]


def gathered(shard):
    count = lax.axis_size("edata")
    shards = [shard]
    for step in range(1, count):
        pairs = [((i + step) % count, i) for i in range(count)]
        shards.append(lax.ppermute(shard, "edata", pairs))
    return shards


def from_owner(piece, step):
    count = lax.axis_size("edata")
    return lax.ppermute(piece, "edata", [(i, (i + step) % count) for i in range(count)])


def dispatch_kernel(turn_ref, pick_ref, weight_ref, x_ref, dy_ref, *out_refs):
    nodes, _, capacity, tile = out_refs[0].shape
    size = nodes * capacity
    for i, out_ref in enumerate(out_refs):
        here = slice(i * size, (i + 1) * size)
        pick = pick_ref[here]
        x = jnp.dot(pick, x_ref[...], preferred_element_type=F32).astype(BF)
        out_ref[:, 0] = x.reshape(nodes, capacity, tile)
        dy = jnp.dot(pick, dy_ref[...], preferred_element_type=F32)
        out_ref[:, 1] = (weight_ref[here] * dy).astype(BF).reshape(nodes, capacity, tile)


def dispatch(turn, pick, weight, tokens, out_grad, nodes, capacity):
    slots, tok_rows = pick.shape
    width = tokens.shape[1]
    count = lax.axis_size("edata")
    tile = min(1024, width // count)
    steps = width // tile
    planes = slots // (nodes * capacity)
    turned = pl.BlockSpec((tok_rows, tile), lambda i, t: (0, (i + t[0] * (steps // count)) % steps))
    return pl.pallas_call(
        dispatch_kernel,
        grid_spec=pltpu.PrefetchScalarGridSpec(
            num_scalar_prefetch=1,
            grid=(steps,),
            in_specs=[
                pl.BlockSpec((slots, tok_rows), lambda i, t: (0, 0)),
                pl.BlockSpec((slots, 1), lambda i, t: (0, 0)),
                turned,
                turned,
            ],
            out_specs=[pl.BlockSpec((nodes, 2, capacity, tile), lambda i, t: (0, 0, 0, i))] * planes,
        ),
        out_shape=[jax.ShapeDtypeStruct((nodes, 2, capacity, width), BF)] * planes,
        compiler_params=params(),
        cost_estimate=CHEAP,
        name="dispatch",
    )(turn, pick, weight, tokens, out_grad)


def expert_kernel(count, rows_ref, *refs):
    ins, outs = refs[:count], refs[count : 2 * count]
    back_ref, inner_ref, act_grad_ref, act_ref = refs[2 * count :]
    nodes, _, capacity, model = rows_ref.shape
    rows = nodes * capacity
    hidden = inner_ref.shape[1]
    width = model // count

    def part(kind, s):
        return rows_ref[:, kind, :, s * width : (s + 1) * width].reshape(rows, width)

    activation = jnp.dot(part(0, 0), ins[0][...], preferred_element_type=F32)
    for s in range(1, count):
        activation += jnp.dot(part(0, s), ins[s][...], preferred_element_type=F32)
    act_ref[...] = activation
    act_gate = act_ref[:, :hidden]
    act_up = act_ref[:, hidden:]
    sig = jax.nn.sigmoid(act_gate)
    swished = act_gate * sig
    inner_ref[...] = (swished * act_up).astype(BF)
    inner_grad = jnp.dot(part(1, 0), outs[0][...], preferred_element_type=F32)
    for s in range(1, count):
        inner_grad += jnp.dot(part(1, s), outs[s][...], preferred_element_type=F32)
    act_grad_ref[:, :hidden] = (
        inner_grad * act_up * sig * (1.0 + act_gate * (1.0 - sig))
    ).astype(BF)
    act_grad_ref[:, hidden:] = (inner_grad * swished).astype(BF)
    for s in range(count):
        here = slice(s * width, (s + 1) * width)
        y = lax.dot_general(inner_ref[...], outs[s][...], COLS_IN, preferred_element_type=F32)
        back_ref[:, 0, :, here] = y.astype(BF).reshape(nodes, capacity, width)
        dx = lax.dot_general(act_grad_ref[...], ins[s][...], COLS_IN, preferred_element_type=F32)
        back_ref[:, 1, :, here] = dx.astype(BF).reshape(nodes, capacity, width)


def expert(arrived, w_ins, w_outs):
    nodes, pieces, capacity, width = arrived.shape
    double = w_ins[0].shape[1]
    hidden = w_outs[0].shape[1]
    rows = nodes * capacity

    def whole(shard):
        return pl.BlockSpec(shard.shape, lambda i: (0, 0), pipeline_mode=pl.Buffered(1))

    def band(columns):
        return pl.BlockSpec((rows, columns), lambda i: (i, 0))

    moved = pl.BlockSpec((nodes, 2, capacity, width), lambda i: (0, i, 0, 0))
    planes = pieces // 2
    return pl.pallas_call(
        lambda *refs: expert_kernel(len(w_ins), *refs),
        grid=(planes,),
        in_specs=[moved] + [whole(s) for s in (*w_ins, *w_outs)],
        out_specs=[moved, band(hidden), band(double)],
        out_shape=[
            jax.ShapeDtypeStruct(arrived.shape, BF),
            jax.ShapeDtypeStruct((planes * rows, hidden), BF),
            jax.ShapeDtypeStruct((planes * rows, double), BF),
        ],
        scratch_shapes=[pltpu.VMEM((rows, double), F32)],
        compiler_params=params(),
        cost_estimate=CHEAP,
        name="expert",
    )(arrived, *w_ins, *w_outs)


def weight_kernel(count, *refs):
    arrived, inners, act_grads = refs[:count], refs[count : 2 * count], refs[2 * count : 3 * count]
    in_ref, out_ref = refs[3 * count :]
    total_in = total_out = None
    for rows_ref, inner, act_grad in zip(arrived, inners, act_grads):
        nodes, pieces, capacity, tile = rows_ref.shape
        rows = nodes * capacity
        for i in range(pieces // 2):
            x = rows_ref[:, 2 * i].reshape(rows, tile)
            dy = rows_ref[:, 2 * i + 1].reshape(rows, tile)
            here = slice(i * rows, (i + 1) * rows)
            one = lax.dot_general(x, act_grad[here], ROWS_IN, preferred_element_type=F32)
            two = lax.dot_general(dy, inner[here], ROWS_IN, preferred_element_type=F32)
            total_in = one if total_in is None else total_in + one
            total_out = two if total_out is None else total_out + two
    in_ref[...] = total_in.astype(BF)
    out_ref[...] = total_out.astype(BF)


def weight_grads(shard, arrived, inners, act_grads):
    width = arrived[0].shape[3]
    size = width // lax.axis_size("edata")
    double, hidden = act_grads[0].shape[1], inners[0].shape[1]
    tile = min(256, size)
    steps = size // tile

    def columns(array):
        return pl.BlockSpec(array.shape[:3] + (tile,), lambda i: (0, 0, 0, shard * steps + i))

    def whole(array):
        return pl.BlockSpec(array.shape, lambda i: (0, 0), pipeline_mode=pl.Buffered(1))

    return pl.pallas_call(
        lambda *refs: weight_kernel(len(arrived), *refs),
        grid=(steps,),
        in_specs=[columns(a) for a in arrived] + [whole(a) for a in (*inners, *act_grads)],
        out_specs=[
            pl.BlockSpec((tile, double), lambda i: (i, 0)),
            pl.BlockSpec((tile, hidden), lambda i: (i, 0)),
        ],
        out_shape=[
            jax.ShapeDtypeStruct((size, double), BF),
            jax.ShapeDtypeStruct((size, hidden), BF),
        ],
        compiler_params=params(),
        cost_estimate=CHEAP,
        name="weight_grads",
    )(*arrived, *inners, *act_grads)


def all_weight_grads(arrived, results):
    inners = [r[1] for r in results]
    act_grads = [r[2] for r in results]
    parts = []
    for shard in range(lax.axis_size("edata")):
        parts += weight_grads(shard, arrived, inners, act_grads)
    return parts


def combine_kernel(
    planes, groups, turn_ref, number_ref, pick_ref, weight_ref, ids_ref, grad_ref, *refs
):
    backs = refs[:planes]
    mixed_ref, token_grad_ref, gate_grad_ref, high_ref, middle_ref, dots_ref = refs[planes:]
    step = pl.program_id(0)
    nodes, _, capacity, tile = backs[0].shape
    size = nodes * capacity

    @pl.when(step == 0)
    def _():
        spread = pick_ref[...].astype(F32) * weight_ref[...]
        high = spread.astype(BF)
        high_ref[...] = high
        middle_ref[...] = (spread - high.astype(F32)).astype(BF)
        dots_ref[...] = jnp.zeros_like(dots_ref)

    mixed = token_grad = None
    for i, back in enumerate(backs):
        here = slice(i * size, (i + 1) * size)
        pick = pick_ref[here]
        y = back[:, 0].reshape(size, tile)
        dx = back[:, 1].reshape(size, tile)
        one = lax.dot_general(high_ref[here], y, ROWS_IN, preferred_element_type=F32)
        one += lax.dot_general(middle_ref[here], y, ROWS_IN, preferred_element_type=F32)
        two = lax.dot_general(pick, dx, ROWS_IN, preferred_element_type=F32)
        mixed = one if mixed is None else mixed + one
        token_grad = two if token_grad is None else token_grad + two
        grad_rows = jnp.dot(pick, grad_ref[...], preferred_element_type=F32)
        dots_ref[here] += jnp.sum(y.astype(F32) * grad_rows, axis=1, keepdims=True)
    mixed_ref[...] = mixed.astype(BF)
    token_grad_ref[...] = token_grad.astype(BF)

    @pl.when(step == pl.num_programs(0) - 1)
    def _():
        tok_rows = pick_ref.shape[1]
        by_token = pick_ref[...].astype(F32) * dots_ref[...]
        by_token = jnp.sum(by_token.reshape(groups, capacity, tok_rows), axis=1)
        ids = ids_ref[...]
        total = jnp.zeros(ids.shape, F32)
        for g in range(groups):
            total += jnp.where(ids == number_ref[g], by_token[g : g + 1], 0.0)
        gate_grad_ref[...] = total


def combine(turn, numbers, pick, weight, ids_t, out_grad, backs):
    slots, tok_rows = pick.shape
    nodes, _, capacity, width = backs[0].shape
    count = lax.axis_size("edata")
    tile = min(512, width // count)
    steps = width // tile
    turned = pl.BlockSpec(
        (tok_rows, tile), lambda i, t, n: (0, (i + t[0] * (steps // count)) % steps)
    )

    def whole(array):
        return pl.BlockSpec(array.shape, lambda i, t, n: (0, 0))

    return pl.pallas_call(
        lambda *refs: combine_kernel(len(backs), numbers.shape[0], *refs),
        grid_spec=pltpu.PrefetchScalarGridSpec(
            num_scalar_prefetch=2,
            grid=(steps,),
            in_specs=[whole(pick), whole(weight), whole(ids_t), turned]
            + [pl.BlockSpec((nodes, 2, capacity, tile), lambda i, t, n: (0, 0, 0, i))] * len(backs),
            out_specs=[turned, turned, whole(ids_t)],
            scratch_shapes=[
                pltpu.VMEM((slots, tok_rows), BF),
                pltpu.VMEM((slots, tok_rows), BF),
                pltpu.VMEM((slots, 1), F32),
            ],
        ),
        out_shape=[
            jax.ShapeDtypeStruct((tok_rows, width), BF),
            jax.ShapeDtypeStruct((tok_rows, width), BF),
            jax.ShapeDtypeStruct(ids_t.shape, F32),
        ],
        compiler_params=params(),
        cost_estimate=CHEAP,
        name="combine",
    )(turn, numbers, pick, weight, ids_t, out_grad, *backs)


def shards(tokens, out_grad, expert_ids, gates, w_gate_up, w_down):
    nodes, planes = lax.axis_size("node"), lax.axis_size("local")
    groups = nodes * planes
    tok_rows = tokens.shape[0]
    capacity = tok_rows * expert_ids.shape[1] // (EXP_DEV * groups)
    half = planes // 2
    near, far = list(range(half)), list(range(half, planes))
    split = half * nodes * capacity
    turn = lax.axis_index("edata").astype(jnp.int32).reshape(1)
    w_ins = gathered(w_gate_up[0])
    w_outs = gathered(w_down[0])
    plane = (lax.axis_index("local") ^ jnp.arange(planes, dtype=jnp.int32))[:, None]
    node = jnp.arange(nodes, dtype=jnp.int32)[None, :]
    node = jnp.where(jnp.arange(planes)[:, None] < half, node, lax.axis_index("node") ^ node)
    numbers = (plane + planes * node).reshape(-1)
    pick, slot_weight = slot_tables(expert_ids, gates, numbers, capacity)

    sent_far = dispatch(
        turn, pick[split:], slot_weight[split:], tokens, out_grad, nodes, capacity
    )
    sent_near = dispatch(
        turn, after(pick[:split], *sent_far), slot_weight[:split], tokens, out_grad, nodes, capacity
    )
    far_in = [to_plane(rows, d) for d, rows in zip(far, sent_far)]
    near_mid = over_nodes(jnp.concatenate(sent_near, axis=1))

    backs = [None] * planes
    arrived, results, back, near_result = [], [], None, None
    far_in[0] = after(far_in[0], *w_ins[1:], *w_outs[1:])
    for d, rows in zip(far, far_in):
        if back is not None:
            rows = after(rows, back)
        blocks = to_nodes([rows[i : i + 1] for i in range(nodes)])
        if back is not None and near_result is None:
            near_in = after(near_in, rows)
            near_result = expert(near_in, w_ins, w_outs)
            blocks[0] = after(blocks[0], near_result[0])
        arrived.append(jnp.concatenate(blocks, axis=0))
        results.append(expert(arrived[-1], w_ins, w_outs))
        if back is None:
            near_mid = after(near_mid, results[0][0])
            near_in = [to_plane(near_mid[:, 2 * i : 2 * i + 2], i) for i in near]
            near_in = jnp.concatenate(near_in, axis=1)
        back = [results[-1][0][i : i + 1] for i in range(nodes)]
        back = jnp.concatenate(to_nodes(back), axis=0)
        if len(results) == len(far):
            parts = all_weight_grads([near_in, *arrived], [near_result, *results])
            back, *parts = lax.optimization_barrier((back, *parts, backs[far[-2]]))[:-1]
        backs[d] = to_plane(back, d)
    near_out = [to_plane(near_result[0][:, 2 * i : 2 * i + 2], i) for i in near]
    near_out = over_nodes(jnp.concatenate(near_out, axis=1))
    for i, d in enumerate(near):
        backs[d] = near_out[:, 2 * i : 2 * i + 2]
    sums = [parts[0].astype(F32), parts[1].astype(F32)]
    for step in range(1, len(w_ins)):
        for i in (0, 1):
            sums[i] = sums[i] + from_owner(parts[2 * step + i], step).astype(F32)

    *backs, sums[0], sums[1] = lax.optimization_barrier((*backs, *sums))
    mixed, token_grad, gate_grad = combine(
        turn, numbers, pick, slot_weight, expert_ids.T, out_grad, backs
    )
    return (mixed, token_grad, gate_grad.T, sums[0][None], sums[1][None])


def solution(mesh):
    rows = P(("node", "local", "edata"), None)
    weights = P(("node", "local"), "edata", None)
    return jax.shard_map(
        shards,
        mesh=mesh,
        in_specs=(rows, rows, rows, rows, weights, weights),
        out_specs=(rows, rows, rows, weights, weights),
        check_vma=False,
    )
```

```python
import jax
import jax.numpy as jnp
from jax import lax
from jax.experimental import pallas as pl
from jax.experimental.pallas import tpu as pltpu
from jax.sharding import PartitionSpec as P

EXP_DEV = 4
BF = jnp.bfloat16
F32 = jnp.float32
ROWS_IN = (((0,), (0,)), ((), ()))
COLS_IN = (((1,), (1,)), ((), ()))
LIMIT = 56 * 1024 * 1024
CHEAP = pl.CostEstimate(flops=1, bytes_accessed=1, transcendentals=0)
VMEM = pl.BlockSpec(memory_space=pltpu.VMEM)


def call(kernel, name, **more):
    return pl.pallas_call(
        kernel,
        compiler_params=pltpu.CompilerParams(vmem_limit_bytes=LIMIT),
        cost_estimate=CHEAP,
        name=name,
        **more,
    )


def shape(*dims, kind=BF):
    return jax.ShapeDtypeStruct(dims, kind)


def after(value, *others):
    return lax.optimization_barrier((value, *others))[0]


def slot_tables(expert_ids, gates, numbers, capacity):
    tok_rows = expert_ids.shape[0]
    ids_t = expert_ids.T
    chosen = ids_t[None, :, :] == numbers[:, None, None]
    routed = jnp.any(chosen, axis=1)
    earlier = jnp.arange(tok_rows)[:, None] < jnp.arange(tok_rows)[None, :]
    order_in = jnp.dot(
        routed.astype(BF), earlier.astype(BF), preferred_element_type=F32
    ).astype(jnp.int32)
    weight = jnp.sum(jnp.where(chosen, gates.T[None, :, :], 0.0), axis=1)
    slot_ids = jnp.arange(capacity, dtype=jnp.int32)
    hits = routed[:, None, :] & (order_in[:, None, :] == slot_ids[None, :, None])
    slot_weight = jnp.sum(jnp.where(hits, weight[:, None, :], 0.0), axis=2)
    return hits.reshape(numbers.shape[0] * capacity, tok_rows).astype(BF), slot_weight.reshape(-1, 1)


class Ring:
    def __init__(self, nodes, planes):
        self.nodes, self.planes, self.half = nodes, planes, planes // 2
        self.cut = nodes // 2
        self.up_size = nodes * (self.half - 1) + self.cut
        self.down_size = nodes * (self.half - 1) + nodes - self.cut

    def shapes(self, capacity, width):
        return [
            shape(n, capacity, width) for n in (self.nodes, self.up_size, self.down_size)
        ]

    def place(self, refs, distance, value, columns=slice(None)):
        own, up, down = refs
        nodes, half = self.nodes, self.half
        if distance == 0:
            own[:, :, columns] = value
        elif distance < half:
            up[(distance - 1) * nodes : distance * nodes, :, columns] = value
        elif distance > half:
            back = self.planes - distance
            down[(back - 1) * nodes : back * nodes, :, columns] = value
        else:
            up[(half - 1) * nodes :, :, columns] = value[: self.cut]
            down[(half - 1) * nodes :, :, columns] = value[self.cut :]

    def send(self, own, up, down):
        got = [own]
        for first, way, last in ((up, 1, self.cut), (down, -1, self.nodes - self.cut)):
            now = first
            for step in range(1, self.half + 1):
                pairs = [(i, (i + way) % self.planes) for i in range(self.planes)]
                now = lax.ppermute(now, "local", pairs)
                got.append(now)
                if step < self.half:
                    now = now[self.nodes :]
        return got

    def take(self, got, distance):
        nodes, half = self.nodes, self.half
        if distance == 0:
            return got[0][...]
        if distance < half:
            return got[distance][:nodes]
        if distance > half:
            return got[half + self.planes - distance][:nodes]
        return jnp.concatenate([got[half][...], got[2 * half][...]], axis=0)


def over_nodes(rows):
    return lax.all_to_all(rows, "node", split_axis=0, concat_axis=0, tiled=True)


def gathered(shard):
    count = lax.axis_size("edata")
    shards = [shard]
    for step in range(1, count):
        pairs = [((i + step) % count, i) for i in range(count)]
        shards.append(lax.ppermute(shard, "edata", pairs))
    return shards


def from_owner(piece, step):
    count = lax.axis_size("edata")
    return lax.ppermute(piece, "edata", [(i, (i + step) % count) for i in range(count)])


def column_tiles(width, most):
    count = lax.axis_size("edata")
    tile = min(most, width // count)
    steps = width // tile
    return tile, steps, lambda i, turn: (i + turn * (steps // count)) % steps


def dispatch_x(ring, turn, pick, tokens, capacity):
    slots, tok_rows = pick.shape
    width = tokens.shape[1]
    tile, steps, turned = column_tiles(width, 1024)
    size = ring.nodes * capacity

    def kernel(turn_ref, pick_ref, x_ref, *refs):
        rows = jnp.dot(pick_ref[...], x_ref[...], preferred_element_type=F32).astype(BF)
        for d in range(ring.planes):
            part = rows[d * size : (d + 1) * size]
            ring.place(refs, d, part.reshape(ring.nodes, capacity, tile))

    shapes = ring.shapes(capacity, width)
    return call(
        kernel,
        "dispatch_x",
        grid_spec=pltpu.PrefetchScalarGridSpec(
            num_scalar_prefetch=1,
            grid=(steps,),
            in_specs=[
                pl.BlockSpec((slots, tok_rows), lambda i, t: (0, 0)),
                pl.BlockSpec((tok_rows, tile), lambda i, t: (0, turned(i, t[0]))),
            ],
            out_specs=[pl.BlockSpec(s.shape[:2] + (tile,), lambda i, t: (0, 0, i)) for s in shapes],
        ),
        out_shape=shapes,
    )(turn, pick, tokens)


def dispatch_dy(ring, turn, pick, weight, out_grad, capacity):
    slots, tok_rows = pick.shape
    width = out_grad.shape[1]
    tile, steps, turned = column_tiles(width, 1024)
    size = ring.nodes * capacity

    def kernel(turn_ref, pick_ref, weight_ref, grad_ref, out_ref, rows_ref):
        rows = jnp.dot(pick_ref[...], grad_ref[...], preferred_element_type=F32)
        rows_ref[...] = rows.astype(BF)
        scaled = (weight_ref[...] * rows).astype(BF)
        for d in range(ring.planes):
            part = scaled[d * size : (d + 1) * size]
            out_ref[:, d] = part.reshape(ring.nodes, capacity, tile)

    return call(
        kernel,
        "dispatch_dy",
        grid_spec=pltpu.PrefetchScalarGridSpec(
            num_scalar_prefetch=1,
            grid=(steps,),
            in_specs=[
                pl.BlockSpec((slots, tok_rows), lambda i, t: (0, 0)),
                pl.BlockSpec((slots, 1), lambda i, t: (0, 0)),
                pl.BlockSpec((tok_rows, tile), lambda i, t: (0, turned(i, t[0]))),
            ],
            out_specs=[
                pl.BlockSpec(
                    (ring.nodes, ring.planes, capacity, tile), lambda i, t: (0, 0, 0, i)
                ),
                pl.BlockSpec((slots, tile), lambda i, t: (0, i)),
            ],
        ),
        out_shape=[
            shape(ring.nodes, ring.planes, capacity, width),
            shape(slots, width),
        ],
    )(turn, pick, weight, out_grad)


def pack(ring, got):
    _, capacity, width = got[0].shape
    tile = min(1024, width)

    def kernel(*refs):
        for d in range(ring.planes):
            refs[-1][:, d] = ring.take(refs[:-1], d)

    used = [ring.nodes]
    for last in (ring.cut, ring.nodes - ring.cut):
        used += [ring.nodes] * (ring.half - 1) + [last]
    return call(
        kernel,
        "pack",
        grid=(width // tile,),
        in_specs=[pl.BlockSpec((n, capacity, tile), lambda i: (0, 0, i)) for n in used],
        out_specs=pl.BlockSpec(
            (ring.nodes, ring.planes, capacity, tile), lambda i: (0, 0, 0, i)
        ),
        out_shape=shape(ring.nodes, ring.planes, capacity, width),
    )(*got)


def unpack(ring, rows, back):
    _, _, capacity, width = rows.shape
    tile = min(1024, width)

    def kernel(rows_ref, *refs):
        for d in range(ring.planes):
            ring.place(refs, -d % ring.planes if back else d, rows_ref[:, d])

    shapes = ring.shapes(capacity, width)
    return call(
        kernel,
        "unpack",
        grid=(width // tile,),
        in_specs=[
            pl.BlockSpec((ring.nodes, ring.planes, capacity, tile), lambda i: (0, 0, 0, i))
        ],
        out_specs=[pl.BlockSpec(s.shape[:2] + (tile,), lambda i: (0, 0, i)) for s in shapes],
        out_shape=shapes,
    )(rows)


def expert(ring, x_rows, dy_got, w_ins, w_outs):
    nodes, planes, capacity, model = x_rows.shape
    size = nodes * capacity
    rows = planes * size
    count = len(w_ins)
    width = model // count
    double, hidden = w_ins[0].shape[1], w_outs[0].shape[1]
    many = max(1, min(256, rows) // size)

    def kernel(x_ref, *refs):
        got, refs = refs[: len(dy_got)], refs[len(dy_got) :]
        ins, outs, refs = refs[:count], refs[count : 2 * count], refs[2 * count :]
        y_refs, (dx_ref, inner_ref, act_grad_ref, xs_ref, dys_ref, act_ref) = refs[:3], refs[3:]
        for first in range(0, planes, many):
            band = slice(first * size, (first + many) * size)
            for d in range(first, first + many):
                here = slice(d * size, (d + 1) * size)
                xs_ref[here] = x_ref[:, d].reshape(size, model)
                dys_ref[here] = ring.take(got, d).reshape(size, model)

            def product(source, weights):
                total = None
                for s in range(count):
                    one = jnp.dot(
                        source[band, s * width : (s + 1) * width],
                        weights[s][...],
                        preferred_element_type=F32,
                    )
                    total = one if total is None else total + one
                return total

            act_ref[...] = product(xs_ref, ins)
            act_gate = act_ref[:, :hidden]
            act_up = act_ref[:, hidden:]
            sig = jax.nn.sigmoid(act_gate)
            swished = act_gate * sig
            inner_ref[band] = (swished * act_up).astype(BF)
            inner_grad = product(dys_ref, outs)
            act_grad_ref[band, :hidden] = (
                inner_grad * act_up * sig * (1.0 + act_gate * (1.0 - sig))
            ).astype(BF)
            act_grad_ref[band, hidden:] = (inner_grad * swished).astype(BF)
            for s in range(count):
                columns = slice(s * width, (s + 1) * width)
                y = lax.dot_general(
                    inner_ref[band], outs[s][...], COLS_IN, preferred_element_type=F32
                ).astype(BF)
                dx = lax.dot_general(
                    act_grad_ref[band], ins[s][...], COLS_IN, preferred_element_type=F32
                ).astype(BF)
                for i in range(many):
                    d = first + i
                    part = slice(i * size, (i + 1) * size)
                    ring.place(
                        y_refs, -d % planes, y[part].reshape(nodes, capacity, width), columns
                    )
                    dx_ref[:, d, :, columns] = dx[part].reshape(nodes, capacity, width)

    operands = (x_rows, *dy_got, *w_ins, *w_outs)
    out_shape = [
        *ring.shapes(capacity, model),
        shape(nodes, planes, capacity, model),
        shape(rows, hidden),
        shape(rows, double),
        shape(rows, model),
        shape(rows, model),
    ]
    return call(
        kernel,
        "expert",
        in_specs=[VMEM] * len(operands),
        out_specs=[VMEM] * len(out_shape),
        out_shape=out_shape,
        scratch_shapes=[pltpu.VMEM((many * size, double), F32)],
    )(*operands)


def weight_grads(shard, xs, dys, inner, act_grad):
    rows, width = xs.shape
    size = width // lax.axis_size("edata")
    double, hidden = act_grad.shape[1], inner.shape[1]
    tile = min(256, size)
    steps = size // tile

    def kernel(x_ref, dy_ref, inner_ref, act_grad_ref, out_ref):
        out_ref[:, :double] = lax.dot_general(
            x_ref[...], act_grad_ref[...], ROWS_IN, preferred_element_type=F32
        ).astype(BF)
        out_ref[:, double:] = lax.dot_general(
            dy_ref[...], inner_ref[...], ROWS_IN, preferred_element_type=F32
        ).astype(BF)

    columns = pl.BlockSpec((rows, tile), lambda i: (0, shard * steps + i))
    return call(
        kernel,
        "weight_grads",
        grid=(steps,),
        in_specs=[
            columns,
            columns,
            pl.BlockSpec((rows, hidden), lambda i: (0, 0)),
            pl.BlockSpec((rows, double), lambda i: (0, 0)),
        ],
        out_specs=pl.BlockSpec((tile, double + hidden), lambda i: (i, 0)),
        out_shape=shape(size, double + hidden),
    )(xs, dys, inner, act_grad)


def combine(ring, turn, numbers, picks, ids_t, grad_rows, y_rows, dx_got):
    pick, pick_t, high_t, middle_t = picks
    slots, tok_rows = pick.shape
    nodes, planes, capacity, width = y_rows.shape
    size = nodes * capacity
    groups = nodes * planes
    tile, steps, turned = column_tiles(width, 512)

    def kernel(turn_ref, number_ref, pick_ref, pick_t_ref, high_ref, middle_ref, *refs):
        ids_ref, grad_ref, y_ref, *got = refs[:-4]
        mixed_ref, token_grad_ref, gate_grad_ref, dots_ref = refs[-4:]
        step = pl.program_id(0)
        order = [-d % planes for d in range(planes)]
        y = jnp.concatenate([y_ref[:, e].reshape(size, tile) for e in order], axis=0)
        dx = jnp.concatenate([ring.take(got, e).reshape(size, tile) for e in order], axis=0)
        mixed_ref[...] = (
            jnp.dot(high_ref[...], y, preferred_element_type=F32)
            + jnp.dot(middle_ref[...], y, preferred_element_type=F32)
        ).astype(BF)
        token_grad_ref[...] = jnp.dot(
            pick_t_ref[...], dx, preferred_element_type=F32
        ).astype(BF)
        dots = jnp.sum(y.astype(F32) * grad_ref[...].astype(F32), axis=1, keepdims=True)

        @pl.when(step == 0)
        def _():
            dots_ref[...] = dots

        @pl.when(step > 0)
        def _():
            dots_ref[...] += dots

        @pl.when(step == steps - 1)
        def _():
            by_token = pick_ref[...].astype(F32) * dots_ref[...]
            by_token = jnp.sum(by_token.reshape(groups, capacity, tok_rows), axis=1)
            ids = ids_ref[...]
            total = jnp.zeros(ids.shape, F32)
            for g in range(groups):
                total += jnp.where(ids == number_ref[g], by_token[g : g + 1], 0.0)
            gate_grad_ref[...] = total

    def whole(array):
        return pl.BlockSpec(array.shape, lambda i, t, n: (0, 0))

    used = [nodes]
    for last in (ring.cut, nodes - ring.cut):
        used += [nodes] * (ring.half - 1) + [last]
    turned_spec = pl.BlockSpec((tok_rows, tile), lambda i, t, n: (0, turned(i, t[0])))
    return call(
        kernel,
        "combine",
        grid_spec=pltpu.PrefetchScalarGridSpec(
            num_scalar_prefetch=2,
            grid=(steps,),
            in_specs=[whole(p) for p in picks]
            + [
                whole(ids_t),
                pl.BlockSpec((slots, tile), lambda i, t, n: (0, i)),
                pl.BlockSpec((nodes, planes, capacity, tile), lambda i, t, n: (0, 0, 0, i)),
            ]
            + [pl.BlockSpec((u, capacity, tile), lambda i, t, n: (0, 0, i)) for u in used],
            out_specs=[turned_spec, turned_spec, whole(ids_t)],
            scratch_shapes=[pltpu.VMEM((slots, 1), F32)],
        ),
        out_shape=[
            shape(tok_rows, width),
            shape(tok_rows, width),
            shape(*ids_t.shape, kind=F32),
        ],
    )(turn, numbers, *picks, ids_t, grad_rows, y_rows, *dx_got)


def shards(tokens, out_grad, expert_ids, gates, w_gate_up, w_down):
    nodes, planes = lax.axis_size("node"), lax.axis_size("local")
    groups = nodes * planes
    tok_rows = tokens.shape[0]
    capacity = tok_rows * expert_ids.shape[1] // (EXP_DEV * groups)
    ring = Ring(nodes, planes)
    turn = lax.axis_index("edata").astype(jnp.int32).reshape(1)
    w_ins = gathered(w_gate_up[0])
    w_outs = gathered(w_down[0])
    plane = (lax.axis_index("local") + jnp.arange(planes, dtype=jnp.int32)) % planes
    numbers = (plane[:, None] + planes * jnp.arange(nodes, dtype=jnp.int32)[None, :]).reshape(-1)
    pick, slot_weight = slot_tables(expert_ids, gates, numbers, capacity)

    x_own, x_up, x_down = dispatch_x(ring, turn, pick, tokens, capacity)
    pick2 = after(pick, x_own, x_up, x_down)
    dy_sent, grad_rows = dispatch_dy(ring, turn, pick2, slot_weight, out_grad, capacity)
    x_got = ring.send(x_own, x_up, x_down)
    dy_mid = over_nodes(dy_sent)
    *x_got, dy_mid = lax.optimization_barrier((*x_got, dy_mid))
    x_rows = over_nodes(pack(ring, x_got))
    dy_got = ring.send(*unpack(ring, dy_mid, False))
    *y_sent, dx_sent, inner, act_grad, xs, dys = expert(ring, x_rows, dy_got, w_ins, w_outs)
    y_got = ring.send(*y_sent)
    dx_mid = over_nodes(dx_sent)
    *y_got, dx_mid = lax.optimization_barrier((*y_got, dx_mid))
    y_packed = pack(ring, y_got)
    y_rows = over_nodes(y_packed)
    dx_sent = unpack(ring, dx_mid, True)
    dx_got = ring.send(*dx_sent)
    inner = after(inner, y_packed, *dx_sent)
    parts = []
    for shard in [*range(1, len(w_ins)), 0]:
        parts.append(weight_grads(shard, xs, dys, inner, act_grad))

    parts = [parts[-1]] + [from_owner(p, step) for step, p in enumerate(parts[:-1], 1)]
    double = w_gate_up.shape[2]
    sums = [
        sum(p[:, columns].astype(F32) for p in parts)
        for columns in (slice(0, double), slice(double, None))
    ]

    spread = pick.astype(F32) * after(slot_weight, y_got[1])
    high = lax.reduce_precision(spread, 8, 7)
    middle = (spread - high).astype(BF)
    picks = (pick, pick.T, high.astype(BF).T, middle.T)
    *dx_got, sums[0], sums[1] = lax.optimization_barrier((*dx_got, *sums))
    mixed, token_grad, gate_grad = combine(
        ring, turn, numbers, picks, expert_ids.T, grad_rows, y_rows, dx_got
    )
    return (mixed, token_grad, gate_grad.T, sums[0][None], sums[1][None])


def solution(mesh):
    rows = P(("node", "local", "edata"), None)
    weights = P(("node", "local"), "edata", None)
    return jax.shard_map(
        shards,
        mesh=mesh,
        in_specs=(rows, rows, rows, rows, weights, weights),
        out_specs=(rows, rows, rows, weights, weights),
        check_vma=False,
    )
```

```python
import jax
import jax.numpy as jnp
from jax import lax
from jax.experimental import pallas as pl
from jax.experimental.pallas import tpu as pltpu
from jax.sharding import PartitionSpec as P

EXP_DEV = 4
BF = jnp.bfloat16
F32 = jnp.float32
ROWS_IN = (((0,), (0,)), ((), ()))
COLS_IN = (((1,), (1,)), ((), ()))
LIMIT = 56 * 1024 * 1024
CHEAP = pl.CostEstimate(flops=1, bytes_accessed=1, transcendentals=0)
VMEM = pl.BlockSpec(memory_space=pltpu.VMEM)


def call(kernel, name, **more):
    return pl.pallas_call(
        kernel,
        compiler_params=pltpu.CompilerParams(vmem_limit_bytes=LIMIT),
        cost_estimate=CHEAP,
        name=name,
        **more,
    )


def shape(*dims, kind=BF):
    return jax.ShapeDtypeStruct(dims, kind)


def after(value, *others):
    return lax.optimization_barrier((value, *others))[0]


def slot_tables(expert_ids, gates, numbers, capacity):
    tok_rows = expert_ids.shape[0]
    ids_t = expert_ids.T
    chosen = ids_t[None, :, :] == numbers[:, None, None]
    routed = jnp.any(chosen, axis=1)
    earlier = jnp.arange(tok_rows)[:, None] < jnp.arange(tok_rows)[None, :]
    order_in = jnp.dot(
        routed.astype(BF), earlier.astype(BF), preferred_element_type=F32
    ).astype(jnp.int32)
    weight = jnp.sum(jnp.where(chosen, gates.T[None, :, :], 0.0), axis=1)
    slot_ids = jnp.arange(capacity, dtype=jnp.int32)
    hits = routed[:, None, :] & (order_in[:, None, :] == slot_ids[None, :, None])
    slot_weight = jnp.sum(jnp.where(hits, weight[:, None, :], 0.0), axis=2)
    return hits.reshape(numbers.shape[0] * capacity, tok_rows).astype(BF), slot_weight.reshape(-1, 1)


def heading(e):
    return 1 - 2 * (e % 2)


class Ring:
    def __init__(self, nodes, planes):
        self.nodes, self.planes, self.half = nodes, planes, planes // 2
        self.cut = nodes // 2
        self.up_size = nodes * (self.half - 1) + self.cut
        self.down_size = nodes * (self.half - 1) + nodes - self.cut

    def shapes(self, capacity, width):
        return [
            shape(n, capacity, width) for n in (self.nodes, self.up_size, self.down_size)
        ]

    def place(self, refs, distance, value, columns=slice(None)):
        own, up, down = refs
        nodes, half = self.nodes, self.half
        if distance == 0:
            own[:, :, columns] = value
        elif distance < half:
            up[(distance - 1) * nodes : distance * nodes, :, columns] = value
        elif distance > half:
            back = self.planes - distance
            down[(back - 1) * nodes : back * nodes, :, columns] = value
        else:
            up[(half - 1) * nodes :, :, columns] = value[: self.cut]
            down[(half - 1) * nodes :, :, columns] = value[self.cut :]

    def pairs(self, way):
        count = lax.axis_size("edata")
        return [
            (p * count + e, (p + way * heading(e)) % self.planes * count + e)
            for p in range(self.planes)
            for e in range(count)
        ]

    def send(self, own, up, down):
        got = [own]
        for first, way, last in ((up, 1, self.cut), (down, -1, self.nodes - self.cut)):
            now = first
            for step in range(1, self.half + 1):
                now = lax.ppermute(now, ("local", "edata"), self.pairs(way))
                got.append(now)
                if step < self.half:
                    now = now[self.nodes :]
        return got

    def take(self, got, distance):
        nodes, half = self.nodes, self.half
        if distance == 0:
            return got[0][...]
        if distance < half:
            return got[distance][:nodes]
        if distance > half:
            return got[half + self.planes - distance][:nodes]
        return jnp.concatenate([got[half][...], got[2 * half][...]], axis=0)


def over_nodes(rows):
    return lax.all_to_all(rows, "node", split_axis=0, concat_axis=0, tiled=True)


def gathered(shard):
    count = lax.axis_size("edata")
    shards = [shard]
    for step in range(1, count):
        pairs = [((i + step) % count, i) for i in range(count)]
        shards.append(lax.ppermute(shard, "edata", pairs))
    return shards


def from_owner(piece, step):
    count = lax.axis_size("edata")
    return lax.ppermute(piece, "edata", [(i, (i + step) % count) for i in range(count)])


def column_tiles(width, most):
    count = lax.axis_size("edata")
    tile = min(most, width // count)
    steps = width // tile
    return tile, steps, lambda i, turn: (i + turn * (steps // count)) % steps


def dispatch_x(ring, turn, pick, tokens, capacity):
    slots, tok_rows = pick.shape
    width = tokens.shape[1]
    tile, steps, turned = column_tiles(width, 1024)
    size = ring.nodes * capacity

    def kernel(turn_ref, pick_ref, x_ref, *refs):
        rows = jnp.dot(pick_ref[...], x_ref[...], preferred_element_type=F32).astype(BF)
        for d in range(ring.planes):
            part = rows[d * size : (d + 1) * size]
            ring.place(refs, d, part.reshape(ring.nodes, capacity, tile))

    shapes = ring.shapes(capacity, width)
    return call(
        kernel,
        "dispatch_x",
        grid_spec=pltpu.PrefetchScalarGridSpec(
            num_scalar_prefetch=1,
            grid=(steps,),
            in_specs=[
                pl.BlockSpec((slots, tok_rows), lambda i, t: (0, 0)),
                pl.BlockSpec((tok_rows, tile), lambda i, t: (0, turned(i, t[0]))),
            ],
            out_specs=[pl.BlockSpec(s.shape[:2] + (tile,), lambda i, t: (0, 0, i)) for s in shapes],
        ),
        out_shape=shapes,
    )(turn, pick, tokens)


def dispatch_dy(ring, turn, pick, weight, out_grad, capacity):
    slots, tok_rows = pick.shape
    width = out_grad.shape[1]
    tile, steps, turned = column_tiles(width, 1024)
    size = ring.nodes * capacity

    def kernel(turn_ref, pick_ref, weight_ref, grad_ref, out_ref, rows_ref):
        rows = jnp.dot(pick_ref[...], grad_ref[...], preferred_element_type=F32)
        rows_ref[...] = rows.astype(BF)
        scaled = (weight_ref[...] * rows).astype(BF)
        for d in range(ring.planes):
            part = scaled[d * size : (d + 1) * size]
            out_ref[:, d] = part.reshape(ring.nodes, capacity, tile)

    return call(
        kernel,
        "dispatch_dy",
        grid_spec=pltpu.PrefetchScalarGridSpec(
            num_scalar_prefetch=1,
            grid=(steps,),
            in_specs=[
                pl.BlockSpec((slots, tok_rows), lambda i, t: (0, 0)),
                pl.BlockSpec((slots, 1), lambda i, t: (0, 0)),
                pl.BlockSpec((tok_rows, tile), lambda i, t: (0, turned(i, t[0]))),
            ],
            out_specs=[
                pl.BlockSpec(
                    (ring.nodes, ring.planes, capacity, tile), lambda i, t: (0, 0, 0, i)
                ),
                pl.BlockSpec((slots, tile), lambda i, t: (0, i)),
            ],
        ),
        out_shape=[
            shape(ring.nodes, ring.planes, capacity, width),
            shape(slots, width),
        ],
    )(turn, pick, weight, out_grad)


def pack(ring, got):
    _, capacity, width = got[0].shape
    tile = min(1024, width)

    def kernel(*refs):
        for d in range(ring.planes):
            refs[-1][:, d] = ring.take(refs[:-1], d)

    used = [ring.nodes]
    for last in (ring.cut, ring.nodes - ring.cut):
        used += [ring.nodes] * (ring.half - 1) + [last]
    return call(
        kernel,
        "pack",
        grid=(width // tile,),
        in_specs=[pl.BlockSpec((n, capacity, tile), lambda i: (0, 0, i)) for n in used],
        out_specs=pl.BlockSpec(
            (ring.nodes, ring.planes, capacity, tile), lambda i: (0, 0, 0, i)
        ),
        out_shape=shape(ring.nodes, ring.planes, capacity, width),
    )(*got)


def unpack(ring, rows, back):
    _, _, capacity, width = rows.shape
    tile = min(1024, width)

    def kernel(rows_ref, *refs):
        for d in range(ring.planes):
            ring.place(refs, -d % ring.planes if back else d, rows_ref[:, d])

    shapes = ring.shapes(capacity, width)
    return call(
        kernel,
        "unpack",
        grid=(width // tile,),
        in_specs=[
            pl.BlockSpec((ring.nodes, ring.planes, capacity, tile), lambda i: (0, 0, 0, i))
        ],
        out_specs=[pl.BlockSpec(s.shape[:2] + (tile,), lambda i: (0, 0, i)) for s in shapes],
        out_shape=shapes,
    )(rows)


def expert(ring, x_rows, dy_got, w_ins, w_outs):
    nodes, planes, capacity, model = x_rows.shape
    size = nodes * capacity
    rows = planes * size
    count = len(w_ins)
    width = model // count
    double, hidden = w_ins[0].shape[1], w_outs[0].shape[1]
    many = max(1, min(256, rows) // size)

    def kernel(x_ref, *refs):
        got, refs = refs[: len(dy_got)], refs[len(dy_got) :]
        ins, outs, refs = refs[:count], refs[count : 2 * count], refs[2 * count :]
        y_refs, (dx_ref, inner_ref, act_grad_ref, xs_ref, dys_ref, act_ref) = refs[:3], refs[3:]
        for first in range(0, planes, many):
            band = slice(first * size, (first + many) * size)
            for d in range(first, first + many):
                here = slice(d * size, (d + 1) * size)
                xs_ref[here] = x_ref[:, d].reshape(size, model)
                dys_ref[here] = ring.take(got, d).reshape(size, model)

            def product(source, weights):
                total = None
                for s in range(count):
                    one = jnp.dot(
                        source[band, s * width : (s + 1) * width],
                        weights[s][...],
                        preferred_element_type=F32,
                    )
                    total = one if total is None else total + one
                return total

            act_ref[...] = product(xs_ref, ins)
            act_gate = act_ref[:, :hidden]
            act_up = act_ref[:, hidden:]
            sig = jax.nn.sigmoid(act_gate)
            swished = act_gate * sig
            inner_ref[band] = (swished * act_up).astype(BF)
            inner_grad = product(dys_ref, outs)
            act_grad_ref[band, :hidden] = (
                inner_grad * act_up * sig * (1.0 + act_gate * (1.0 - sig))
            ).astype(BF)
            act_grad_ref[band, hidden:] = (inner_grad * swished).astype(BF)
            for s in range(count):
                columns = slice(s * width, (s + 1) * width)
                y = lax.dot_general(
                    inner_ref[band], outs[s][...], COLS_IN, preferred_element_type=F32
                ).astype(BF)
                dx = lax.dot_general(
                    act_grad_ref[band], ins[s][...], COLS_IN, preferred_element_type=F32
                ).astype(BF)
                for i in range(many):
                    d = first + i
                    part = slice(i * size, (i + 1) * size)
                    ring.place(
                        y_refs, -d % planes, y[part].reshape(nodes, capacity, width), columns
                    )
                    dx_ref[:, d, :, columns] = dx[part].reshape(nodes, capacity, width)

    operands = (x_rows, *dy_got, *w_ins, *w_outs)
    out_shape = [
        *ring.shapes(capacity, model),
        shape(nodes, planes, capacity, model),
        shape(rows, hidden),
        shape(rows, double),
        shape(rows, model),
        shape(rows, model),
    ]
    return call(
        kernel,
        "expert",
        in_specs=[VMEM] * len(operands),
        out_specs=[VMEM] * len(out_shape),
        out_shape=out_shape,
        scratch_shapes=[pltpu.VMEM((many * size, double), F32)],
    )(*operands)


def weight_grads(shard, xs, dys, inner, act_grad):
    rows, width = xs.shape
    size = width // lax.axis_size("edata")
    double, hidden = act_grad.shape[1], inner.shape[1]
    tile = min(256, size)
    steps = size // tile

    def kernel(x_ref, dy_ref, inner_ref, act_grad_ref, out_ref):
        out_ref[:, :double] = lax.dot_general(
            x_ref[...], act_grad_ref[...], ROWS_IN, preferred_element_type=F32
        ).astype(BF)
        out_ref[:, double:] = lax.dot_general(
            dy_ref[...], inner_ref[...], ROWS_IN, preferred_element_type=F32
        ).astype(BF)

    columns = pl.BlockSpec((rows, tile), lambda i: (0, shard * steps + i))
    return call(
        kernel,
        "weight_grads",
        grid=(steps,),
        in_specs=[
            columns,
            columns,
            pl.BlockSpec((rows, hidden), lambda i: (0, 0)),
            pl.BlockSpec((rows, double), lambda i: (0, 0)),
        ],
        out_specs=pl.BlockSpec((tile, double + hidden), lambda i: (i, 0)),
        out_shape=shape(size, double + hidden),
    )(xs, dys, inner, act_grad)


def combine(ring, turn, numbers, picks, ids_t, grad_rows, y_rows, dx_got):
    pick, pick_t, high_t, middle_t = picks
    slots, tok_rows = pick.shape
    nodes, planes, capacity, width = y_rows.shape
    size = nodes * capacity
    groups = nodes * planes
    tile, steps, turned = column_tiles(width, 512)

    def kernel(turn_ref, number_ref, pick_ref, pick_t_ref, high_ref, middle_ref, *refs):
        ids_ref, grad_ref, y_ref, *got = refs[:-4]
        mixed_ref, token_grad_ref, gate_grad_ref, dots_ref = refs[-4:]
        step = pl.program_id(0)
        order = [-d % planes for d in range(planes)]
        y = jnp.concatenate([y_ref[:, e].reshape(size, tile) for e in order], axis=0)
        dx = jnp.concatenate([ring.take(got, e).reshape(size, tile) for e in order], axis=0)
        mixed_ref[...] = (
            jnp.dot(high_ref[...], y, preferred_element_type=F32)
            + jnp.dot(middle_ref[...], y, preferred_element_type=F32)
        ).astype(BF)
        token_grad_ref[...] = jnp.dot(
            pick_t_ref[...], dx, preferred_element_type=F32
        ).astype(BF)
        dots = jnp.sum(y.astype(F32) * grad_ref[...].astype(F32), axis=1, keepdims=True)

        @pl.when(step == 0)
        def _():
            dots_ref[...] = dots

        @pl.when(step > 0)
        def _():
            dots_ref[...] += dots

        @pl.when(step == steps - 1)
        def _():
            by_token = pick_ref[...].astype(F32) * dots_ref[...]
            by_token = jnp.sum(by_token.reshape(groups, capacity, tok_rows), axis=1)
            ids = ids_ref[...]
            total = jnp.zeros(ids.shape, F32)
            for g in range(groups):
                total += jnp.where(ids == number_ref[g], by_token[g : g + 1], 0.0)
            gate_grad_ref[...] = total

    def whole(array):
        return pl.BlockSpec(array.shape, lambda i, t, n: (0, 0))

    used = [nodes]
    for last in (ring.cut, nodes - ring.cut):
        used += [nodes] * (ring.half - 1) + [last]
    turned_spec = pl.BlockSpec((tok_rows, tile), lambda i, t, n: (0, turned(i, t[0])))
    return call(
        kernel,
        "combine",
        grid_spec=pltpu.PrefetchScalarGridSpec(
            num_scalar_prefetch=2,
            grid=(steps,),
            in_specs=[whole(p) for p in picks]
            + [
                whole(ids_t),
                pl.BlockSpec((slots, tile), lambda i, t, n: (0, i)),
                pl.BlockSpec((nodes, planes, capacity, tile), lambda i, t, n: (0, 0, 0, i)),
            ]
            + [pl.BlockSpec((u, capacity, tile), lambda i, t, n: (0, 0, i)) for u in used],
            out_specs=[turned_spec, turned_spec, whole(ids_t)],
            scratch_shapes=[pltpu.VMEM((slots, 1), F32)],
        ),
        out_shape=[
            shape(tok_rows, width),
            shape(tok_rows, width),
            shape(*ids_t.shape, kind=F32),
        ],
    )(turn, numbers, *picks, ids_t, grad_rows, y_rows, *dx_got)


def shards(tokens, out_grad, expert_ids, gates, w_gate_up, w_down):
    nodes, planes = lax.axis_size("node"), lax.axis_size("local")
    groups = nodes * planes
    tok_rows = tokens.shape[0]
    capacity = tok_rows * expert_ids.shape[1] // (EXP_DEV * groups)
    ring = Ring(nodes, planes)
    turn = lax.axis_index("edata").astype(jnp.int32).reshape(1)
    w_ins = gathered(w_gate_up[0])
    w_outs = gathered(w_down[0])
    along = heading(lax.axis_index("edata")) * jnp.arange(planes, dtype=jnp.int32)
    plane = (lax.axis_index("local") + along + planes) % planes
    numbers = (plane[:, None] + planes * jnp.arange(nodes, dtype=jnp.int32)[None, :]).reshape(-1)
    pick, slot_weight = slot_tables(expert_ids, gates, numbers, capacity)

    x_own, x_up, x_down = dispatch_x(ring, turn, pick, tokens, capacity)
    pick2 = after(pick, x_own, x_up, x_down)
    dy_sent, grad_rows = dispatch_dy(ring, turn, pick2, slot_weight, out_grad, capacity)
    x_got = ring.send(x_own, x_up, x_down)
    dy_mid = over_nodes(dy_sent)
    *x_got, dy_mid = lax.optimization_barrier((*x_got, dy_mid))
    x_rows = over_nodes(pack(ring, x_got))
    dy_got = ring.send(*unpack(ring, dy_mid, False))
    *y_sent, dx_sent, inner, act_grad, xs, dys = expert(ring, x_rows, dy_got, w_ins, w_outs)
    y_got = ring.send(*y_sent)
    dx_mid = over_nodes(dx_sent)
    *y_got, dx_mid = lax.optimization_barrier((*y_got, dx_mid))
    y_packed = pack(ring, y_got)
    y_rows = over_nodes(y_packed)
    dx_sent = unpack(ring, dx_mid, True)
    dx_got = ring.send(*dx_sent)
    inner = after(inner, y_packed, *dx_sent)
    parts = []
    for shard in [*range(1, len(w_ins)), 0]:
        parts.append(weight_grads(shard, xs, dys, inner, act_grad))

    parts = [parts[-1]] + [from_owner(p, step) for step, p in enumerate(parts[:-1], 1)]
    double = w_gate_up.shape[2]
    sums = [
        sum(p[:, columns].astype(F32) for p in parts)
        for columns in (slice(0, double), slice(double, None))
    ]

    spread = pick.astype(F32) * after(slot_weight, y_got[1])
    high = lax.reduce_precision(spread, 8, 7)
    middle = (spread - high).astype(BF)
    picks = (pick, pick.T, high.astype(BF).T, middle.T)
    *dx_got, sums[0], sums[1] = lax.optimization_barrier((*dx_got, *sums))
    mixed, token_grad, gate_grad = combine(
        ring, turn, numbers, picks, expert_ids.T, grad_rows, y_rows, dx_got
    )
    return (mixed, token_grad, gate_grad.T, sums[0][None], sums[1][None])


def solution(mesh):
    rows = P(("node", "local", "edata"), None)
    weights = P(("node", "local"), "edata", None)
    return jax.shard_map(
        shards,
        mesh=mesh,
        in_specs=(rows, rows, rows, rows, weights, weights),
        out_specs=(rows, rows, rows, weights, weights),
        check_vma=False,
    )
```

```python
import jax
import jax.numpy as jnp
from jax import lax
from jax.experimental import pallas as pl
from jax.experimental.pallas import tpu as pltpu
from jax.sharding import PartitionSpec as P

EXP_DEV = 4
BF = jnp.bfloat16
F32 = jnp.float32
ROWS_IN = (((0,), (0,)), ((), ()))
COLS_IN = (((1,), (1,)), ((), ()))
LIMIT = 56 * 1024 * 1024
CHEAP = pl.CostEstimate(flops=1, bytes_accessed=1, transcendentals=0)
VMEM = pl.BlockSpec(memory_space=pltpu.VMEM)
SMEM = pl.BlockSpec(memory_space=pltpu.SMEM)
SHARE = 4


def call(kernel, name, **more):
    return pl.pallas_call(
        kernel,
        compiler_params=pltpu.CompilerParams(vmem_limit_bytes=LIMIT),
        cost_estimate=CHEAP,
        name=name,
        **more,
    )


def shape(*dims, kind=BF):
    return jax.ShapeDtypeStruct(dims, kind)


def after(value, *others):
    return lax.optimization_barrier((value, *others))[0]


def gathered(shard):
    count = lax.axis_size("edata")
    shards = [shard]
    for step in range(1, count):
        pairs = [((i + step) % count, i) for i in range(count)]
        shards.append(lax.ppermute(shard, "edata", pairs))
    return shards


def from_owner(piece, step):
    count = lax.axis_size("edata")
    return lax.ppermute(piece, "edata", [(i, (i + step) % count) for i in range(count)])


def exchange(everything, blocks):
    axes = ("node", "local")
    count = len(blocks)
    got = [blocks[0]]
    for j in range(1, count):
        got.append(lax.ppermute(blocks[j], axes, [(i, i ^ j) for i in range(count)]))
    return lax.all_to_all(everything, axes, split_axis=0, concat_axis=0, tiled=True), got


def slots_of(j, me, capacity):
    return pl.ds(pl.multiple_of((me ^ j) * capacity, capacity), capacity)


def shard_at(s, turn, count, width):
    return pl.ds(pl.multiple_of((turn + s) % count * width, width), width)


def dispatch(where, ids_t, gates_t, tokens, out_grad, groups, capacity):
    top, tok_rows = ids_t.shape
    model = tokens.shape[1]
    count = lax.axis_size("edata")
    width = model // count
    part = model // SHARE
    slots = groups * capacity

    def kernel(where_ref, ids_ref, gates_ref, x_ref, grad_ref, sent_ref, *refs):
        blocks, (rows_ref, pick_ref, weight_ref, dy_ref) = refs[:groups], refs[groups:]
        me, turn = where_ref[0], where_ref[1]
        numbers = lax.broadcasted_iota(jnp.int32, (groups, tok_rows), 0)
        routed = jnp.zeros((groups, tok_rows), F32)
        weight = jnp.zeros((groups, tok_rows), F32)
        for k in range(top):
            chosen = ids_ref[k : k + 1, :] == numbers
            routed = jnp.where(chosen, 1.0, routed)
            weight += jnp.where(chosen, gates_ref[k : k + 1, :], 0.0)
        first = lax.broadcasted_iota(jnp.int32, (tok_rows, tok_rows), 0)
        second = lax.broadcasted_iota(jnp.int32, (tok_rows, tok_rows), 1)
        earlier = jnp.where(first < second, 1.0, 0.0).astype(BF)
        order = jnp.dot(routed.astype(BF), earlier, preferred_element_type=F32)
        order = jnp.where(routed > 0.0, order, -1.0)
        places = lax.broadcasted_iota(jnp.int32, (capacity, tok_rows), 0).astype(F32)
        for g in range(groups):
            hits = order[g : g + 1, :] == places
            here = slice(g * capacity, (g + 1) * capacity)
            pick_ref[here] = jnp.where(hits, 1.0, 0.0).astype(BF)
            weight_ref[here] = jnp.sum(
                jnp.where(hits, weight[g : g + 1, :], 0.0), axis=1, keepdims=True
            )
        for s in range(count):
            source = shard_at(s, turn, count, width)
            here = slice(s * width, (s + 1) * width)
            x = jnp.dot(pick_ref[...], x_ref[:, source], preferred_element_type=F32).astype(BF)
            sent_ref[:, :, here] = x.reshape(groups, capacity, width)
            rows = jnp.dot(pick_ref[...], grad_ref[:, source], preferred_element_type=F32)
            rows_ref[:, here] = rows.astype(BF)
            dy_ref[:, here] = (weight_ref[...] * rows).astype(BF)
        sent_ref[:, :, model:] = dy_ref[:, :part].reshape(groups, capacity, part)
        for j, block in enumerate(blocks):
            block[...] = dy_ref[slots_of(j, me, capacity), part:]

    out_shape = [
        shape(groups, capacity, model + part),
        *[shape(capacity, model - part)] * groups,
        shape(slots, model),
        shape(slots, tok_rows),
        shape(slots, 1, kind=F32),
    ]
    sent, *blocks, rows, pick, weight = call(
        kernel,
        "dispatch",
        in_specs=[SMEM] + [VMEM] * 4,
        out_specs=[VMEM] * len(out_shape),
        out_shape=out_shape,
        scratch_shapes=[pltpu.VMEM((slots, model), BF)],
    )(where, ids_t, gates_t, tokens, out_grad)
    return sent, blocks, rows, pick, weight


def expert(where, got, got_blocks, w_ins, w_outs):
    groups, capacity, _ = got.shape
    count = len(w_ins)
    width = w_ins[0].shape[0]
    model = width * count
    part = model // SHARE
    double, hidden = w_ins[0].shape[1], w_outs[0].shape[1]
    slots = groups * capacity
    many = max(1, 256 // capacity)
    rows = many * capacity

    def kernel(where_ref, got_ref, *refs):
        got_blocks, refs = refs[:groups], refs[groups:]
        ins, outs, refs = refs[:count], refs[count : 2 * count], refs[2 * count :]
        back_ref, blocks, refs = refs[0], refs[1 : 1 + groups], refs[1 + groups :]
        inner_ref, act_grad_ref, dy_ref, dx_ref, act_ref = refs
        me = where_ref[0]
        dy_ref[:, :part] = got_ref[:, :, model:].reshape(slots, part)
        for j, block in enumerate(got_blocks):
            dy_ref[slots_of(j, me, capacity), part:] = block[...]
        for first in range(0, groups, many):
            theirs = slice(first, first + many)
            band = slice(first * capacity, first * capacity + rows)
            total = None
            for s in range(count):
                x = got_ref[theirs, :, s * width : (s + 1) * width].reshape(rows, width)
                one = jnp.dot(x, ins[s][...], preferred_element_type=F32)
                total = one if total is None else total + one
            act_ref[...] = total
            act_gate = act_ref[:, :hidden]
            act_up = act_ref[:, hidden:]
            sig = jax.nn.sigmoid(act_gate)
            swished = act_gate * sig
            inner_ref[band] = (swished * act_up).astype(BF)
            total = None
            for s in range(count):
                dy = dy_ref[band, s * width : (s + 1) * width]
                one = jnp.dot(dy, outs[s][...], preferred_element_type=F32)
                total = one if total is None else total + one
            act_grad_ref[band, :hidden] = (
                total * act_up * sig * (1.0 + act_gate * (1.0 - sig))
            ).astype(BF)
            act_grad_ref[band, hidden:] = (total * swished).astype(BF)
            for s in range(count):
                here = slice(s * width, (s + 1) * width)
                y = lax.dot_general(
                    inner_ref[band], outs[s][...], COLS_IN, preferred_element_type=F32
                )
                back_ref[theirs, :, here] = y.astype(BF).reshape(many, capacity, width)
                dx_ref[band, here] = lax.dot_general(
                    act_grad_ref[band], ins[s][...], COLS_IN, preferred_element_type=F32
                ).astype(BF)
        back_ref[:, :, model:] = dx_ref[:, :part].reshape(groups, capacity, part)
        for j, block in enumerate(blocks):
            block[...] = dx_ref[slots_of(j, me, capacity), part:]

    operands = (where, got, *got_blocks, *w_ins, *w_outs)
    out_shape = [
        shape(groups, capacity, model + part),
        *[shape(capacity, model - part)] * groups,
        shape(slots, hidden),
        shape(slots, double),
        shape(slots, model),
    ]
    back, *rest = call(
        kernel,
        "expert",
        in_specs=[SMEM] + [VMEM] * (len(operands) - 1),
        out_specs=[VMEM] * len(out_shape),
        out_shape=out_shape,
        scratch_shapes=[pltpu.VMEM((slots, model), BF), pltpu.VMEM((rows, double), F32)],
    )(*operands)
    return back, rest[:groups], *rest[groups:]


def weight_grads(shard, got, dys, inner, act_grad):
    groups, capacity, _ = got.shape
    slots, model = dys.shape
    size = model // lax.axis_size("edata")
    double, hidden = act_grad.shape[1], inner.shape[1]
    tile = min(256, size)
    steps = size // tile

    def kernel(x_ref, dy_ref, inner_ref, act_grad_ref, out_ref):
        x = x_ref[...].reshape(slots, tile)
        out_ref[:, :double] = lax.dot_general(
            x, act_grad_ref[...], ROWS_IN, preferred_element_type=F32
        ).astype(BF)
        out_ref[:, double:] = lax.dot_general(
            dy_ref[...], inner_ref[...], ROWS_IN, preferred_element_type=F32
        ).astype(BF)

    return call(
        kernel,
        "weight_grads",
        grid=(steps,),
        in_specs=[
            pl.BlockSpec((groups, capacity, tile), lambda i: (0, 0, shard * steps + i)),
            pl.BlockSpec((slots, tile), lambda i: (0, shard * steps + i)),
            pl.BlockSpec((slots, hidden), lambda i: (0, 0)),
            pl.BlockSpec((slots, double), lambda i: (0, 0)),
        ],
        out_specs=pl.BlockSpec((tile, double + hidden), lambda i: (i, 0)),
        out_shape=shape(size, double + hidden),
    )(got, dys, inner, act_grad)


def combine(where, picks, ids_t, grad_rows, back, back_blocks):
    groups, capacity, _ = back.shape
    slots, tok_rows = picks[0].shape
    model = grad_rows.shape[1]
    count = lax.axis_size("edata")
    width = model // count
    part = model // SHARE

    def kernel(where_ref, pick_ref, pick_t_ref, high_ref, middle_ref, ids_ref, *refs):
        rows_ref, back_ref, refs = refs[0], refs[1], refs[2:]
        blocks, (mixed_ref, token_grad_ref, gate_grad_ref, dx_ref) = refs[:groups], refs[groups:]
        me, turn = where_ref[0], where_ref[1]
        dx_ref[:, :part] = back_ref[:, :, model:].reshape(slots, part)
        for j, block in enumerate(blocks):
            dx_ref[slots_of(j, me, capacity), part:] = block[...]
        dots = jnp.zeros((slots, 1), F32)
        for s in range(count):
            here = slice(s * width, (s + 1) * width)
            target = shard_at(s, turn, count, width)
            y = back_ref[:, :, here].reshape(slots, width)
            mixed_ref[:, target] = (
                jnp.dot(high_ref[...], y, preferred_element_type=F32)
                + jnp.dot(middle_ref[...], y, preferred_element_type=F32)
            ).astype(BF)
            token_grad_ref[:, target] = jnp.dot(
                pick_t_ref[...], dx_ref[:, here], preferred_element_type=F32
            ).astype(BF)
            dots += jnp.sum(
                y.astype(F32) * rows_ref[:, here].astype(F32), axis=1, keepdims=True
            )
        by_token = pick_ref[...].astype(F32) * dots
        by_token = jnp.sum(by_token.reshape(groups, capacity, tok_rows), axis=1)
        ids = ids_ref[...]
        total = jnp.zeros(ids.shape, F32)
        for g in range(groups):
            total += jnp.where(ids == g, by_token[g : g + 1], 0.0)
        gate_grad_ref[...] = total

    operands = (where, *picks, ids_t, grad_rows, back, *back_blocks)
    return call(
        kernel,
        "combine",
        in_specs=[SMEM] + [VMEM] * (len(operands) - 1),
        out_specs=[VMEM] * 3,
        out_shape=[
            shape(tok_rows, model),
            shape(tok_rows, model),
            shape(*ids_t.shape, kind=F32),
        ],
        scratch_shapes=[pltpu.VMEM((slots, model), BF)],
    )(*operands)


def shards(tokens, out_grad, expert_ids, gates, w_gate_up, w_down):
    groups = lax.axis_size("node") * lax.axis_size("local")
    tok_rows = tokens.shape[0]
    capacity = tok_rows * expert_ids.shape[1] // (EXP_DEV * groups)
    where = jnp.stack([lax.axis_index(("node", "local")), lax.axis_index("edata")])
    where = where.astype(jnp.int32)
    w_ins = gathered(w_gate_up[0])
    w_outs = gathered(w_down[0])
    ids_t = expert_ids.T
    sent, blocks, grad_rows, pick, slot_weight = dispatch(
        where, ids_t, gates.T, tokens, out_grad, groups, capacity
    )
    for j in range(4, groups):
        blocks[j] = after(blocks[j], *w_ins[1:], *w_outs[1:])
    got, got_blocks = exchange(sent, blocks)
    sent, blocks, inner, act_grad, dys = expert(where, got, got_blocks, w_ins, w_outs)
    back, back_blocks = exchange(sent, blocks)

    inner = after(inner, back_blocks[1])
    parts = []
    for shard in [*range(1, len(w_ins)), 0]:
        parts.append(weight_grads(shard, got, dys, inner, act_grad))
    parts = [parts[-1]] + [from_owner(p, step) for step, p in enumerate(parts[:-1], 1)]
    double = w_gate_up.shape[2]
    sums = [
        sum(p[:, columns].astype(F32) for p in parts)
        for columns in (slice(0, double), slice(double, None))
    ]
    spread = pick.astype(F32) * after(slot_weight, inner)
    high = lax.reduce_precision(spread, 8, 7)
    middle = (spread - high).astype(BF)
    picks = (pick, pick.T, high.astype(BF).T, middle.T)
    *back_blocks, sums[0], sums[1] = lax.optimization_barrier((*back_blocks, *sums))
    mixed, token_grad, gate_grad = combine(where, picks, ids_t, grad_rows, back, back_blocks)
    return (mixed, token_grad, gate_grad.T, sums[0][None], sums[1][None])


def solution(mesh):
    rows = P(("node", "local", "edata"), None)
    weights = P(("node", "local"), "edata", None)
    return jax.shard_map(
        shards,
        mesh=mesh,
        in_specs=(rows, rows, rows, rows, weights, weights),
        out_specs=(rows, rows, rows, weights, weights),
        check_vma=False,
    )
```

```python
import jax
import jax.numpy as jnp
from jax import lax
from jax.experimental import pallas as pl
from jax.experimental.pallas import tpu as pltpu
from jax.sharding import PartitionSpec as P

EXP_DEV = 4
BF = jnp.bfloat16
F32 = jnp.float32
ROWS_IN = (((0,), (0,)), ((), ()))
COLS_IN = (((1,), (1,)), ((), ()))
LIMIT = 56 * 1024 * 1024
def work(flops):
    return pl.CostEstimate(flops=flops, bytes_accessed=flops // 400, transcendentals=0)


WINDOW = 4
CHEAP = pl.CostEstimate(flops=1, bytes_accessed=1, transcendentals=0)
VMEM = pl.BlockSpec(memory_space=pltpu.VMEM)
SMEM = pl.BlockSpec(memory_space=pltpu.SMEM)
def call(kernel, name, cost=CHEAP, **more):
    return pl.pallas_call(
        kernel,
        compiler_params=pltpu.CompilerParams(vmem_limit_bytes=LIMIT),
        cost_estimate=cost,
        name=name,
        **more,
    )


def shape(*dims, kind=BF):
    return jax.ShapeDtypeStruct(dims, kind)


def after(value, *others):
    return lax.optimization_barrier((value, *others))[0]


def gathered(shard):
    count = lax.axis_size("edata")
    shards = [shard]
    for step in range(1, count):
        pairs = [((i + step) % count, i) for i in range(count)]
        shards.append(lax.ppermute(shard, "edata", pairs))
    return shards


def from_owner(piece, step):
    count = lax.axis_size("edata")
    return lax.ppermute(piece, "edata", [(i, (i + step) % count) for i in range(count)])


def to_partner(block, j):
    if j == 0:
        return block
    count = lax.axis_size("node") * lax.axis_size("local")
    return lax.ppermute(block, ("node", "local"), [(i, i ^ j) for i in range(count)])


def shard_at(s, turn, count, width):
    return pl.ds(pl.multiple_of((turn + s) % count * width, width), width)


def dispatch(where, ids_t, gates_t, tokens, out_grad, groups, capacity):
    top, tok_rows = ids_t.shape
    model = tokens.shape[1]
    count = lax.axis_size("edata")
    width = model // count
    slots = groups * capacity

    def kernel(where_ref, ids_ref, gates_ref, x_ref, grad_ref, *refs):
        blocks, (rows_ref, pick_ref, weight_ref) = refs[:groups], refs[groups:]
        me, turn = where_ref[0], where_ref[1]
        numbers = me ^ lax.broadcasted_iota(jnp.int32, (groups, tok_rows), 0)
        routed = jnp.zeros((groups, tok_rows), F32)
        weight = jnp.zeros((groups, tok_rows), F32)
        for k in range(top):
            chosen = ids_ref[k : k + 1, :] == numbers
            routed = jnp.where(chosen, 1.0, routed)
            weight += jnp.where(chosen, gates_ref[k : k + 1, :], 0.0)
        first = lax.broadcasted_iota(jnp.int32, (tok_rows, tok_rows), 0)
        second = lax.broadcasted_iota(jnp.int32, (tok_rows, tok_rows), 1)
        earlier = jnp.where(first < second, 1.0, 0.0).astype(BF)
        order = jnp.dot(routed.astype(BF), earlier, preferred_element_type=F32)
        order = jnp.where(routed > 0.0, order, -1.0)
        places = lax.broadcasted_iota(jnp.int32, (capacity, tok_rows), 0).astype(F32)
        for g in range(groups):
            hits = order[g : g + 1, :] == places
            here = slice(g * capacity, (g + 1) * capacity)
            pick_ref[here] = jnp.where(hits, 1.0, 0.0).astype(BF)
            weight_ref[here] = jnp.sum(
                jnp.where(hits, weight[g : g + 1, :], 0.0), axis=1, keepdims=True
            )
        for s in range(count):
            source = shard_at(s, turn, count, width)
            here = slice(s * width, (s + 1) * width)
            x = jnp.dot(pick_ref[...], x_ref[:, source], preferred_element_type=F32).astype(BF)
            rows = jnp.dot(pick_ref[...], grad_ref[:, source], preferred_element_type=F32)
            rows_ref[:, here] = rows.astype(BF)
            dy = (weight_ref[...] * rows).astype(BF)
            for j, block in enumerate(blocks):
                block[0, :, here] = x[j * capacity : (j + 1) * capacity]
                block[1, :, here] = dy[j * capacity : (j + 1) * capacity]

    out_shape = [
        *[shape(2, capacity, model)] * groups,
        shape(slots, model),
        shape(slots, tok_rows),
        shape(slots, 1, kind=F32),
    ]
    *blocks, rows, pick, weight = call(
        kernel,
        "dispatch",
        in_specs=[SMEM] + [VMEM] * 4,
        out_specs=[VMEM] * len(out_shape),
        out_shape=out_shape,
    )(where, ids_t, gates_t, tokens, out_grad)
    return list(blocks), rows, pick, weight


def expert(got, w_ins, w_outs):
    _, capacity, model = got[0].shape
    many = len(got)
    count = len(w_ins)
    width = w_ins[0].shape[0]
    double, hidden = w_ins[0].shape[1], w_outs[0].shape[1]
    rows = many * capacity

    def kernel(*refs):
        got, refs = refs[:many], refs[many:]
        ins, outs, refs = refs[:count], refs[count : 2 * count], refs[2 * count :]
        blocks, (inner_ref, act_grad_ref, x_ref, dy_ref, act_ref) = refs[:many], refs[many:]
        for j, block in enumerate(got):
            x_ref[j * capacity : (j + 1) * capacity] = block[0]
            dy_ref[j * capacity : (j + 1) * capacity] = block[1]

        def product(source, weights):
            total = None
            for s in range(count):
                one = jnp.dot(
                    source[:, s * width : (s + 1) * width],
                    weights[s][...],
                    preferred_element_type=F32,
                )
                total = one if total is None else total + one
            return total

        act_ref[...] = product(x_ref, ins)
        act_gate = act_ref[:, :hidden]
        act_up = act_ref[:, hidden:]
        sig = jax.nn.sigmoid(act_gate)
        swished = act_gate * sig
        inner_ref[...] = (swished * act_up).astype(BF)
        inner_grad = product(dy_ref, outs)
        act_grad_ref[:, :hidden] = (
            inner_grad * act_up * sig * (1.0 + act_gate * (1.0 - sig))
        ).astype(BF)
        act_grad_ref[:, hidden:] = (inner_grad * swished).astype(BF)
        for s in range(count):
            here = slice(s * width, (s + 1) * width)
            y = lax.dot_general(
                inner_ref[...], outs[s][...], COLS_IN, preferred_element_type=F32
            ).astype(BF)
            dx = lax.dot_general(
                act_grad_ref[...], ins[s][...], COLS_IN, preferred_element_type=F32
            ).astype(BF)
            for j, block in enumerate(blocks):
                block[0, :, here] = y[j * capacity : (j + 1) * capacity]
                block[1, :, here] = dx[j * capacity : (j + 1) * capacity]

    operands = (*got, *w_ins, *w_outs)
    out_shape = [
        *[shape(2, capacity, model)] * many,
        shape(rows, hidden),
        shape(rows, double),
        shape(rows, model),
        shape(rows, model),
    ]
    results = call(
        kernel,
        "expert",
        cost=work(12 * rows * model * hidden),
        in_specs=[VMEM] * len(operands),
        out_specs=[VMEM] * len(out_shape),
        out_shape=out_shape,
        scratch_shapes=[pltpu.VMEM((rows, double), F32)],
    )(*operands)
    return list(results[:many]), results[many:]


def weight_grads(shard, bands):
    rows, model = bands[0][3].shape
    hidden, double = bands[0][0].shape[1], bands[0][1].shape[1]
    size = model // lax.axis_size("edata")
    tile = min(256, size)
    steps = size // tile
    count = len(bands)

    def kernel(*refs):
        inners, act_grads = refs[:count], refs[count : 2 * count]
        xs, dys, out_ref = refs[2 * count : 3 * count], refs[3 * count : 4 * count], refs[-1]
        for rights, lefts, columns in (
            (act_grads, xs, slice(0, double)),
            (inners, dys, slice(double, None)),
        ):
            total = None
            for left, right in zip(lefts, rights):
                one = lax.dot_general(
                    left[...], right[...], ROWS_IN, preferred_element_type=F32
                )
                total = one if total is None else total + one
            out_ref[:, columns] = total.astype(BF)

    tall = pl.BlockSpec((rows, tile), lambda i: (0, shard * steps + i))
    return call(
        kernel,
        "weight_grads",
        cost=work(6 * count * rows * size * hidden),
        grid=(steps,),
        in_specs=[pl.BlockSpec((rows, hidden), lambda i: (0, 0))] * count
        + [pl.BlockSpec((rows, double), lambda i: (0, 0))] * count
        + [tall] * (2 * count),
        out_specs=pl.BlockSpec((tile, double + hidden), lambda i: (i, 0)),
        out_shape=shape(size, double + hidden),
    )(*[band[i] for i in range(4) for band in bands])


def combine(where, picks, ids_t, grad_rows, blocks):
    groups = len(blocks)
    _, capacity, model = blocks[0].shape
    slots, tok_rows = picks[0].shape
    count = lax.axis_size("edata")
    width = model // count

    def kernel(where_ref, pick_ref, pick_t_ref, high_ref, middle_ref, ids_ref, rows_ref, *refs):
        blocks, (mixed_ref, token_grad_ref, gate_grad_ref) = refs[:groups], refs[groups:]
        me, turn = where_ref[0], where_ref[1]
        dots = jnp.zeros((slots, 1), F32)
        for s in range(count):
            here = slice(s * width, (s + 1) * width)
            target = shard_at(s, turn, count, width)
            y = jnp.concatenate([block[0, :, here] for block in blocks], axis=0)
            mixed_ref[:, target] = (
                jnp.dot(high_ref[...], y, preferred_element_type=F32)
                + jnp.dot(middle_ref[...], y, preferred_element_type=F32)
            ).astype(BF)
            dots += jnp.sum(
                y.astype(F32) * rows_ref[:, here].astype(F32), axis=1, keepdims=True
            )
            dx = jnp.concatenate([block[1, :, here] for block in blocks], axis=0)
            token_grad_ref[:, target] = jnp.dot(
                pick_t_ref[...], dx, preferred_element_type=F32
            ).astype(BF)
        by_token = pick_ref[...].astype(F32) * dots
        by_token = jnp.sum(by_token.reshape(groups, capacity, tok_rows), axis=1)
        ids = ids_ref[...]
        total = jnp.zeros(ids.shape, F32)
        for g in range(groups):
            total += jnp.where(ids == (me ^ g), by_token[g : g + 1], 0.0)
        gate_grad_ref[...] = total

    operands = (where, *picks, ids_t, grad_rows, *blocks)
    return call(
        kernel,
        "combine",
        in_specs=[SMEM] + [VMEM] * (len(operands) - 1),
        out_specs=[VMEM] * 3,
        out_shape=[
            shape(tok_rows, model),
            shape(tok_rows, model),
            shape(*ids_t.shape, kind=F32),
        ],
    )(*operands)


def shards(tokens, out_grad, expert_ids, gates, w_gate_up, w_down):
    groups = lax.axis_size("node") * lax.axis_size("local")
    half, quarter = groups // 2, groups // 4
    tok_rows = tokens.shape[0]
    capacity = tok_rows * expert_ids.shape[1] // (EXP_DEV * groups)
    where = jnp.stack([lax.axis_index(("node", "local")), lax.axis_index("edata")])
    where = where.astype(jnp.int32)
    w_ins = gathered(w_gate_up[0])
    w_outs = gathered(w_down[0])
    ids_t = expert_ids.T
    blocks, grad_rows, pick, slot_weight = dispatch(
        where, ids_t, gates.T, tokens, out_grad, groups, capacity
    )
    for j in range(quarter, groups):
        blocks[j] = after(blocks[j], *w_ins[1:], *w_outs[1:])
    got = [to_partner(blocks[j], j) for j in range(half + quarter)]
    sent, first = expert(got[:half], w_ins, w_outs)
    for j in range(half + quarter, groups):
        got.append(to_partner(after(blocks[j], sent[0]), j))
    more, second = expert(got[half:], w_ins, w_outs)
    back = []
    for j, block in enumerate([*sent, *more]):
        if j == 1:
            block = after(block, got[half + quarter - 1])
        elif j > WINDOW:
            block = after(block, *back[max(1, j - WINDOW - 1) : j - WINDOW + 1])
        back.append(to_partner(block, j))

    parts = []
    for shard in [*range(1, len(w_ins)), 0]:
        hint = back[1:half] if shard > 0 else back[half : half + quarter]
        band = [after(first[0], *hint), *first[1:]]
        parts.append(weight_grads(shard, [band, second]))
    parts = [parts[-1]] + [from_owner(p, step) for step, p in enumerate(parts[:-1], 1)]
    double = w_gate_up.shape[2]
    sums = [
        sum(p[:, columns].astype(F32) for p in parts)
        for columns in (slice(0, double), slice(double, None))
    ]
    spread = pick.astype(F32) * after(slot_weight, first[0])
    high = lax.reduce_precision(spread, 8, 7)
    middle = (spread - high).astype(BF)
    picks = (pick, pick.T, high.astype(BF).T, middle.T)
    *back, sums[0], sums[1] = lax.optimization_barrier((*back, *sums))
    mixed, token_grad, gate_grad = combine(where, picks, ids_t, grad_rows, back)
    return (mixed, token_grad, gate_grad.T, sums[0][None], sums[1][None])


def solution(mesh):
    rows = P(("node", "local", "edata"), None)
    weights = P(("node", "local"), "edata", None)
    return jax.shard_map(
        shards,
        mesh=mesh,
        in_specs=(rows, rows, rows, rows, weights, weights),
        out_specs=(rows, rows, rows, weights, weights),
        check_vma=False,
    )
```

```python
import jax
import jax.numpy as jnp
from jax import lax
from jax.experimental import pallas as pl
from jax.experimental.pallas import tpu as pltpu
from jax.sharding import PartitionSpec as P

EXP_DEV = 4
BF = jnp.bfloat16
F32 = jnp.float32
ROWS_IN = (((0,), (0,)), ((), ()))
COLS_IN = (((1,), (1,)), ((), ()))
LIMIT = 56 * 1024 * 1024
def work(flops):
    return pl.CostEstimate(flops=flops, bytes_accessed=flops // 400, transcendentals=0)


WINDOW = 4
CHEAP = pl.CostEstimate(flops=1, bytes_accessed=1, transcendentals=0)
VMEM = pl.BlockSpec(memory_space=pltpu.VMEM)
SMEM = pl.BlockSpec(memory_space=pltpu.SMEM)
def call(kernel, name, cost=CHEAP, **more):
    return pl.pallas_call(
        kernel,
        compiler_params=pltpu.CompilerParams(vmem_limit_bytes=LIMIT),
        cost_estimate=cost,
        name=name,
        **more,
    )


def shape(*dims, kind=BF):
    return jax.ShapeDtypeStruct(dims, kind)


def after(value, *others):
    return lax.optimization_barrier((value, *others))[0]


def gathered(shard):
    count = lax.axis_size("edata")
    shards = [shard]
    for step in range(1, count):
        pairs = [((i + step) % count, i) for i in range(count)]
        shards.append(lax.ppermute(shard, "edata", pairs))
    return shards


def from_owner(piece, step):
    count = lax.axis_size("edata")
    return lax.ppermute(piece, "edata", [(i, (i + step) % count) for i in range(count)])


def to_partner(block, j):
    if j == 0:
        return block
    count = lax.axis_size("node") * lax.axis_size("local")
    return lax.ppermute(block, ("node", "local"), [(i, i ^ j) for i in range(count)])


def shard_at(s, turn, count, width):
    return pl.ds(pl.multiple_of((turn + s) % count * width, width), width)


def dispatch(where, ids_t, gates_t, tokens, out_grad, groups, capacity):
    top, tok_rows = ids_t.shape
    model = tokens.shape[1]
    count = lax.axis_size("edata")
    width = model // count
    slots = groups * capacity

    def kernel(where_ref, ids_ref, gates_ref, x_ref, grad_ref, *refs):
        blocks, (rows_ref, pick_ref, weight_ref) = refs[:groups], refs[groups:]
        me, turn = where_ref[0], where_ref[1]
        numbers = me ^ lax.broadcasted_iota(jnp.int32, (groups, tok_rows), 0)
        routed = jnp.zeros((groups, tok_rows), F32)
        weight = jnp.zeros((groups, tok_rows), F32)
        for k in range(top):
            chosen = ids_ref[k : k + 1, :] == numbers
            routed = jnp.where(chosen, 1.0, routed)
            weight += jnp.where(chosen, gates_ref[k : k + 1, :], 0.0)
        first = lax.broadcasted_iota(jnp.int32, (tok_rows, tok_rows), 0)
        second = lax.broadcasted_iota(jnp.int32, (tok_rows, tok_rows), 1)
        earlier = jnp.where(first < second, 1.0, 0.0).astype(BF)
        order = jnp.dot(routed.astype(BF), earlier, preferred_element_type=F32)
        order = jnp.where(routed > 0.0, order, -1.0)
        places = lax.broadcasted_iota(jnp.int32, (capacity, tok_rows), 0).astype(F32)
        for g in range(groups):
            hits = order[g : g + 1, :] == places
            here = slice(g * capacity, (g + 1) * capacity)
            pick_ref[here] = jnp.where(hits, 1.0, 0.0).astype(BF)
            weight_ref[here] = jnp.sum(
                jnp.where(hits, weight[g : g + 1, :], 0.0), axis=1, keepdims=True
            )
        for s in range(count):
            source = shard_at(s, turn, count, width)
            here = slice(s * width, (s + 1) * width)
            x = jnp.dot(pick_ref[...], x_ref[:, source], preferred_element_type=F32).astype(BF)
            rows = jnp.dot(pick_ref[...], grad_ref[:, source], preferred_element_type=F32)
            rows_ref[:, here] = rows.astype(BF)
            dy = (weight_ref[...] * rows).astype(BF)
            for j, block in enumerate(blocks):
                block[0, :, here] = x[j * capacity : (j + 1) * capacity]
                block[1, :, here] = dy[j * capacity : (j + 1) * capacity]

    out_shape = [
        *[shape(2, capacity, model)] * groups,
        shape(slots, model),
        shape(slots, tok_rows),
        shape(slots, 1, kind=F32),
    ]
    *blocks, rows, pick, weight = call(
        kernel,
        "dispatch",
        in_specs=[SMEM] + [VMEM] * 4,
        out_specs=[VMEM] * len(out_shape),
        out_shape=out_shape,
    )(where, ids_t, gates_t, tokens, out_grad)
    return list(blocks), rows, pick, weight


def expert(got, w_ins, w_outs):
    _, capacity, model = got[0].shape
    many = len(got)
    count = len(w_ins)
    width = w_ins[0].shape[0]
    double, hidden = w_ins[0].shape[1], w_outs[0].shape[1]
    rows = many * capacity

    def kernel(*refs):
        got, refs = refs[:many], refs[many:]
        ins, outs, refs = refs[:count], refs[count : 2 * count], refs[2 * count :]
        blocks, (inner_ref, act_grad_ref, x_ref, dy_ref, act_ref) = refs[:many], refs[many:]
        for j, block in enumerate(got):
            x_ref[j * capacity : (j + 1) * capacity] = block[0]
            dy_ref[j * capacity : (j + 1) * capacity] = block[1]

        def product(source, weights):
            total = None
            for s in range(count):
                one = jnp.dot(
                    source[:, s * width : (s + 1) * width],
                    weights[s][...],
                    preferred_element_type=F32,
                )
                total = one if total is None else total + one
            return total

        act_ref[...] = product(x_ref, ins)
        act_gate = act_ref[:, :hidden]
        act_up = act_ref[:, hidden:]
        sig = jax.nn.sigmoid(act_gate)
        swished = act_gate * sig
        inner_ref[...] = (swished * act_up).astype(BF)
        inner_grad = product(dy_ref, outs)
        act_grad_ref[:, :hidden] = (
            inner_grad * act_up * sig * (1.0 + act_gate * (1.0 - sig))
        ).astype(BF)
        act_grad_ref[:, hidden:] = (inner_grad * swished).astype(BF)
        for s in range(count):
            here = slice(s * width, (s + 1) * width)
            y = lax.dot_general(
                inner_ref[...], outs[s][...], COLS_IN, preferred_element_type=F32
            ).astype(BF)
            dx = lax.dot_general(
                act_grad_ref[...], ins[s][...], COLS_IN, preferred_element_type=F32
            ).astype(BF)
            for j, block in enumerate(blocks):
                block[0, :, here] = y[j * capacity : (j + 1) * capacity]
                block[1, :, here] = dx[j * capacity : (j + 1) * capacity]

    operands = (*got, *w_ins, *w_outs)
    out_shape = [
        *[shape(2, capacity, model)] * many,
        shape(rows, hidden),
        shape(rows, double),
        shape(rows, model),
        shape(rows, model),
    ]
    results = call(
        kernel,
        "expert",
        cost=work(12 * rows * model * hidden),
        in_specs=[VMEM] * len(operands),
        out_specs=[VMEM] * len(out_shape),
        out_shape=out_shape,
        scratch_shapes=[pltpu.VMEM((rows, double), F32)],
    )(*operands)
    return list(results[:many]), results[many:]


def weight_grads(shard, bands):
    rows, model = bands[0][3].shape
    hidden, double = bands[0][0].shape[1], bands[0][1].shape[1]
    size = model // lax.axis_size("edata")
    tile = min(256, size)
    steps = size // tile
    count = len(bands)

    def kernel(*refs):
        inners, act_grads = refs[:count], refs[count : 2 * count]
        xs, dys, out_ref = refs[2 * count : 3 * count], refs[3 * count : 4 * count], refs[-1]
        for rights, lefts, columns in (
            (act_grads, xs, slice(0, double)),
            (inners, dys, slice(double, None)),
        ):
            total = None
            for left, right in zip(lefts, rights):
                one = lax.dot_general(
                    left[...], right[...], ROWS_IN, preferred_element_type=F32
                )
                total = one if total is None else total + one
            out_ref[:, columns] = total.astype(BF)

    tall = pl.BlockSpec((rows, tile), lambda i: (0, shard * steps + i))
    return call(
        kernel,
        "weight_grads",
        cost=work(6 * count * rows * size * hidden),
        grid=(steps,),
        in_specs=[pl.BlockSpec((rows, hidden), lambda i: (0, 0))] * count
        + [pl.BlockSpec((rows, double), lambda i: (0, 0))] * count
        + [tall] * (2 * count),
        out_specs=pl.BlockSpec((tile, double + hidden), lambda i: (i, 0)),
        out_shape=shape(size, double + hidden),
    )(*[band[i] for i in range(4) for band in bands])


def combine(where, picks, ids_t, grad_rows, blocks):
    groups = len(blocks)
    _, capacity, model = blocks[0].shape
    slots, tok_rows = picks[0].shape
    count = lax.axis_size("edata")
    width = model // count

    def kernel(where_ref, pick_ref, pick_t_ref, high_ref, middle_ref, ids_ref, rows_ref, *refs):
        blocks, (mixed_ref, token_grad_ref, gate_grad_ref) = refs[:groups], refs[groups:]
        me, turn = where_ref[0], where_ref[1]
        dots = jnp.zeros((slots, 1), F32)
        for s in range(count):
            here = slice(s * width, (s + 1) * width)
            target = shard_at(s, turn, count, width)
            y = jnp.concatenate([block[0, :, here] for block in blocks], axis=0)
            mixed_ref[:, target] = (
                jnp.dot(high_ref[...], y, preferred_element_type=F32)
                + jnp.dot(middle_ref[...], y, preferred_element_type=F32)
            ).astype(BF)
            dots += jnp.sum(
                y.astype(F32) * rows_ref[:, here].astype(F32), axis=1, keepdims=True
            )
            dx = jnp.concatenate([block[1, :, here] for block in blocks], axis=0)
            token_grad_ref[:, target] = jnp.dot(
                pick_t_ref[...], dx, preferred_element_type=F32
            ).astype(BF)
        by_token = pick_ref[...].astype(F32) * dots
        by_token = jnp.sum(by_token.reshape(groups, capacity, tok_rows), axis=1)
        ids = ids_ref[...]
        total = jnp.zeros(ids.shape, F32)
        for g in range(groups):
            total += jnp.where(ids == (me ^ g), by_token[g : g + 1], 0.0)
        gate_grad_ref[...] = total

    operands = (where, *picks, ids_t, grad_rows, *blocks)
    return call(
        kernel,
        "combine",
        in_specs=[SMEM] + [VMEM] * (len(operands) - 1),
        out_specs=[VMEM] * 3,
        out_shape=[
            shape(tok_rows, model),
            shape(tok_rows, model),
            shape(*ids_t.shape, kind=F32),
        ],
    )(*operands)


def shards(tokens, out_grad, expert_ids, gates, w_gate_up, w_down):
    groups = lax.axis_size("node") * lax.axis_size("local")
    half, quarter = groups // 2, groups // 4
    tok_rows = tokens.shape[0]
    capacity = tok_rows * expert_ids.shape[1] // (EXP_DEV * groups)
    where = jnp.stack([lax.axis_index(("node", "local")), lax.axis_index("edata")])
    where = where.astype(jnp.int32)
    w_ins = gathered(w_gate_up[0])
    w_outs = gathered(w_down[0])
    ids_t = expert_ids.T
    blocks, grad_rows, pick, slot_weight = dispatch(
        where, ids_t, gates.T, tokens, out_grad, groups, capacity
    )
    planes = lax.axis_size("local")
    hops = [min(j % planes, 2 if j % planes == planes // 2 else 1) for j in range(groups)]
    low, high = range(half), range(half, groups)
    late = sorted(high, key=lambda j: -hops[j])
    early = [j for j in low if j]
    arrived = []

    def move(block, j, *needs):
        if len(arrived) >= WINDOW:
            needs += tuple(arrived[-WINDOW - 1 : len(arrived) - WINDOW + 1])
        arrived.append(to_partner(after(block, *needs) if needs else block, j))
        return arrived[-1]

    got = {0: blocks[0]}
    for i, j in enumerate(early):
        got[j] = move(blocks[j], j, *(w_ins[1:] + w_outs[1:] if i == quarter - 1 else ()))
    for j in late[:quarter]:
        got[j] = move(blocks[j], j)
    sent, first = expert([got[j] for j in low], w_ins, w_outs)
    for j in late[quarter:]:
        got[j] = move(blocks[j], j, sent[0])
    more, second = expert([got[j] for j in high], w_ins, w_outs)
    front = sorted(early, key=lambda j: -hops[j])
    results = [*sent, *more]
    back = {0: results[0]}
    for i, j in enumerate(front + late):
        back[j] = move(results[j], j, *(more[:1] if i >= WINDOW else ()))

    parts = []
    hint = [back[j] for j in front]
    for shard in [*range(1, len(w_ins)), 0]:
        band = [after(first[0], *hint), *first[1:]]
        parts.append(weight_grads(shard, [band, second]))
        hint = [parts[-1]]
    middle = late[1 : quarter]
    held = lax.optimization_barrier((*parts, *[back[j] for j in middle]))
    parts = list(held[: len(parts)])
    for j, block in zip(middle, held[len(parts) :]):
        back[j] = block
    back = [back[j] for j in range(groups)]
    parts = [parts[-1]] + [from_owner(p, step) for step, p in enumerate(parts[:-1], 1)]
    double = w_gate_up.shape[2]
    sums = [
        sum(p[:, columns].astype(F32) for p in parts)
        for columns in (slice(0, double), slice(double, None))
    ]
    spread = pick.astype(F32) * after(slot_weight, first[0])
    high = lax.reduce_precision(spread, 8, 7)
    middle = (spread - high).astype(BF)
    picks = (pick, pick.T, high.astype(BF).T, middle.T)
    *back, sums[0], sums[1] = lax.optimization_barrier((*back, *sums))
    mixed, token_grad, gate_grad = combine(where, picks, ids_t, grad_rows, back)
    return (mixed, token_grad, gate_grad.T, sums[0][None], sums[1][None])


def solution(mesh):
    rows = P(("node", "local", "edata"), None)
    weights = P(("node", "local"), "edata", None)
    return jax.shard_map(
        shards,
        mesh=mesh,
        in_specs=(rows, rows, rows, rows, weights, weights),
        out_specs=(rows, rows, rows, weights, weights),
        check_vma=False,
    )
```

```python
import jax
import jax.numpy as jnp
from jax import lax
from jax.experimental import pallas as pl
from jax.experimental.pallas import tpu as pltpu
from jax.sharding import PartitionSpec as P

EXP_DEV = 4
BF = jnp.bfloat16
F32 = jnp.float32
ROWS_IN = (((0,), (0,)), ((), ()))
COLS_IN = (((1,), (1,)), ((), ()))
LIMIT = 56 * 1024 * 1024
CHEAP = pl.CostEstimate(flops=1, bytes_accessed=1, transcendentals=0)
VMEM = pl.BlockSpec(memory_space=pltpu.VMEM)
SMEM = pl.BlockSpec(memory_space=pltpu.SMEM)


def call(kernel, name, cost=CHEAP, **more):
    return pl.pallas_call(
        kernel,
        compiler_params=pltpu.CompilerParams(vmem_limit_bytes=LIMIT),
        cost_estimate=cost,
        name=name,
        **more,
    )


def shape(*dims, kind=BF):
    return jax.ShapeDtypeStruct(dims, kind)


def after(value, *others):
    return lax.optimization_barrier((value, *others))[0]


def gathered(shard):
    count = lax.axis_size("edata")
    shards = [shard]
    for step in range(1, count):
        pairs = [((i + step) % count, i) for i in range(count)]
        shards.append(lax.ppermute(shard, "edata", pairs))
    return shards


def from_owner(piece, step):
    count = lax.axis_size("edata")
    return lax.ppermute(piece, "edata", [(i, (i + step) % count) for i in range(count)])


def over_planes(rows):
    planes = lax.axis_size("local")
    shaped = rows.reshape(planes, -1, rows.shape[-1])
    out = lax.all_to_all(shaped, "local", split_axis=0, concat_axis=0, tiled=True)
    return out.reshape(rows.shape)


def to_nodes(pieces):
    count = len(pieces)
    return [pieces[0]] + [
        lax.ppermute(pieces[d], "node", [(i, i ^ d) for i in range(count)]) for d in range(1, count)
    ]


def shard_at(s, turn, count, width):
    return pl.ds(pl.multiple_of((turn + s) % count * width, width), width)


def dispatch_x(where, numbers, ids_t, gates_t, tokens, nodes, planes, capacity):
    top, tok_rows = ids_t.shape
    model = tokens.shape[1]
    count = lax.axis_size("edata")
    width = model // count
    groups = nodes * planes
    slots = groups * capacity

    def kernel(where_ref, numbers_ref, ids_ref, gates_ref, x_ref, sent_ref, pick_ref, weight_ref):
        turn = where_ref[0]
        numbers = jnp.broadcast_to(numbers_ref[...], (groups, tok_rows))
        routed = jnp.zeros((groups, tok_rows), F32)
        weight = jnp.zeros((groups, tok_rows), F32)
        for k in range(top):
            chosen = ids_ref[k : k + 1, :] == numbers
            routed = jnp.where(chosen, 1.0, routed)
            weight += jnp.where(chosen, gates_ref[k : k + 1, :], 0.0)
        first = lax.broadcasted_iota(jnp.int32, (tok_rows, tok_rows), 0)
        second = lax.broadcasted_iota(jnp.int32, (tok_rows, tok_rows), 1)
        earlier = jnp.where(first < second, 1.0, 0.0).astype(BF)
        order = jnp.dot(routed.astype(BF), earlier, preferred_element_type=F32)
        order = jnp.where(routed > 0.0, order, -1.0)
        places = lax.broadcasted_iota(jnp.int32, (capacity, tok_rows), 0).astype(F32)
        for g in range(groups):
            hits = order[g : g + 1, :] == places
            here = slice(g * capacity, (g + 1) * capacity)
            pick_ref[here] = jnp.where(hits, 1.0, 0.0).astype(BF)
            weight_ref[here] = jnp.sum(
                jnp.where(hits, weight[g : g + 1, :], 0.0), axis=1, keepdims=True
            )
        for s in range(count):
            source = shard_at(s, turn, count, width)
            x = jnp.dot(pick_ref[...], x_ref[:, source], preferred_element_type=F32).astype(BF)
            sent_ref[:, :, :, s * width : (s + 1) * width] = x.reshape(
                planes, nodes, capacity, width
            )

    return call(
        kernel,
        "dispatch_x",
        in_specs=[SMEM] + [VMEM] * 4,
        out_specs=[VMEM] * 3,
        out_shape=[
            shape(planes, nodes, capacity, model),
            shape(slots, tok_rows),
            shape(slots, 1, kind=F32),
        ],
    )(where, numbers, ids_t, gates_t, tokens)


def dispatch_dy(where, pick, weight, out_grad, nodes, planes, capacity):
    slots, tok_rows = pick.shape
    model = out_grad.shape[1]
    count = lax.axis_size("edata")
    width = model // count

    def kernel(where_ref, pick_ref, weight_ref, grad_ref, sent_ref, rows_ref):
        turn = where_ref[0]
        for s in range(count):
            source = shard_at(s, turn, count, width)
            here = slice(s * width, (s + 1) * width)
            rows = jnp.dot(pick_ref[...], grad_ref[:, source], preferred_element_type=F32)
            rows_ref[:, here] = rows.astype(BF)
            sent_ref[:, :, :, here] = (
                (weight_ref[...] * rows).astype(BF).reshape(planes, nodes, capacity, width)
            )

    return call(
        kernel,
        "dispatch_dy",
        in_specs=[SMEM] + [VMEM] * 3,
        out_specs=[VMEM] * 2,
        out_shape=[shape(planes, nodes, capacity, model), shape(slots, model)],
    )(where, pick, weight, out_grad)


def split(rows):
    return [rows[:, d] for d in range(rows.shape[1])]


def pack(pieces):
    count = len(pieces)
    planes, capacity, width = pieces[0].shape
    tile = min(1024, width)

    def kernel(*refs):
        for d in range(count):
            refs[-1][:, d] = refs[d][...]

    return call(
        kernel,
        "pack",
        grid=(width // tile,),
        in_specs=[pl.BlockSpec((planes, capacity, tile), lambda i: (0, 0, i))] * count,
        out_specs=pl.BlockSpec((planes, count, capacity, tile), lambda i: (0, 0, 0, i)),
        out_shape=shape(planes, count, capacity, width),
    )(*pieces)


def product(left, weights):
    width = weights[0].shape[0]
    total = None
    for s, shard in enumerate(weights):
        one = jnp.dot(
            left[:, s * width : (s + 1) * width], shard[...], preferred_element_type=F32
        )
        total = one if total is None else total + one
    return total


def expert_forward(pieces, w_ins, w_outs):
    planes, capacity, model = pieces[0].shape
    nodes, count = len(pieces), len(w_ins)
    width = model // count
    double, hidden = w_ins[0].shape[1], w_outs[0].shape[1]
    size = planes * capacity
    band = min(2, nodes)

    def kernel(*refs):
        got, refs = refs[:nodes], refs[nodes:]
        ins, outs, refs = refs[:count], refs[count : 2 * count], refs[2 * count :]
        y_refs, (act_ref, inner_ref) = refs[:nodes], refs[nodes:]
        for first in range(0, nodes, band):
            here = slice(first * size, (first + band) * size)
            x = jnp.concatenate(
                [got[first + i][...].reshape(size, model) for i in range(band)], axis=0
            )
            act_ref[here] = product(x, ins)
            act_gate = act_ref[here, :hidden]
            inner_ref[here] = (act_gate * jax.nn.sigmoid(act_gate) * act_ref[here, hidden:]).astype(
                BF
            )
            for s in range(count):
                y = lax.dot_general(
                    inner_ref[here], outs[s][...], COLS_IN, preferred_element_type=F32
                ).astype(BF)
                for i in range(band):
                    part = y[i * size : (i + 1) * size].reshape(planes, capacity, width)
                    y_refs[first + i][:, :, s * width : (s + 1) * width] = part

    operands = (*pieces, *w_ins, *w_outs)
    results = call(
        kernel,
        "expert_forward",
        in_specs=[VMEM] * len(operands),
        out_specs=[VMEM] * (nodes + 2),
        out_shape=[
            *[shape(planes, capacity, model)] * nodes,
            shape(nodes * size, double, kind=F32),
            shape(nodes * size, hidden),
        ],
    )(*operands)
    return list(results[:nodes]), *results[nodes:]


def expert_backward(pieces, act, w_ins, w_outs):
    planes, capacity, model = pieces[0].shape
    nodes, count = len(pieces), len(w_ins)
    width = model // count
    double, hidden = w_ins[0].shape[1], w_outs[0].shape[1]
    size = planes * capacity
    band = min(2, nodes)

    def kernel(*refs):
        got, act_ref, refs = refs[:nodes], refs[nodes], refs[nodes + 1 :]
        ins, outs, refs = refs[:count], refs[count : 2 * count], refs[2 * count :]
        dx_refs, act_grad_ref = refs[:nodes], refs[nodes]
        for first in range(0, nodes, band):
            here = slice(first * size, (first + band) * size)
            dy = jnp.concatenate(
                [got[first + i][...].reshape(size, model) for i in range(band)], axis=0
            )
            inner_grad = product(dy, outs)
            act_gate = act_ref[here, :hidden]
            act_up = act_ref[here, hidden:]
            sig = jax.nn.sigmoid(act_gate)
            act_grad_ref[here, :hidden] = (
                inner_grad * act_up * sig * (1.0 + act_gate * (1.0 - sig))
            ).astype(BF)
            act_grad_ref[here, hidden:] = (inner_grad * (act_gate * sig)).astype(BF)
            for s in range(count):
                dx = lax.dot_general(
                    act_grad_ref[here], ins[s][...], COLS_IN, preferred_element_type=F32
                ).astype(BF)
                for i in range(band):
                    part = dx[i * size : (i + 1) * size].reshape(planes, capacity, width)
                    dx_refs[first + i][:, :, s * width : (s + 1) * width] = part

    operands = (*pieces, act, *w_ins, *w_outs)
    results = call(
        kernel,
        "expert_backward",
        in_specs=[VMEM] * len(operands),
        out_specs=[VMEM] * (nodes + 1),
        out_shape=[
            *[shape(planes, capacity, model)] * nodes,
            shape(nodes * size, double),
        ],
    )(*operands)
    return list(results[:nodes]), results[nodes]


def weight_grads(shard, xs, dys, inner, act_grad):
    nodes = len(xs)
    planes, capacity, model = xs[0].shape
    rows = planes * capacity
    hidden, double = inner.shape[1], act_grad.shape[1]
    size = model // lax.axis_size("edata")
    tile = min(256, size)
    steps = size // tile

    def kernel(*refs):
        x_refs, dy_refs, (inner_ref, act_grad_ref, out_ref) = (
            refs[:nodes],
            refs[nodes : 2 * nodes],
            refs[2 * nodes :],
        )
        for lefts, right, columns in (
            (x_refs, act_grad_ref, slice(0, double)),
            (dy_refs, inner_ref, slice(double, None)),
        ):
            left = jnp.concatenate([r[...].reshape(rows, tile) for r in lefts], axis=0)
            out_ref[:, columns] = lax.dot_general(
                left, right[...], ROWS_IN, preferred_element_type=F32
            ).astype(BF)

    tall = pl.BlockSpec((planes, capacity, tile), lambda i: (0, 0, shard * steps + i))
    return call(
        kernel,
        "weight_grads",
        grid=(steps,),
        in_specs=[tall] * (2 * nodes)
        + [
            pl.BlockSpec(inner.shape, lambda i: (0, 0)),
            pl.BlockSpec(act_grad.shape, lambda i: (0, 0)),
        ],
        out_specs=pl.BlockSpec((tile, double + hidden), lambda i: (i, 0)),
        out_shape=shape(size, double + hidden),
    )(*xs, *dys, inner, act_grad)


def combine_y(where, numbers, picks, ids_t, grad_rows, rows):
    pick, high_t, middle_t = picks
    slots, tok_rows = pick.shape
    planes, nodes, capacity, model = rows.shape
    groups = planes * nodes
    count = lax.axis_size("edata")
    width = model // count

    def kernel(where_ref, number_ref, pick_ref, high_ref, middle_ref, ids_ref, grad_ref, *refs):
        y_ref, mixed_ref, gate_grad_ref = refs
        turn = where_ref[0]
        dots = jnp.zeros((slots, 1), F32)
        for s in range(count):
            here = slice(s * width, (s + 1) * width)
            y = y_ref[:, :, :, here].reshape(slots, width)
            mixed_ref[:, shard_at(s, turn, count, width)] = (
                jnp.dot(high_ref[...], y, preferred_element_type=F32)
                + jnp.dot(middle_ref[...], y, preferred_element_type=F32)
            ).astype(BF)
            dots += jnp.sum(
                y.astype(F32) * grad_ref[:, here].astype(F32), axis=1, keepdims=True
            )
        by_token = pick_ref[...].astype(F32) * dots
        by_token = jnp.sum(by_token.reshape(groups, capacity, tok_rows), axis=1)
        ids = ids_ref[...]
        total = jnp.zeros(ids.shape, F32)
        for g in range(groups):
            total += jnp.where(ids == number_ref[g], by_token[g : g + 1], 0.0)
        gate_grad_ref[...] = total

    return call(
        kernel,
        "combine_y",
        in_specs=[SMEM, SMEM] + [VMEM] * 6,
        out_specs=[VMEM] * 2,
        out_shape=[shape(tok_rows, model), shape(*ids_t.shape, kind=F32)],
    )(where, numbers, pick, high_t, middle_t, ids_t, grad_rows, rows)


def combine_dx(where, pick_t, rows):
    tok_rows, slots = pick_t.shape
    planes, nodes, capacity, model = rows.shape
    count = lax.axis_size("edata")
    tile = min(512, model // count)
    steps = model // tile

    def kernel(where_ref, pick_ref, rows_ref, out_ref):
        out_ref[...] = jnp.dot(
            pick_ref[...], rows_ref[...].reshape(slots, tile), preferred_element_type=F32
        ).astype(BF)

    return call(
        kernel,
        "combine_dx",
        grid_spec=pltpu.PrefetchScalarGridSpec(
            num_scalar_prefetch=1,
            grid=(steps,),
            in_specs=[
                pl.BlockSpec((tok_rows, slots), lambda i, t: (0, 0)),
                pl.BlockSpec((planes, nodes, capacity, tile), lambda i, t: (0, 0, 0, i)),
            ],
            out_specs=pl.BlockSpec(
                (tok_rows, tile), lambda i, t: (0, (i + t[0] * (steps // count)) % steps)
            ),
        ),
        out_shape=shape(tok_rows, model),
    )(where, pick_t, rows)


def shards(tokens, out_grad, expert_ids, gates, w_gate_up, w_down):
    nodes, planes = lax.axis_size("node"), lax.axis_size("local")
    groups = nodes * planes
    tok_rows = tokens.shape[0]
    capacity = tok_rows * expert_ids.shape[1] // (EXP_DEV * groups)
    where = lax.axis_index("edata").astype(jnp.int32).reshape(1)
    w_ins = gathered(w_gate_up[0])
    w_outs = gathered(w_down[0])
    node = lax.axis_index("node") ^ jnp.arange(nodes, dtype=jnp.int32)
    numbers = jnp.arange(planes, dtype=jnp.int32)[:, None] + planes * node[None, :]
    numbers = numbers.reshape(-1)
    ids_t = expert_ids.T
    x_sent, pick, weight = dispatch_x(
        where, numbers[:, None], ids_t, gates.T, tokens, nodes, planes, capacity
    )
    dy_sent, grad_rows = dispatch_dy(where, pick, weight, out_grad, nodes, planes, capacity)
    x_mid = over_planes(x_sent)
    dy_mid = over_planes(after(dy_sent, x_mid))
    xs = to_nodes(split(x_mid))
    xs[0] = after(xs[0], *w_ins[1:], *w_outs[1:])
    ys, act, inner = expert_forward(xs, w_ins, w_outs)
    y_packed = pack(to_nodes(ys))
    y_packed, dy_mid = lax.optimization_barrier((y_packed, dy_mid))
    y_rows = over_planes(y_packed)
    dys = to_nodes(split(dy_mid))
    dxs, act_grad = expert_backward(dys, act, w_ins, w_outs)
    dxs = to_nodes(dxs)
    parts = [weight_grads(s, xs, dys, inner, act_grad) for s in range(1, len(w_ins))]
    held = lax.optimization_barrier((*dxs, *parts))
    dx_packed, parts = pack(held[:nodes]), held[nodes:]
    dx_packed, y_rows = lax.optimization_barrier((dx_packed, y_rows))
    dx_rows = over_planes(dx_packed)

    act_grad = after(act_grad, dx_packed)
    parts = [from_owner(p, step) for step, p in enumerate(parts, 1)]
    parts.append(weight_grads(0, xs, dys, inner, act_grad))
    double = w_gate_up.shape[2]
    sums = [
        sum(p[:, columns].astype(F32) for p in parts)
        for columns in (slice(0, double), slice(double, None))
    ]
    spread = pick.astype(F32) * after(weight, y_packed)
    high = lax.reduce_precision(spread, 8, 7)
    middle = (spread - high).astype(BF)
    mixed, gate_grad = combine_y(
        where, numbers, (pick, high.astype(BF).T, middle.T), ids_t, grad_rows, y_rows
    )
    held = lax.optimization_barrier((dx_rows, *sums, mixed, gate_grad, pick.T))
    dx_rows, grad_in, grad_down, mixed, gate_grad, pick_t = held
    token_grad = combine_dx(where, pick_t, dx_rows)
    return (mixed, token_grad, gate_grad.T, grad_in[None], grad_down[None])


def solution(mesh):
    rows = P(("node", "local", "edata"), None)
    weights = P(("node", "local"), "edata", None)
    return jax.shard_map(
        shards,
        mesh=mesh,
        in_specs=(rows, rows, rows, rows, weights, weights),
        out_specs=(rows, rows, rows, weights, weights),
        check_vma=False,
    )
```

```python
import jax
import jax.numpy as jnp
from jax import lax
from jax.experimental import pallas as pl
from jax.experimental.pallas import tpu as pltpu
from jax.sharding import PartitionSpec as P

EXP_DEV = 4
BF = jnp.bfloat16
F32 = jnp.float32
ROWS_IN = (((0,), (0,)), ((), ()))
COLS_IN = (((1,), (1,)), ((), ()))
LIMIT = 56 * 1024 * 1024
def work(flops):
    return pl.CostEstimate(flops=flops, bytes_accessed=flops // 200, transcendentals=0)


CHEAP = pl.CostEstimate(flops=1, bytes_accessed=1, transcendentals=0)
VMEM = pl.BlockSpec(memory_space=pltpu.VMEM)
SMEM = pl.BlockSpec(memory_space=pltpu.SMEM)

def call(kernel, name, cost=CHEAP, **more):
    return pl.pallas_call(
        kernel,
        compiler_params=pltpu.CompilerParams(vmem_limit_bytes=LIMIT),
        cost_estimate=cost,
        name=name,
        **more,
    )


def shape(*dims, kind=BF):
    return jax.ShapeDtypeStruct(dims, kind)


def after(value, *others):
    return lax.optimization_barrier((value, *others))[0]


def gathered(shard):
    count = lax.axis_size("edata")
    shards = [shard]
    for step in range(1, count):
        pairs = [((i + step) % count, i) for i in range(count)]
        shards.append(lax.ppermute(shard, "edata", pairs))
    return shards


def from_owner(piece, step):
    count = lax.axis_size("edata")
    return lax.ppermute(piece, "edata", [(i, (i + step) % count) for i in range(count)])


def to_all(rows):
    return lax.all_to_all(rows, ("node", "local"), split_axis=0, concat_axis=0, tiled=True)


def to_partner(block, j):
    count = lax.axis_size("node") * lax.axis_size("local")
    return lax.ppermute(block, ("node", "local"), [(i, i ^ j) for i in range(count)])


def slots_of(j, me, capacity):
    return pl.ds(pl.multiple_of((me ^ j) * capacity, capacity), capacity)


def shard_at(s, turn, count, width):
    return pl.ds(pl.multiple_of((turn + s) % count * width, width), width)


def dispatch_x(where, ids_t, gates_t, tokens, groups, capacity):
    top, tok_rows = ids_t.shape
    model = tokens.shape[1]
    count = lax.axis_size("edata")
    width = model // count
    slots = groups * capacity

    def kernel(where_ref, ids_ref, gates_ref, x_ref, sent_ref, pick_ref, weight_ref):
        turn = where_ref[1]
        numbers = lax.broadcasted_iota(jnp.int32, (groups, tok_rows), 0)
        routed = jnp.zeros((groups, tok_rows), F32)
        weight = jnp.zeros((groups, tok_rows), F32)
        for k in range(top):
            chosen = ids_ref[k : k + 1, :] == numbers
            routed = jnp.where(chosen, 1.0, routed)
            weight += jnp.where(chosen, gates_ref[k : k + 1, :], 0.0)
        first = lax.broadcasted_iota(jnp.int32, (tok_rows, tok_rows), 0)
        second = lax.broadcasted_iota(jnp.int32, (tok_rows, tok_rows), 1)
        earlier = jnp.where(first < second, 1.0, 0.0).astype(BF)
        order = jnp.dot(routed.astype(BF), earlier, preferred_element_type=F32)
        order = jnp.where(routed > 0.0, order, -1.0)
        places = lax.broadcasted_iota(jnp.int32, (capacity, tok_rows), 0).astype(F32)
        for g in range(groups):
            hits = order[g : g + 1, :] == places
            here = slice(g * capacity, (g + 1) * capacity)
            pick_ref[here] = jnp.where(hits, 1.0, 0.0).astype(BF)
            weight_ref[here] = jnp.sum(
                jnp.where(hits, weight[g : g + 1, :], 0.0), axis=1, keepdims=True
            )
        for s in range(count):
            source = shard_at(s, turn, count, width)
            x = jnp.dot(pick_ref[...], x_ref[:, source], preferred_element_type=F32).astype(BF)
            sent_ref[:, :, s * width : (s + 1) * width] = x.reshape(groups, capacity, width)

    return call(
        kernel,
        "dispatch_x",
        in_specs=[SMEM] + [VMEM] * 3,
        out_specs=[VMEM] * 3,
        out_shape=[
            shape(groups, capacity, model),
            shape(slots, tok_rows),
            shape(slots, 1, kind=F32),
        ],
    )(where, ids_t, gates_t, tokens)


def dispatch_dy(where, pick, weight, out_grad, groups, capacity):
    slots, tok_rows = pick.shape
    model = out_grad.shape[1]
    count = lax.axis_size("edata")
    width = model // count

    def kernel(where_ref, pick_ref, weight_ref, grad_ref, *refs):
        blocks, (rows_ref, relative_ref, dy_ref) = refs[:groups], refs[groups:]
        me, turn = where_ref[0], where_ref[1]
        for s in range(count):
            source = shard_at(s, turn, count, width)
            here = slice(s * width, (s + 1) * width)
            rows = jnp.dot(pick_ref[...], grad_ref[:, source], preferred_element_type=F32)
            rows_ref[:, here] = rows.astype(BF)
            dy_ref[:, here] = (weight_ref[...] * rows).astype(BF)
        for j, block in enumerate(blocks):
            block[...] = dy_ref[slots_of(j, me, capacity), :]
            relative_ref[j * capacity : (j + 1) * capacity] = pick_ref[slots_of(j, me, capacity), :]

    results = call(
        kernel,
        "dispatch_dy",
        in_specs=[SMEM] + [VMEM] * 3,
        out_specs=[VMEM] * (groups + 2),
        out_shape=[
            *[shape(capacity, model)] * groups,
            shape(slots, model),
            shape(slots, tok_rows),
        ],
        scratch_shapes=[pltpu.VMEM((slots, model), BF)],
    )(where, pick, weight, out_grad)
    return list(results[:groups]), *results[groups:]


def product(left, weights):
    width = weights[0].shape[0]
    total = None
    for s, shard in enumerate(weights):
        one = jnp.dot(
            left[:, s * width : (s + 1) * width], shard[...], preferred_element_type=F32
        )
        total = one if total is None else total + one
    return total


def expert_forward(got, w_ins, w_outs):
    groups, capacity, model = got.shape
    count = len(w_ins)
    width = model // count
    double, hidden = w_ins[0].shape[1], w_outs[0].shape[1]
    slots = groups * capacity
    many = max(1, 256 // capacity)

    def kernel(got_ref, *refs):
        ins, outs, (y_ref, act_ref, inner_ref) = refs[:count], refs[count:-3], refs[-3:]
        for first in range(0, groups, many):
            theirs = slice(first, first + many)
            band = slice(first * capacity, (first + many) * capacity)
            x = got_ref[theirs].reshape(many * capacity, model)
            act_ref[band] = product(x, ins)
            act_gate = act_ref[band, :hidden]
            inner_ref[band] = (
                act_gate * jax.nn.sigmoid(act_gate) * act_ref[band, hidden:]
            ).astype(BF)
            for s in range(count):
                y = lax.dot_general(
                    inner_ref[band], outs[s][...], COLS_IN, preferred_element_type=F32
                ).astype(BF)
                y_ref[theirs, :, s * width : (s + 1) * width] = y.reshape(many, capacity, width)

    operands = (got, *w_ins, *w_outs)
    return call(
        kernel,
        "expert_forward",
        cost=work(6 * slots * model * hidden),
        in_specs=[VMEM] * len(operands),
        out_specs=[VMEM] * 3,
        out_shape=[
            shape(groups, capacity, model),
            shape(slots, double, kind=F32),
            shape(slots, hidden),
        ],
    )(*operands)


def expert_backward(where, blocks, act, w_ins, w_outs):
    groups = len(blocks)
    capacity, model = blocks[0].shape
    count = len(w_ins)
    width = model // count
    double, hidden = w_ins[0].shape[1], w_outs[0].shape[1]
    slots = groups * capacity
    rows = min(256, slots)

    def kernel(where_ref, *refs):
        got, act_ref, refs = refs[:groups], refs[groups], refs[groups + 1 :]
        ins, outs, refs = refs[:count], refs[count : 2 * count], refs[2 * count :]
        sent, (act_grad_ref, dy_ref, dx_ref) = refs[:groups], refs[groups:]
        me = where_ref[0]
        for j, block in enumerate(got):
            dy_ref[slots_of(j, me, capacity), :] = block[...]
        for first in range(0, slots, rows):
            band = slice(first, first + rows)
            inner_grad = product(dy_ref[band], outs)
            act_gate = act_ref[band, :hidden]
            act_up = act_ref[band, hidden:]
            sig = jax.nn.sigmoid(act_gate)
            act_grad_ref[band, :hidden] = (
                inner_grad * act_up * sig * (1.0 + act_gate * (1.0 - sig))
            ).astype(BF)
            act_grad_ref[band, hidden:] = (inner_grad * (act_gate * sig)).astype(BF)
            for s in range(count):
                dx_ref[band, s * width : (s + 1) * width] = lax.dot_general(
                    act_grad_ref[band], ins[s][...], COLS_IN, preferred_element_type=F32
                ).astype(BF)
        for j, block in enumerate(sent):
            block[...] = dx_ref[slots_of(j, me, capacity), :]

    operands = (where, *blocks, act, *w_ins, *w_outs)
    results = call(
        kernel,
        "expert_backward",
        cost=work(6 * slots * model * hidden),
        in_specs=[SMEM] + [VMEM] * (len(operands) - 1),
        out_specs=[VMEM] * (groups + 2),
        out_shape=[
            *[shape(capacity, model)] * groups,
            shape(slots, double),
            shape(slots, model),
        ],
        scratch_shapes=[pltpu.VMEM((slots, model), BF)],
    )(*operands)
    return list(results[:groups]), *results[groups:]


def weight_grads(shard, got, dys, inner, act_grad):
    groups, capacity, _ = got.shape
    slots, model = dys.shape
    size = model // lax.axis_size("edata")
    double, hidden = act_grad.shape[1], inner.shape[1]
    tile = min(256, size)
    steps = size // tile

    def kernel(x_ref, dy_ref, inner_ref, act_grad_ref, out_ref):
        x = x_ref[...].reshape(slots, tile)
        out_ref[:, :double] = lax.dot_general(
            x, act_grad_ref[...], ROWS_IN, preferred_element_type=F32
        ).astype(BF)
        out_ref[:, double:] = lax.dot_general(
            dy_ref[...], inner_ref[...], ROWS_IN, preferred_element_type=F32
        ).astype(BF)

    return call(
        kernel,
        "weight_grads",
        cost=work(6 * slots * size * hidden),
        grid=(steps,),
        in_specs=[
            pl.BlockSpec((groups, capacity, tile), lambda i: (0, 0, shard * steps + i)),
            pl.BlockSpec((slots, tile), lambda i: (0, shard * steps + i)),
            pl.BlockSpec((slots, hidden), lambda i: (0, 0)),
            pl.BlockSpec((slots, double), lambda i: (0, 0)),
        ],
        out_specs=pl.BlockSpec((tile, double + hidden), lambda i: (i, 0)),
        out_shape=shape(size, double + hidden),
    )(got, dys, inner, act_grad)


def combine_y(where, picks, ids_t, grad_rows, rows):
    pick, high_t, middle_t = picks
    slots, tok_rows = pick.shape
    groups, capacity, model = rows.shape
    count = lax.axis_size("edata")
    width = model // count

    def kernel(where_ref, pick_ref, high_ref, middle_ref, ids_ref, grad_ref, *refs):
        y_ref, mixed_ref, gate_grad_ref = refs
        turn = where_ref[1]
        dots = jnp.zeros((slots, 1), F32)
        for s in range(count):
            here = slice(s * width, (s + 1) * width)
            y = y_ref[:, :, here].reshape(slots, width)
            mixed_ref[:, shard_at(s, turn, count, width)] = (
                jnp.dot(high_ref[...], y, preferred_element_type=F32)
                + jnp.dot(middle_ref[...], y, preferred_element_type=F32)
            ).astype(BF)
            dots += jnp.sum(
                y.astype(F32) * grad_ref[:, here].astype(F32), axis=1, keepdims=True
            )
        by_token = pick_ref[...].astype(F32) * dots
        by_token = jnp.sum(by_token.reshape(groups, capacity, tok_rows), axis=1)
        ids = ids_ref[...]
        total = jnp.zeros(ids.shape, F32)
        for g in range(groups):
            total += jnp.where(ids == g, by_token[g : g + 1], 0.0)
        gate_grad_ref[...] = total

    return call(
        kernel,
        "combine_y",
        in_specs=[SMEM] + [VMEM] * 6,
        out_specs=[VMEM] * 2,
        out_shape=[shape(tok_rows, model), shape(*ids_t.shape, kind=F32)],
    )(where, pick, high_t, middle_t, ids_t, grad_rows, rows)


def combine_dx(where, relative_t, blocks):
    tok_rows, slots = relative_t.shape
    capacity, model = blocks[0].shape
    count = lax.axis_size("edata")
    width = model // count

    def kernel(where_ref, relative_ref, *refs):
        blocks, out_ref = refs[:-1], refs[-1]
        for s in range(count):
            here = slice(s * width, (s + 1) * width)
            dx = jnp.concatenate([block[:, here] for block in blocks], axis=0)
            out_ref[:, shard_at(s, where_ref[1], count, width)] = jnp.dot(
                relative_ref[...], dx, preferred_element_type=F32
            ).astype(BF)

    return call(
        kernel,
        "combine_dx",
        in_specs=[SMEM] + [VMEM] * (1 + len(blocks)),
        out_specs=VMEM,
        out_shape=shape(tok_rows, model),
    )(where, relative_t, *blocks)


def shards(tokens, out_grad, expert_ids, gates, w_gate_up, w_down):
    groups = lax.axis_size("node") * lax.axis_size("local")
    tok_rows = tokens.shape[0]
    capacity = tok_rows * expert_ids.shape[1] // (EXP_DEV * groups)
    queued = min(5, groups - 1)
    where = jnp.stack([lax.axis_index(("node", "local")), lax.axis_index("edata")])
    where = where.astype(jnp.int32)
    w_ins = gathered(w_gate_up[0])
    w_outs = gathered(w_down[0])
    ids_t = expert_ids.T
    sent, pick, weight = dispatch_x(where, ids_t, gates.T, tokens, groups, capacity)
    got = to_all(sent)
    blocks, grad_rows, relative = dispatch_dy(where, pick, weight, out_grad, groups, capacity)
    blocks = [blocks[0], *(after(b, *w_ins[1:], *w_outs[1:]) for b in blocks[1:])]
    y_sent, act, inner = expert_forward(got, w_ins, w_outs)
    dys = [blocks[0]]
    for j in range(1, groups):
        needs = (inner, dys[j - queued]) if j > queued else ()
        dys.append(to_partner(after(blocks[j], *needs) if needs else blocks[j], j))
    y_got = to_all(after(y_sent, *dys[1:]))
    dxs, act_grad, dy_rows = expert_backward(where, dys, act, w_ins, w_outs)
    backs = [dxs[0]]
    for j in range(1, groups):
        needs = (y_got, backs[j - queued]) if j > queued else ()
        backs.append(to_partner(after(dxs[j], *needs) if needs else dxs[j], j))

    parts = []
    for shard in [*range(1, len(w_ins)), 0]:
        parts.append(weight_grads(shard, got, dy_rows, inner, act_grad))
    parts = [parts[-1]] + [from_owner(after(p, y_got), step) for step, p in enumerate(parts[:-1], 1)]
    double = w_gate_up.shape[2]
    sums = [
        sum(p[:, columns].astype(F32) for p in parts)
        for columns in (slice(0, double), slice(double, None))
    ]
    spread = pick.astype(F32) * after(weight, inner)
    high = lax.reduce_precision(spread, 8, 7)
    middle = (spread - high).astype(BF)
    mixed, gate_grad = combine_y(
        where, (pick, high.astype(BF).T, middle.T), ids_t, grad_rows, y_got
    )
    held = lax.optimization_barrier((*backs, *sums, mixed, gate_grad, relative.T))
    *backs, grad_in, grad_down, mixed, gate_grad, relative_t = held
    token_grad = combine_dx(where, relative_t, backs)
    return (mixed, token_grad, gate_grad.T, grad_in[None], grad_down[None])


def solution(mesh):
    rows = P(("node", "local", "edata"), None)
    weights = P(("node", "local"), "edata", None)
    return jax.shard_map(
        shards,
        mesh=mesh,
        in_specs=(rows, rows, rows, rows, weights, weights),
        out_specs=(rows, rows, rows, weights, weights),
        check_vma=False,
    )
```

```python
import jax
import jax.numpy as jnp
from jax import lax
from jax.experimental import pallas as pl
from jax.experimental.pallas import tpu as pltpu
from jax.sharding import PartitionSpec as P

EXP_DEV = 4
BF = jnp.bfloat16
F32 = jnp.float32
ROWS_IN = (((0,), (0,)), ((), ()))
COLS_IN = (((1,), (1,)), ((), ()))
LIMIT = 56 * 1024 * 1024
def work(flops):
    return pl.CostEstimate(flops=flops, bytes_accessed=flops // 200, transcendentals=0)


CHEAP = pl.CostEstimate(flops=1, bytes_accessed=1, transcendentals=0)
VMEM = pl.BlockSpec(memory_space=pltpu.VMEM)
SMEM = pl.BlockSpec(memory_space=pltpu.SMEM)

def call(kernel, name, cost=CHEAP, **more):
    return pl.pallas_call(
        kernel,
        compiler_params=pltpu.CompilerParams(vmem_limit_bytes=LIMIT),
        cost_estimate=cost,
        name=name,
        **more,
    )


def shape(*dims, kind=BF):
    return jax.ShapeDtypeStruct(dims, kind)


def after(value, *others):
    return lax.optimization_barrier((value, *others))[0]


def gathered(shard):
    count = lax.axis_size("edata")
    shards = [shard]
    for step in range(1, count):
        pairs = [((i + step) % count, i) for i in range(count)]
        shards.append(lax.ppermute(shard, "edata", pairs))
    return shards


def from_owner(piece, step):
    count = lax.axis_size("edata")
    return lax.ppermute(piece, "edata", [(i, (i + step) % count) for i in range(count)])


def to_all(rows):
    return lax.all_to_all(rows, ("node", "local"), split_axis=0, concat_axis=0, tiled=True)


def to_partner(block, j):
    count = lax.axis_size("node") * lax.axis_size("local")
    return lax.ppermute(block, ("node", "local"), [(i, i ^ j) for i in range(count)])


def slots_of(j, me, capacity):
    return pl.ds(pl.multiple_of((me ^ j) * capacity, capacity), capacity)


def shard_at(s, turn, count, width):
    return pl.ds(pl.multiple_of((turn + s) % count * width, width), width)


def dispatch_x(where, ids_t, gates_t, tokens, groups, capacity):
    top, tok_rows = ids_t.shape
    model = tokens.shape[1]
    count = lax.axis_size("edata")
    width = model // count
    slots = groups * capacity

    def kernel(where_ref, ids_ref, gates_ref, x_ref, sent_ref, pick_ref, weight_ref):
        turn = where_ref[1]
        numbers = lax.broadcasted_iota(jnp.int32, (groups, tok_rows), 0)
        routed = jnp.zeros((groups, tok_rows), F32)
        weight = jnp.zeros((groups, tok_rows), F32)
        for k in range(top):
            chosen = ids_ref[k : k + 1, :] == numbers
            routed = jnp.where(chosen, 1.0, routed)
            weight += jnp.where(chosen, gates_ref[k : k + 1, :], 0.0)
        first = lax.broadcasted_iota(jnp.int32, (tok_rows, tok_rows), 0)
        second = lax.broadcasted_iota(jnp.int32, (tok_rows, tok_rows), 1)
        earlier = jnp.where(first < second, 1.0, 0.0).astype(BF)
        order = jnp.dot(routed.astype(BF), earlier, preferred_element_type=F32)
        order = jnp.where(routed > 0.0, order, -1.0)
        places = lax.broadcasted_iota(jnp.int32, (capacity, tok_rows), 0).astype(F32)
        for g in range(groups):
            hits = order[g : g + 1, :] == places
            here = slice(g * capacity, (g + 1) * capacity)
            pick_ref[here] = jnp.where(hits, 1.0, 0.0).astype(BF)
            weight_ref[here] = jnp.sum(
                jnp.where(hits, weight[g : g + 1, :], 0.0), axis=1, keepdims=True
            )
        for s in range(count):
            source = shard_at(s, turn, count, width)
            x = jnp.dot(pick_ref[...], x_ref[:, source], preferred_element_type=F32).astype(BF)
            sent_ref[:, :, s * width : (s + 1) * width] = x.reshape(groups, capacity, width)

    return call(
        kernel,
        "dispatch_x",
        in_specs=[SMEM] + [VMEM] * 3,
        out_specs=[VMEM] * 3,
        out_shape=[
            shape(groups, capacity, model),
            shape(slots, tok_rows),
            shape(slots, 1, kind=F32),
        ],
    )(where, ids_t, gates_t, tokens)


def dispatch_dy(where, pick, weight, out_grad, groups, capacity):
    slots, tok_rows = pick.shape
    model = out_grad.shape[1]
    count = lax.axis_size("edata")
    width = model // count

    def kernel(where_ref, pick_ref, weight_ref, grad_ref, *refs):
        blocks, (rows_ref, relative_ref, dy_ref) = refs[:groups], refs[groups:]
        me, turn = where_ref[0], where_ref[1]
        for s in range(count):
            source = shard_at(s, turn, count, width)
            here = slice(s * width, (s + 1) * width)
            rows = jnp.dot(pick_ref[...], grad_ref[:, source], preferred_element_type=F32)
            rows_ref[:, here] = rows.astype(BF)
            dy_ref[:, here] = (weight_ref[...] * rows).astype(BF)
        for j, block in enumerate(blocks):
            block[...] = dy_ref[slots_of(j, me, capacity), :]
            relative_ref[j * capacity : (j + 1) * capacity] = pick_ref[slots_of(j, me, capacity), :]

    results = call(
        kernel,
        "dispatch_dy",
        in_specs=[SMEM] + [VMEM] * 3,
        out_specs=[VMEM] * (groups + 2),
        out_shape=[
            *[shape(capacity, model)] * groups,
            shape(slots, model),
            shape(slots, tok_rows),
        ],
        scratch_shapes=[pltpu.VMEM((slots, model), BF)],
    )(where, pick, weight, out_grad)
    return list(results[:groups]), *results[groups:]


def product(left, weights):
    width = weights[0].shape[0]
    total = None
    for s, shard in enumerate(weights):
        one = jnp.dot(
            left[:, s * width : (s + 1) * width], shard[...], preferred_element_type=F32
        )
        total = one if total is None else total + one
    return total


def expert_forward(got, w_ins, w_outs):
    groups, capacity, model = got.shape
    count = len(w_ins)
    width = model // count
    double, hidden = w_ins[0].shape[1], w_outs[0].shape[1]
    slots = groups * capacity
    many = max(1, 256 // capacity)

    def kernel(got_ref, *refs):
        ins, outs, (y_ref, act_ref, inner_ref) = refs[:count], refs[count:-3], refs[-3:]
        for first in range(0, groups, many):
            theirs = slice(first, first + many)
            band = slice(first * capacity, (first + many) * capacity)
            x = got_ref[theirs].reshape(many * capacity, model)
            act_ref[band] = product(x, ins)
            act_gate = act_ref[band, :hidden]
            inner_ref[band] = (
                act_gate * jax.nn.sigmoid(act_gate) * act_ref[band, hidden:]
            ).astype(BF)
            for s in range(count):
                y = lax.dot_general(
                    inner_ref[band], outs[s][...], COLS_IN, preferred_element_type=F32
                ).astype(BF)
                y_ref[theirs, :, s * width : (s + 1) * width] = y.reshape(many, capacity, width)

    operands = (got, *w_ins, *w_outs)
    return call(
        kernel,
        "expert_forward",
        cost=work(6 * slots * model * hidden),
        in_specs=[VMEM] * len(operands),
        out_specs=[VMEM] * 3,
        out_shape=[
            shape(groups, capacity, model),
            shape(slots, double, kind=F32),
            shape(slots, hidden),
        ],
    )(*operands)


def expert_backward(where, blocks, act, w_ins, w_outs):
    groups = len(blocks)
    capacity, model = blocks[0].shape
    count = len(w_ins)
    width = model // count
    double, hidden = w_ins[0].shape[1], w_outs[0].shape[1]
    slots = groups * capacity
    rows = min(256, slots)

    def kernel(where_ref, *refs):
        got, act_ref, refs = refs[:groups], refs[groups], refs[groups + 1 :]
        ins, outs, refs = refs[:count], refs[count : 2 * count], refs[2 * count :]
        sent, (act_grad_ref, dy_ref, dx_ref) = refs[:groups], refs[groups:]
        me = where_ref[0]
        for j, block in enumerate(got):
            dy_ref[slots_of(j, me, capacity), :] = block[...]
        for first in range(0, slots, rows):
            band = slice(first, first + rows)
            inner_grad = product(dy_ref[band], outs)
            act_gate = act_ref[band, :hidden]
            act_up = act_ref[band, hidden:]
            sig = jax.nn.sigmoid(act_gate)
            act_grad_ref[band, :hidden] = (
                inner_grad * act_up * sig * (1.0 + act_gate * (1.0 - sig))
            ).astype(BF)
            act_grad_ref[band, hidden:] = (inner_grad * (act_gate * sig)).astype(BF)
            for s in range(count):
                dx_ref[band, s * width : (s + 1) * width] = lax.dot_general(
                    act_grad_ref[band], ins[s][...], COLS_IN, preferred_element_type=F32
                ).astype(BF)
        for j, block in enumerate(sent):
            block[...] = dx_ref[slots_of(j, me, capacity), :]

    operands = (where, *blocks, act, *w_ins, *w_outs)
    results = call(
        kernel,
        "expert_backward",
        cost=work(6 * slots * model * hidden),
        in_specs=[SMEM] + [VMEM] * (len(operands) - 1),
        out_specs=[VMEM] * (groups + 2),
        out_shape=[
            *[shape(capacity, model)] * groups,
            shape(slots, double),
            shape(slots, model),
        ],
        scratch_shapes=[pltpu.VMEM((slots, model), BF)],
    )(*operands)
    return list(results[:groups]), *results[groups:]


def weight_grads(shard, got, dys, inner, act_grad):
    groups, capacity, _ = got.shape
    slots, model = dys.shape
    size = model // lax.axis_size("edata")
    double, hidden = act_grad.shape[1], inner.shape[1]
    tile = min(256, size)
    steps = size // tile

    def kernel(x_ref, dy_ref, inner_ref, act_grad_ref, out_ref):
        x = x_ref[...].reshape(slots, tile)
        out_ref[:, :double] = lax.dot_general(
            x, act_grad_ref[...], ROWS_IN, preferred_element_type=F32
        ).astype(BF)
        out_ref[:, double:] = lax.dot_general(
            dy_ref[...], inner_ref[...], ROWS_IN, preferred_element_type=F32
        ).astype(BF)

    return call(
        kernel,
        "weight_grads",
        cost=work(6 * slots * size * hidden),
        grid=(steps,),
        in_specs=[
            pl.BlockSpec((groups, capacity, tile), lambda i: (0, 0, shard * steps + i)),
            pl.BlockSpec((slots, tile), lambda i: (0, shard * steps + i)),
            pl.BlockSpec((slots, hidden), lambda i: (0, 0)),
            pl.BlockSpec((slots, double), lambda i: (0, 0)),
        ],
        out_specs=pl.BlockSpec((tile, double + hidden), lambda i: (i, 0)),
        out_shape=shape(size, double + hidden),
    )(got, dys, inner, act_grad)


def combine_y(where, picks, ids_t, grad_rows, rows):
    pick, high_t, middle_t = picks
    slots, tok_rows = pick.shape
    groups, capacity, model = rows.shape
    count = lax.axis_size("edata")
    width = model // count

    def kernel(where_ref, pick_ref, high_ref, middle_ref, ids_ref, grad_ref, *refs):
        y_ref, mixed_ref, gate_grad_ref = refs
        turn = where_ref[1]
        dots = jnp.zeros((slots, 1), F32)
        for s in range(count):
            here = slice(s * width, (s + 1) * width)
            y = y_ref[:, :, here].reshape(slots, width)
            mixed_ref[:, shard_at(s, turn, count, width)] = (
                jnp.dot(high_ref[...], y, preferred_element_type=F32)
                + jnp.dot(middle_ref[...], y, preferred_element_type=F32)
            ).astype(BF)
            dots += jnp.sum(
                y.astype(F32) * grad_ref[:, here].astype(F32), axis=1, keepdims=True
            )
        by_token = pick_ref[...].astype(F32) * dots
        by_token = jnp.sum(by_token.reshape(groups, capacity, tok_rows), axis=1)
        ids = ids_ref[...]
        total = jnp.zeros(ids.shape, F32)
        for g in range(groups):
            total += jnp.where(ids == g, by_token[g : g + 1], 0.0)
        gate_grad_ref[...] = total

    return call(
        kernel,
        "combine_y",
        in_specs=[SMEM] + [VMEM] * 6,
        out_specs=[VMEM] * 2,
        out_shape=[shape(tok_rows, model), shape(*ids_t.shape, kind=F32)],
    )(where, pick, high_t, middle_t, ids_t, grad_rows, rows)


def combine_dx(where, relative_t, blocks):
    tok_rows, slots = relative_t.shape
    capacity, model = blocks[0].shape
    count = lax.axis_size("edata")
    width = model // count

    def kernel(where_ref, relative_ref, *refs):
        blocks, out_ref = refs[:-1], refs[-1]
        for s in range(count):
            here = slice(s * width, (s + 1) * width)
            dx = jnp.concatenate([block[:, here] for block in blocks], axis=0)
            out_ref[:, shard_at(s, where_ref[1], count, width)] = jnp.dot(
                relative_ref[...], dx, preferred_element_type=F32
            ).astype(BF)

    return call(
        kernel,
        "combine_dx",
        in_specs=[SMEM] + [VMEM] * (1 + len(blocks)),
        out_specs=VMEM,
        out_shape=shape(tok_rows, model),
    )(where, relative_t, *blocks)


def shards(tokens, out_grad, expert_ids, gates, w_gate_up, w_down):
    groups = lax.axis_size("node") * lax.axis_size("local")
    tok_rows = tokens.shape[0]
    capacity = tok_rows * expert_ids.shape[1] // (EXP_DEV * groups)
    queued = min(5, groups - 1)
    where = jnp.stack([lax.axis_index(("node", "local")), lax.axis_index("edata")])
    where = where.astype(jnp.int32)
    w_ins = gathered(w_gate_up[0])
    w_outs = gathered(w_down[0])
    ids_t = expert_ids.T
    sent, pick, weight = dispatch_x(where, ids_t, gates.T, tokens, groups, capacity)
    got = to_all(sent)
    blocks, grad_rows, relative = dispatch_dy(where, pick, weight, out_grad, groups, capacity)
    blocks = [blocks[0], *(after(b, *w_ins[1:], *w_outs[1:]) for b in blocks[1:])]
    dys = [blocks[0]]
    for j in range(1, groups):
        needs = (dys[j - queued],) if j > queued else ()
        if j == 2 * queued + 1:
            y_sent, act, inner = expert_forward(after(got, *dys[1 : queued + 1]), w_ins, w_outs)
        if j > 2 * queued:
            needs += (inner,)
        dys.append(to_partner(after(blocks[j], *needs) if needs else blocks[j], j))
    y_got = to_all(after(y_sent, *dys[1:]))
    dxs, act_grad, dy_rows = expert_backward(where, dys, act, w_ins, w_outs)
    backs = [dxs[0]]
    for j in range(1, groups):
        needs = (y_got, backs[j - queued]) if j > queued else ()
        backs.append(to_partner(after(dxs[j], *needs) if needs else dxs[j], j))

    parts = []
    for shard in [*range(1, len(w_ins)), 0]:
        parts.append(weight_grads(shard, got, dy_rows, inner, act_grad))
    *parts, y_got = lax.optimization_barrier((*parts, y_got))
    parts = [parts[-1]] + [from_owner(p, step) for step, p in enumerate(parts[:-1], 1)]
    double = w_gate_up.shape[2]
    sums = [
        sum(p[:, columns].astype(F32) for p in parts)
        for columns in (slice(0, double), slice(double, None))
    ]
    spread = pick.astype(F32) * after(weight, inner)
    high = lax.reduce_precision(spread, 8, 7)
    middle = (spread - high).astype(BF)
    mixed, gate_grad = combine_y(
        where, (pick, high.astype(BF).T, middle.T), ids_t, grad_rows, y_got
    )
    held = lax.optimization_barrier((*backs, *sums, mixed, gate_grad, relative.T))
    *backs, grad_in, grad_down, mixed, gate_grad, relative_t = held
    token_grad = combine_dx(where, relative_t, backs)
    return (mixed, token_grad, gate_grad.T, grad_in[None], grad_down[None])


def solution(mesh):
    rows = P(("node", "local", "edata"), None)
    weights = P(("node", "local"), "edata", None)
    return jax.shard_map(
        shards,
        mesh=mesh,
        in_specs=(rows, rows, rows, rows, weights, weights),
        out_specs=(rows, rows, rows, weights, weights),
        check_vma=False,
    )
```

```python
import jax
import jax.numpy as jnp
from jax import lax
from jax.experimental import pallas as pl
from jax.experimental.pallas import tpu as pltpu
from jax.sharding import PartitionSpec as P

EXP_DEV = 4
BF = jnp.bfloat16
F32 = jnp.float32
ROWS_IN = (((0,), (0,)), ((), ()))
COLS_IN = (((1,), (1,)), ((), ()))
LIMIT = 56 * 1024 * 1024
def work(flops):
    return pl.CostEstimate(flops=flops, bytes_accessed=flops // 200, transcendentals=0)


CHEAP = pl.CostEstimate(flops=1, bytes_accessed=1, transcendentals=0)
VMEM = pl.BlockSpec(memory_space=pltpu.VMEM)
SMEM = pl.BlockSpec(memory_space=pltpu.SMEM)

def call(kernel, name, cost=CHEAP, **more):
    return pl.pallas_call(
        kernel,
        compiler_params=pltpu.CompilerParams(vmem_limit_bytes=LIMIT),
        cost_estimate=cost,
        name=name,
        **more,
    )


def shape(*dims, kind=BF):
    return jax.ShapeDtypeStruct(dims, kind)


def after(value, *others):
    return lax.optimization_barrier((value, *others))[0]


def gathered(shard):
    count = lax.axis_size("edata")
    shards = [shard]
    for step in range(1, count):
        pairs = [((i + step) % count, i) for i in range(count)]
        shards.append(lax.ppermute(shard, "edata", pairs))
    return shards


def from_owner(piece, step):
    count = lax.axis_size("edata")
    return lax.ppermute(piece, "edata", [(i, (i + step) % count) for i in range(count)])


def to_all(rows):
    return lax.all_to_all(rows, ("node", "local"), split_axis=0, concat_axis=0, tiled=True)


def to_partner(block, j):
    count = lax.axis_size("node") * lax.axis_size("local")
    return lax.ppermute(block, ("node", "local"), [(i, i ^ j) for i in range(count)])


def slots_of(j, me, capacity):
    return pl.ds(pl.multiple_of((me ^ j) * capacity, capacity), capacity)


def shard_at(s, turn, count, width):
    return pl.ds(pl.multiple_of((turn + s) % count * width, width), width)


def dispatch_x(where, ids_t, gates_t, tokens, groups, capacity):
    top, tok_rows = ids_t.shape
    model = tokens.shape[1]
    count = lax.axis_size("edata")
    width = model // count
    slots = groups * capacity

    def kernel(where_ref, ids_ref, gates_ref, x_ref, sent_ref, pick_ref, weight_ref):
        turn = where_ref[1]
        numbers = lax.broadcasted_iota(jnp.int32, (groups, tok_rows), 0)
        routed = jnp.zeros((groups, tok_rows), F32)
        weight = jnp.zeros((groups, tok_rows), F32)
        for k in range(top):
            chosen = ids_ref[k : k + 1, :] == numbers
            routed = jnp.where(chosen, 1.0, routed)
            weight += jnp.where(chosen, gates_ref[k : k + 1, :], 0.0)
        first = lax.broadcasted_iota(jnp.int32, (tok_rows, tok_rows), 0)
        second = lax.broadcasted_iota(jnp.int32, (tok_rows, tok_rows), 1)
        earlier = jnp.where(first < second, 1.0, 0.0).astype(BF)
        order = jnp.dot(routed.astype(BF), earlier, preferred_element_type=F32)
        order = jnp.where(routed > 0.0, order, -1.0)
        places = lax.broadcasted_iota(jnp.int32, (capacity, tok_rows), 0).astype(F32)
        for g in range(groups):
            hits = order[g : g + 1, :] == places
            here = slice(g * capacity, (g + 1) * capacity)
            pick_ref[here] = jnp.where(hits, 1.0, 0.0).astype(BF)
            weight_ref[here] = jnp.sum(
                jnp.where(hits, weight[g : g + 1, :], 0.0), axis=1, keepdims=True
            )
        for s in range(count):
            source = shard_at(s, turn, count, width)
            x = jnp.dot(pick_ref[...], x_ref[:, source], preferred_element_type=F32).astype(BF)
            sent_ref[:, :, s * width : (s + 1) * width] = x.reshape(groups, capacity, width)

    return call(
        kernel,
        "dispatch_x",
        in_specs=[SMEM] + [VMEM] * 3,
        out_specs=[VMEM] * 3,
        out_shape=[
            shape(groups, capacity, model),
            shape(slots, tok_rows),
            shape(slots, 1, kind=F32),
        ],
    )(where, ids_t, gates_t, tokens)


def dispatch_dy(where, pick, weight, out_grad, groups, capacity):
    slots, tok_rows = pick.shape
    model = out_grad.shape[1]
    count = lax.axis_size("edata")
    width = model // count

    def kernel(where_ref, pick_ref, weight_ref, grad_ref, *refs):
        blocks, (rows_ref, relative_ref, dy_ref) = refs[:groups], refs[groups:]
        me, turn = where_ref[0], where_ref[1]
        for s in range(count):
            source = shard_at(s, turn, count, width)
            here = slice(s * width, (s + 1) * width)
            rows = jnp.dot(pick_ref[...], grad_ref[:, source], preferred_element_type=F32)
            rows_ref[:, here] = rows.astype(BF)
            dy_ref[:, here] = (weight_ref[...] * rows).astype(BF)
        for j, block in enumerate(blocks):
            block[...] = dy_ref[slots_of(j, me, capacity), :]
            relative_ref[j * capacity : (j + 1) * capacity] = pick_ref[slots_of(j, me, capacity), :]

    results = call(
        kernel,
        "dispatch_dy",
        in_specs=[SMEM] + [VMEM] * 3,
        out_specs=[VMEM] * (groups + 2),
        out_shape=[
            *[shape(capacity, model)] * groups,
            shape(slots, model),
            shape(slots, tok_rows),
        ],
        scratch_shapes=[pltpu.VMEM((slots, model), BF)],
    )(where, pick, weight, out_grad)
    return list(results[:groups]), *results[groups:]


def product(left, weights):
    width = weights[0].shape[0]
    total = None
    for s, shard in enumerate(weights):
        one = jnp.dot(
            left[:, s * width : (s + 1) * width], shard[...], preferred_element_type=F32
        )
        total = one if total is None else total + one
    return total


def expert_forward(got, w_ins, w_outs):
    groups, capacity, model = got.shape
    count = len(w_ins)
    width = model // count
    double, hidden = w_ins[0].shape[1], w_outs[0].shape[1]
    slots = groups * capacity
    many = max(1, 256 // capacity)

    def kernel(got_ref, *refs):
        ins, outs, (y_ref, act_ref, inner_ref) = refs[:count], refs[count:-3], refs[-3:]
        for first in range(0, groups, many):
            theirs = slice(first, first + many)
            band = slice(first * capacity, (first + many) * capacity)
            x = got_ref[theirs].reshape(many * capacity, model)
            act_ref[band] = product(x, ins)
            act_gate = act_ref[band, :hidden]
            inner_ref[band] = (
                act_gate * jax.nn.sigmoid(act_gate) * act_ref[band, hidden:]
            ).astype(BF)
            for s in range(count):
                y = lax.dot_general(
                    inner_ref[band], outs[s][...], COLS_IN, preferred_element_type=F32
                ).astype(BF)
                y_ref[theirs, :, s * width : (s + 1) * width] = y.reshape(many, capacity, width)

    operands = (got, *w_ins, *w_outs)
    return call(
        kernel,
        "expert_forward",
        cost=work(6 * slots * model * hidden),
        in_specs=[VMEM] * len(operands),
        out_specs=[VMEM] * 3,
        out_shape=[
            shape(groups, capacity, model),
            shape(slots, double, kind=F32),
            shape(slots, hidden),
        ],
    )(*operands)


def expert_backward(where, blocks, act, w_ins, w_outs):
    groups = len(blocks)
    capacity, model = blocks[0].shape
    count = len(w_ins)
    width = model // count
    double, hidden = w_ins[0].shape[1], w_outs[0].shape[1]
    slots = groups * capacity
    rows = min(256, slots)

    def kernel(where_ref, *refs):
        got, act_ref, refs = refs[:groups], refs[groups], refs[groups + 1 :]
        ins, outs, refs = refs[:count], refs[count : 2 * count], refs[2 * count :]
        sent, (act_grad_ref, dy_ref, dx_ref) = refs[:groups], refs[groups:]
        me = where_ref[0]
        for j, block in enumerate(got):
            dy_ref[slots_of(j, me, capacity), :] = block[...]
        for first in range(0, slots, rows):
            band = slice(first, first + rows)
            inner_grad = product(dy_ref[band], outs)
            act_gate = act_ref[band, :hidden]
            act_up = act_ref[band, hidden:]
            sig = jax.nn.sigmoid(act_gate)
            act_grad_ref[band, :hidden] = (
                inner_grad * act_up * sig * (1.0 + act_gate * (1.0 - sig))
            ).astype(BF)
            act_grad_ref[band, hidden:] = (inner_grad * (act_gate * sig)).astype(BF)
            for s in range(count):
                dx_ref[band, s * width : (s + 1) * width] = lax.dot_general(
                    act_grad_ref[band], ins[s][...], COLS_IN, preferred_element_type=F32
                ).astype(BF)
        for j, block in enumerate(sent):
            block[...] = dx_ref[slots_of(j, me, capacity), :]

    operands = (where, *blocks, act, *w_ins, *w_outs)
    results = call(
        kernel,
        "expert_backward",
        cost=work(6 * slots * model * hidden),
        in_specs=[SMEM] + [VMEM] * (len(operands) - 1),
        out_specs=[VMEM] * (groups + 2),
        out_shape=[
            *[shape(capacity, model)] * groups,
            shape(slots, double),
            shape(slots, model),
        ],
        scratch_shapes=[pltpu.VMEM((slots, model), BF)],
    )(*operands)
    return list(results[:groups]), *results[groups:]


def weight_grads(shard, got, dys, inner, act_grad):
    groups, capacity, _ = got.shape
    slots, model = dys.shape
    size = model // lax.axis_size("edata")
    double, hidden = act_grad.shape[1], inner.shape[1]
    tile = min(256, size)
    steps = size // tile

    def kernel(x_ref, dy_ref, inner_ref, act_grad_ref, out_ref):
        x = x_ref[...].reshape(slots, tile)
        out_ref[:, :double] = lax.dot_general(
            x, act_grad_ref[...], ROWS_IN, preferred_element_type=F32
        ).astype(BF)
        out_ref[:, double:] = lax.dot_general(
            dy_ref[...], inner_ref[...], ROWS_IN, preferred_element_type=F32
        ).astype(BF)

    return call(
        kernel,
        "weight_grads",
        cost=work(6 * slots * size * hidden),
        grid=(steps,),
        in_specs=[
            pl.BlockSpec((groups, capacity, tile), lambda i: (0, 0, shard * steps + i)),
            pl.BlockSpec((slots, tile), lambda i: (0, shard * steps + i)),
            pl.BlockSpec((slots, hidden), lambda i: (0, 0)),
            pl.BlockSpec((slots, double), lambda i: (0, 0)),
        ],
        out_specs=pl.BlockSpec((tile, double + hidden), lambda i: (i, 0)),
        out_shape=shape(size, double + hidden),
    )(got, dys, inner, act_grad)


def combine_y(where, picks, ids_t, grad_rows, rows):
    pick, high_t, middle_t = picks
    slots, tok_rows = pick.shape
    groups, capacity, model = rows.shape
    count = lax.axis_size("edata")
    width = model // count

    def kernel(where_ref, pick_ref, high_ref, middle_ref, ids_ref, grad_ref, *refs):
        y_ref, mixed_ref, gate_grad_ref = refs
        turn = where_ref[1]
        dots = jnp.zeros((slots, 1), F32)
        for s in range(count):
            here = slice(s * width, (s + 1) * width)
            y = y_ref[:, :, here].reshape(slots, width)
            mixed_ref[:, shard_at(s, turn, count, width)] = (
                jnp.dot(high_ref[...], y, preferred_element_type=F32)
                + jnp.dot(middle_ref[...], y, preferred_element_type=F32)
            ).astype(BF)
            dots += jnp.sum(
                y.astype(F32) * grad_ref[:, here].astype(F32), axis=1, keepdims=True
            )
        by_token = pick_ref[...].astype(F32) * dots
        by_token = jnp.sum(by_token.reshape(groups, capacity, tok_rows), axis=1)
        ids = ids_ref[...]
        total = jnp.zeros(ids.shape, F32)
        for g in range(groups):
            total += jnp.where(ids == g, by_token[g : g + 1], 0.0)
        gate_grad_ref[...] = total

    return call(
        kernel,
        "combine_y",
        in_specs=[SMEM] + [VMEM] * 6,
        out_specs=[VMEM] * 2,
        out_shape=[shape(tok_rows, model), shape(*ids_t.shape, kind=F32)],
    )(where, pick, high_t, middle_t, ids_t, grad_rows, rows)


def combine_dx(where, relative_t, blocks):
    tok_rows, slots = relative_t.shape
    capacity, model = blocks[0].shape
    count = lax.axis_size("edata")
    width = model // count

    def kernel(where_ref, relative_ref, *refs):
        blocks, out_ref = refs[:-1], refs[-1]
        for s in range(count):
            here = slice(s * width, (s + 1) * width)
            dx = jnp.concatenate([block[:, here] for block in blocks], axis=0)
            out_ref[:, shard_at(s, where_ref[1], count, width)] = jnp.dot(
                relative_ref[...], dx, preferred_element_type=F32
            ).astype(BF)

    return call(
        kernel,
        "combine_dx",
        in_specs=[SMEM] + [VMEM] * (1 + len(blocks)),
        out_specs=VMEM,
        out_shape=shape(tok_rows, model),
    )(where, relative_t, *blocks)


def shards(tokens, out_grad, expert_ids, gates, w_gate_up, w_down):
    groups = lax.axis_size("node") * lax.axis_size("local")
    tok_rows = tokens.shape[0]
    capacity = tok_rows * expert_ids.shape[1] // (EXP_DEV * groups)
    queued = min(5, groups - 1)
    where = jnp.stack([lax.axis_index(("node", "local")), lax.axis_index("edata")])
    where = where.astype(jnp.int32)
    w_ins = gathered(w_gate_up[0])
    w_outs = gathered(w_down[0])
    ids_t = expert_ids.T
    sent, pick, weight = dispatch_x(where, ids_t, gates.T, tokens, groups, capacity)
    got = to_all(sent)
    blocks, grad_rows, relative = dispatch_dy(where, pick, weight, out_grad, groups, capacity)
    blocks = [blocks[0], *(after(b, *w_ins[1:], *w_outs[1:]) for b in blocks[1:])]
    dys = [blocks[0]]
    for j in range(1, groups):
        needs = (dys[j - queued],) if j > queued else ()
        if j == 2 * queued + 1:
            y_sent, act, inner = expert_forward(after(got, *dys[1 : queued + 1]), w_ins, w_outs)
        if j > 2 * queued:
            needs += (inner,)
        dys.append(to_partner(after(blocks[j], *needs) if needs else blocks[j], j))
    y_got = to_all(after(y_sent, *dys[1:]))
    dxs, act_grad, dy_rows = expert_backward(where, dys, act, w_ins, w_outs)
    backs = [dxs[0]]
    for j in range(1, groups):
        needs = (backs[j - queued],) if j > queued else ()
        backs.append(to_partner(after(dxs[j], *needs) if needs else dxs[j], j))
    y_got = after(y_got, *backs[1 : queued + 1])

    parts = []
    for shard in [*range(1, len(w_ins)), 0]:
        parts.append(weight_grads(shard, got, dy_rows, inner, act_grad))
    *parts, y_got = lax.optimization_barrier((*parts, y_got))
    parts = [parts[-1]] + [from_owner(p, step) for step, p in enumerate(parts[:-1], 1)]
    double = w_gate_up.shape[2]
    sums = [
        sum(p[:, columns].astype(F32) for p in parts)
        for columns in (slice(0, double), slice(double, None))
    ]
    spread = pick.astype(F32) * after(weight, inner)
    high = lax.reduce_precision(spread, 8, 7)
    middle = (spread - high).astype(BF)
    mixed, gate_grad = combine_y(
        where, (pick, high.astype(BF).T, middle.T), ids_t, grad_rows, y_got
    )
    held = lax.optimization_barrier((*backs, *sums, mixed, gate_grad, relative.T))
    *backs, grad_in, grad_down, mixed, gate_grad, relative_t = held
    token_grad = combine_dx(where, relative_t, backs)
    return (mixed, token_grad, gate_grad.T, grad_in[None], grad_down[None])


def solution(mesh):
    rows = P(("node", "local", "edata"), None)
    weights = P(("node", "local"), "edata", None)
    return jax.shard_map(
        shards,
        mesh=mesh,
        in_specs=(rows, rows, rows, rows, weights, weights),
        out_specs=(rows, rows, rows, weights, weights),
        check_vma=False,
    )
```

```python
import jax
import jax.numpy as jnp
from jax import lax
from jax.experimental import pallas as pl
from jax.experimental.pallas import tpu as pltpu
from jax.sharding import PartitionSpec as P

EXP_DEV = 4
BF = jnp.bfloat16
F32 = jnp.float32
ROWS_IN = (((0,), (0,)), ((), ()))
COLS_IN = (((1,), (1,)), ((), ()))
LIMIT = 56 * 1024 * 1024
def work(flops):
    return pl.CostEstimate(flops=flops, bytes_accessed=flops // 200, transcendentals=0)


CHEAP = pl.CostEstimate(flops=1, bytes_accessed=1, transcendentals=0)
VMEM = pl.BlockSpec(memory_space=pltpu.VMEM)
SMEM = pl.BlockSpec(memory_space=pltpu.SMEM)

def call(kernel, name, cost=CHEAP, **more):
    return pl.pallas_call(
        kernel,
        compiler_params=pltpu.CompilerParams(vmem_limit_bytes=LIMIT),
        cost_estimate=cost,
        name=name,
        **more,
    )


def shape(*dims, kind=BF):
    return jax.ShapeDtypeStruct(dims, kind)


def after(value, *others):
    return lax.optimization_barrier((value, *others))[0]


def gathered(shard):
    count = lax.axis_size("edata")
    shards = [shard]
    for step in range(1, count):
        pairs = [((i + step) % count, i) for i in range(count)]
        shards.append(lax.ppermute(shard, "edata", pairs))
    return shards


def from_owner(piece, step):
    count = lax.axis_size("edata")
    return lax.ppermute(piece, "edata", [(i, (i + step) % count) for i in range(count)])


def to_all(rows):
    return lax.all_to_all(rows, ("node", "local"), split_axis=0, concat_axis=0, tiled=True)


def to_partner(block, j):
    count = lax.axis_size("node") * lax.axis_size("local")
    return lax.ppermute(block, ("node", "local"), [(i, i ^ j) for i in range(count)])


def slots_of(j, me, capacity):
    return pl.ds(pl.multiple_of((me ^ j) * capacity, capacity), capacity)


def shard_at(s, turn, count, width):
    return pl.ds(pl.multiple_of((turn + s) % count * width, width), width)


def dispatch_x(where, ids_t, gates_t, tokens, groups, capacity):
    top, tok_rows = ids_t.shape
    model = tokens.shape[1]
    count = lax.axis_size("edata")
    width = model // count
    slots = groups * capacity

    def kernel(where_ref, ids_ref, gates_ref, x_ref, sent_ref, pick_ref, weight_ref):
        turn = where_ref[1]
        numbers = lax.broadcasted_iota(jnp.int32, (groups, tok_rows), 0)
        routed = jnp.zeros((groups, tok_rows), F32)
        weight = jnp.zeros((groups, tok_rows), F32)
        for k in range(top):
            chosen = ids_ref[k : k + 1, :] == numbers
            routed = jnp.where(chosen, 1.0, routed)
            weight += jnp.where(chosen, gates_ref[k : k + 1, :], 0.0)
        first = lax.broadcasted_iota(jnp.int32, (tok_rows, tok_rows), 0)
        second = lax.broadcasted_iota(jnp.int32, (tok_rows, tok_rows), 1)
        earlier = jnp.where(first < second, 1.0, 0.0).astype(BF)
        order = jnp.dot(routed.astype(BF), earlier, preferred_element_type=F32)
        order = jnp.where(routed > 0.0, order, -1.0)
        places = lax.broadcasted_iota(jnp.int32, (capacity, tok_rows), 0).astype(F32)
        for g in range(groups):
            hits = order[g : g + 1, :] == places
            here = slice(g * capacity, (g + 1) * capacity)
            pick_ref[here] = jnp.where(hits, 1.0, 0.0).astype(BF)
            weight_ref[here] = jnp.sum(
                jnp.where(hits, weight[g : g + 1, :], 0.0), axis=1, keepdims=True
            )
        for s in range(count):
            source = shard_at(s, turn, count, width)
            x = jnp.dot(pick_ref[...], x_ref[:, source], preferred_element_type=F32).astype(BF)
            sent_ref[:, :, s * width : (s + 1) * width] = x.reshape(groups, capacity, width)

    return call(
        kernel,
        "dispatch_x",
        in_specs=[SMEM] + [VMEM] * 3,
        out_specs=[VMEM] * 3,
        out_shape=[
            shape(groups, capacity, model),
            shape(slots, tok_rows),
            shape(slots, 1, kind=F32),
        ],
    )(where, ids_t, gates_t, tokens)


def dispatch_dy(where, pick, weight, out_grad, groups, capacity):
    slots, tok_rows = pick.shape
    model = out_grad.shape[1]
    count = lax.axis_size("edata")
    width = model // count

    def kernel(where_ref, pick_ref, weight_ref, grad_ref, *refs):
        blocks, refs = refs[:groups], refs[groups:]
        rows_ref, relative_ref, weights_ref, all_rows_ref, dy_ref = refs
        me, turn = where_ref[0], where_ref[1]
        for s in range(count):
            source = shard_at(s, turn, count, width)
            here = slice(s * width, (s + 1) * width)
            rows = jnp.dot(pick_ref[...], grad_ref[:, source], preferred_element_type=F32)
            all_rows_ref[:, here] = rows.astype(BF)
            dy_ref[:, here] = (weight_ref[...] * rows).astype(BF)
        for j, block in enumerate(blocks):
            here = slice(j * capacity, (j + 1) * capacity)
            there = slots_of(j, me, capacity)
            block[...] = dy_ref[there, :]
            rows_ref[here] = all_rows_ref[there, :]
            relative_ref[here] = pick_ref[there, :]
            weights_ref[here] = weight_ref[there, :]

    results = call(
        kernel,
        "dispatch_dy",
        in_specs=[SMEM] + [VMEM] * 3,
        out_specs=[VMEM] * (groups + 3),
        out_shape=[
            *[shape(capacity, model)] * groups,
            shape(slots, model),
            shape(slots, tok_rows),
            shape(slots, 1, kind=F32),
        ],
        scratch_shapes=[pltpu.VMEM((slots, model), BF)] * 2,
    )(where, pick, weight, out_grad)
    return list(results[:groups]), *results[groups:]


def product(left, weights):
    width = weights[0].shape[0]
    total = None
    for s, shard in enumerate(weights):
        one = jnp.dot(
            left[:, s * width : (s + 1) * width], shard[...], preferred_element_type=F32
        )
        total = one if total is None else total + one
    return total


def expert_forward(where, got, w_ins, w_outs):
    groups, capacity, model = got.shape
    count = len(w_ins)
    width = model // count
    double, hidden = w_ins[0].shape[1], w_outs[0].shape[1]
    slots = groups * capacity
    many = max(1, 256 // capacity)

    def kernel(where_ref, got_ref, *refs):
        ins, outs, refs = refs[:count], refs[count : 2 * count], refs[2 * count :]
        sent, (act_ref, inner_ref, y_ref) = refs[:groups], refs[groups:]
        me = where_ref[0]
        for first in range(0, groups, many):
            theirs = slice(first, first + many)
            band = slice(first * capacity, (first + many) * capacity)
            x = got_ref[theirs].reshape(many * capacity, model)
            act_ref[band] = product(x, ins)
            act_gate = act_ref[band, :hidden]
            inner_ref[band] = (
                act_gate * jax.nn.sigmoid(act_gate) * act_ref[band, hidden:]
            ).astype(BF)
            for s in range(count):
                y_ref[band, s * width : (s + 1) * width] = lax.dot_general(
                    inner_ref[band], outs[s][...], COLS_IN, preferred_element_type=F32
                ).astype(BF)
        for j, block in enumerate(sent):
            block[...] = y_ref[slots_of(j, me, capacity), :]

    operands = (where, got, *w_ins, *w_outs)
    results = call(
        kernel,
        "expert_forward",
        cost=work(6 * slots * model * hidden),
        in_specs=[SMEM] + [VMEM] * (len(operands) - 1),
        out_specs=[VMEM] * (groups + 2),
        out_shape=[
            *[shape(capacity, model)] * groups,
            shape(slots, double, kind=F32),
            shape(slots, hidden),
        ],
        scratch_shapes=[pltpu.VMEM((slots, model), BF)],
    )(*operands)
    return list(results[:groups]), *results[groups:]


def expert_backward(where, blocks, act, w_ins, w_outs):
    groups = len(blocks)
    capacity, model = blocks[0].shape
    count = len(w_ins)
    width = model // count
    double, hidden = w_ins[0].shape[1], w_outs[0].shape[1]
    slots = groups * capacity
    rows = min(256, slots)

    def kernel(where_ref, *refs):
        got, act_ref, refs = refs[:groups], refs[groups], refs[groups + 1 :]
        ins, outs, refs = refs[:count], refs[count : 2 * count], refs[2 * count :]
        dx_ref, act_grad_ref, dy_ref = refs
        me = where_ref[0]
        for j, block in enumerate(got):
            dy_ref[slots_of(j, me, capacity), :] = block[...]
        for first in range(0, slots, rows):
            band = slice(first, first + rows)
            inner_grad = product(dy_ref[band], outs)
            act_gate = act_ref[band, :hidden]
            act_up = act_ref[band, hidden:]
            sig = jax.nn.sigmoid(act_gate)
            act_grad_ref[band, :hidden] = (
                inner_grad * act_up * sig * (1.0 + act_gate * (1.0 - sig))
            ).astype(BF)
            act_grad_ref[band, hidden:] = (inner_grad * (act_gate * sig)).astype(BF)
            for s in range(count):
                dx = lax.dot_general(
                    act_grad_ref[band], ins[s][...], COLS_IN, preferred_element_type=F32
                ).astype(BF)
                theirs = slice(first // capacity, (first + rows) // capacity)
                dx_ref[theirs, :, s * width : (s + 1) * width] = dx.reshape(-1, capacity, width)

    operands = (where, *blocks, act, *w_ins, *w_outs)
    return call(
        kernel,
        "expert_backward",
        cost=work(6 * slots * model * hidden),
        in_specs=[SMEM] + [VMEM] * (len(operands) - 1),
        out_specs=[VMEM] * 3,
        out_shape=[
            shape(groups, capacity, model),
            shape(slots, double),
            shape(slots, model),
        ],
    )(*operands)


def weight_grads(shard, got, dys, inner, act_grad):
    groups, capacity, _ = got.shape
    slots, model = dys.shape
    size = model // lax.axis_size("edata")
    double, hidden = act_grad.shape[1], inner.shape[1]
    tile = min(256, size)
    steps = size // tile

    def kernel(x_ref, dy_ref, inner_ref, act_grad_ref, out_ref):
        x = x_ref[...].reshape(slots, tile)
        out_ref[:, :double] = lax.dot_general(
            x, act_grad_ref[...], ROWS_IN, preferred_element_type=F32
        ).astype(BF)
        out_ref[:, double:] = lax.dot_general(
            dy_ref[...], inner_ref[...], ROWS_IN, preferred_element_type=F32
        ).astype(BF)

    return call(
        kernel,
        "weight_grads",
        cost=work(6 * slots * size * hidden),
        grid=(steps,),
        in_specs=[
            pl.BlockSpec((groups, capacity, tile), lambda i: (0, 0, shard * steps + i)),
            pl.BlockSpec((slots, tile), lambda i: (0, shard * steps + i)),
            pl.BlockSpec((slots, hidden), lambda i: (0, 0)),
            pl.BlockSpec((slots, double), lambda i: (0, 0)),
        ],
        out_specs=pl.BlockSpec((tile, double + hidden), lambda i: (i, 0)),
        out_shape=shape(size, double + hidden),
    )(got, dys, inner, act_grad)


def combine_y(where, picks, ids_t, grad_rows, blocks):
    pick, high_t, middle_t = picks
    slots, tok_rows = pick.shape
    groups = len(blocks)
    capacity, model = blocks[0].shape
    count = lax.axis_size("edata")
    width = model // count

    def kernel(where_ref, pick_ref, high_ref, middle_ref, ids_ref, grad_ref, *refs):
        blocks, (mixed_ref, gate_grad_ref) = refs[:groups], refs[groups:]
        me, turn = where_ref[0], where_ref[1]
        dots = jnp.zeros((slots, 1), F32)
        for s in range(count):
            here = slice(s * width, (s + 1) * width)
            y = jnp.concatenate([block[:, here] for block in blocks], axis=0)
            mixed_ref[:, shard_at(s, turn, count, width)] = (
                jnp.dot(high_ref[...], y, preferred_element_type=F32)
                + jnp.dot(middle_ref[...], y, preferred_element_type=F32)
            ).astype(BF)
            dots += jnp.sum(
                y.astype(F32) * grad_ref[:, here].astype(F32), axis=1, keepdims=True
            )
        by_token = pick_ref[...].astype(F32) * dots
        by_token = jnp.sum(by_token.reshape(groups, capacity, tok_rows), axis=1)
        ids = ids_ref[...]
        total = jnp.zeros(ids.shape, F32)
        for j in range(groups):
            total += jnp.where(ids == (me ^ j), by_token[j : j + 1], 0.0)
        gate_grad_ref[...] = total

    return call(
        kernel,
        "combine_y",
        in_specs=[SMEM] + [VMEM] * (5 + groups),
        out_specs=[VMEM] * 2,
        out_shape=[shape(tok_rows, model), shape(*ids_t.shape, kind=F32)],
    )(where, pick, high_t, middle_t, ids_t, grad_rows, *blocks)


def combine_dx(where, pick, rows):
    slots, tok_rows = pick.shape
    groups, capacity, model = rows.shape
    count = lax.axis_size("edata")
    tile = min(512, model // count)
    steps = model // tile

    def kernel(where_ref, pick_ref, rows_ref, out_ref):
        out_ref[...] = lax.dot_general(
            pick_ref[...], rows_ref[...].reshape(slots, tile), ROWS_IN, preferred_element_type=F32
        ).astype(BF)

    return call(
        kernel,
        "combine_dx",
        grid_spec=pltpu.PrefetchScalarGridSpec(
            num_scalar_prefetch=1,
            grid=(steps,),
            in_specs=[
                pl.BlockSpec((slots, tok_rows), lambda i, w: (0, 0)),
                pl.BlockSpec((groups, capacity, tile), lambda i, w: (0, 0, i)),
            ],
            out_specs=pl.BlockSpec(
                (tok_rows, tile), lambda i, w: (0, (i + w[1] * (steps // count)) % steps)
            ),
        ),
        out_shape=shape(tok_rows, model),
    )(where, pick, rows)


def shards(tokens, out_grad, expert_ids, gates, w_gate_up, w_down):
    groups = lax.axis_size("node") * lax.axis_size("local")
    tok_rows = tokens.shape[0]
    capacity = tok_rows * expert_ids.shape[1] // (EXP_DEV * groups)
    queued = min(5, groups - 1)
    where = jnp.stack([lax.axis_index(("node", "local")), lax.axis_index("edata")])
    where = where.astype(jnp.int32)
    w_ins = gathered(w_gate_up[0])
    w_outs = gathered(w_down[0])
    ids_t = expert_ids.T
    sent, pick, weight = dispatch_x(where, ids_t, gates.T, tokens, groups, capacity)
    got = to_all(sent)
    blocks, grad_rows, relative, weights = dispatch_dy(where, pick, weight, out_grad, groups, capacity)
    blocks = [blocks[0], *(after(b, *w_ins[1:], *w_outs[1:]) for b in blocks[1:])]
    dys = [blocks[0]]
    for j in range(1, groups):
        needs = (dys[j - queued],) if j > queued else ()
        if j == 2 * queued + 1:
            held = after(got, *dys[1 : queued + 1])
            y_sent, act, inner = expert_forward(where, held, w_ins, w_outs)
        if j > 2 * queued:
            needs += (inner,)
        dys.append(to_partner(after(blocks[j], *needs) if needs else blocks[j], j))
    dx_sent, act_grad, dy_rows = expert_backward(where, dys, act, w_ins, w_outs)
    ys = [y_sent[0]]
    for j in range(1, groups):
        needs = (ys[j - queued], dx_sent) if j > queued else (dys[groups - 1 - queued + j],)
        if j == 2 * queued + 1:
            held = after(inner, *ys[1 : queued + 1])
            parts = [
                weight_grads(shard, got, dy_rows, held, act_grad) for shard in range(1, len(w_ins))
            ]
        if j > 2 * queued:
            needs += tuple(parts)
        ys.append(to_partner(after(y_sent[j], *needs), j))
    dx_got = to_all(after(dx_sent, *ys[1:]))

    parts = [from_owner(p, step) for step, p in enumerate(parts, 1)]
    parts.append(weight_grads(0, got, dy_rows, after(inner, *ys[1:]), act_grad))
    double = w_gate_up.shape[2]
    sums = [
        sum(p[:, columns].astype(F32) for p in parts)
        for columns in (slice(0, double), slice(double, None))
    ]
    spread = relative.astype(F32) * after(weights, inner)
    high = lax.reduce_precision(spread, 8, 7)
    middle = (spread - high).astype(BF)
    mixed, gate_grad = combine_y(
        where, (relative, high.astype(BF).T, middle.T), ids_t, grad_rows, ys
    )
    held = lax.optimization_barrier((dx_got, *sums, mixed, gate_grad))
    dx_got, grad_in, grad_down, mixed, gate_grad = held
    token_grad = combine_dx(where, pick, dx_got)
    return (mixed, token_grad, gate_grad.T, grad_in[None], grad_down[None])


def solution(mesh):
    rows = P(("node", "local", "edata"), None)
    weights = P(("node", "local"), "edata", None)
    return jax.shard_map(
        shards,
        mesh=mesh,
        in_specs=(rows, rows, rows, rows, weights, weights),
        out_specs=(rows, rows, rows, weights, weights),
        check_vma=False,
    )
```

```python
import jax
import jax.numpy as jnp
from jax import lax
from jax.experimental import pallas as pl
from jax.experimental.pallas import tpu as pltpu
from jax.sharding import PartitionSpec as P

EXP_DEV = 4
BF = jnp.bfloat16
F32 = jnp.float32
ROWS_IN = (((0,), (0,)), ((), ()))
COLS_IN = (((1,), (1,)), ((), ()))
LIMIT = 56 * 1024 * 1024
def work(flops):
    return pl.CostEstimate(flops=flops, bytes_accessed=flops // 200, transcendentals=0)


CHEAP = pl.CostEstimate(flops=1, bytes_accessed=1, transcendentals=0)
VMEM = pl.BlockSpec(memory_space=pltpu.VMEM)
SMEM = pl.BlockSpec(memory_space=pltpu.SMEM)

def call(kernel, name, cost=CHEAP, **more):
    return pl.pallas_call(
        kernel,
        compiler_params=pltpu.CompilerParams(vmem_limit_bytes=LIMIT),
        cost_estimate=cost,
        name=name,
        **more,
    )


def shape(*dims, kind=BF):
    return jax.ShapeDtypeStruct(dims, kind)


def after(value, *others):
    return lax.optimization_barrier((value, *others))[0]


def gathered(shard):
    count = lax.axis_size("edata")
    shards = [shard]
    for step in range(1, count):
        pairs = [((i + step) % count, i) for i in range(count)]
        shards.append(lax.ppermute(shard, "edata", pairs))
    return shards


def from_owner(piece, step):
    count = lax.axis_size("edata")
    return lax.ppermute(piece, "edata", [(i, (i + step) % count) for i in range(count)])


def to_all(rows):
    return lax.all_to_all(rows, ("node", "local"), split_axis=0, concat_axis=0, tiled=True)


def to_partner(block, j):
    count = lax.axis_size("node") * lax.axis_size("local")
    return lax.ppermute(block, ("node", "local"), [(i, i ^ j) for i in range(count)])


def slots_of(j, me, capacity):
    return pl.ds(pl.multiple_of((me ^ j) * capacity, capacity), capacity)


def shard_at(s, turn, count, width):
    return pl.ds(pl.multiple_of((turn + s) % count * width, width), width)


def dispatch_x(where, ids_t, gates_t, tokens, groups, capacity):
    top, tok_rows = ids_t.shape
    model = tokens.shape[1]
    count = lax.axis_size("edata")
    width = model // count
    slots = groups * capacity

    def kernel(where_ref, ids_ref, gates_ref, x_ref, sent_ref, pick_ref, weight_ref):
        turn = where_ref[1]
        numbers = lax.broadcasted_iota(jnp.int32, (groups, tok_rows), 0)
        routed = jnp.zeros((groups, tok_rows), F32)
        weight = jnp.zeros((groups, tok_rows), F32)
        for k in range(top):
            chosen = ids_ref[k : k + 1, :] == numbers
            routed = jnp.where(chosen, 1.0, routed)
            weight += jnp.where(chosen, gates_ref[k : k + 1, :], 0.0)
        first = lax.broadcasted_iota(jnp.int32, (tok_rows, tok_rows), 0)
        second = lax.broadcasted_iota(jnp.int32, (tok_rows, tok_rows), 1)
        earlier = jnp.where(first < second, 1.0, 0.0).astype(BF)
        order = jnp.dot(routed.astype(BF), earlier, preferred_element_type=F32)
        order = jnp.where(routed > 0.0, order, -1.0)
        places = lax.broadcasted_iota(jnp.int32, (capacity, tok_rows), 0).astype(F32)
        for g in range(groups):
            hits = order[g : g + 1, :] == places
            here = slice(g * capacity, (g + 1) * capacity)
            pick_ref[here] = jnp.where(hits, 1.0, 0.0).astype(BF)
            weight_ref[here] = jnp.sum(
                jnp.where(hits, weight[g : g + 1, :], 0.0), axis=1, keepdims=True
            )
        for s in range(count):
            source = shard_at(s, turn, count, width)
            x = jnp.dot(pick_ref[...], x_ref[:, source], preferred_element_type=F32).astype(BF)
            sent_ref[:, :, s * width : (s + 1) * width] = x.reshape(groups, capacity, width)

    return call(
        kernel,
        "dispatch_x",
        in_specs=[SMEM] + [VMEM] * 3,
        out_specs=[VMEM] * 3,
        out_shape=[
            shape(groups, capacity, model),
            shape(slots, tok_rows),
            shape(slots, 1, kind=F32),
        ],
    )(where, ids_t, gates_t, tokens)


def dispatch_dy(where, pick, weight, out_grad, groups, capacity):
    slots, tok_rows = pick.shape
    model = out_grad.shape[1]
    count = lax.axis_size("edata")
    width = model // count

    def kernel(where_ref, pick_ref, weight_ref, grad_ref, *refs):
        blocks, (rows_ref, relative_ref, dy_ref) = refs[:groups], refs[groups:]
        me, turn = where_ref[0], where_ref[1]
        for s in range(count):
            source = shard_at(s, turn, count, width)
            here = slice(s * width, (s + 1) * width)
            rows = jnp.dot(pick_ref[...], grad_ref[:, source], preferred_element_type=F32)
            rows_ref[:, here] = rows.astype(BF)
            dy_ref[:, here] = (weight_ref[...] * rows).astype(BF)
        for j, block in enumerate(blocks):
            block[...] = dy_ref[slots_of(j, me, capacity), :]
            relative_ref[j * capacity : (j + 1) * capacity] = pick_ref[slots_of(j, me, capacity), :]

    results = call(
        kernel,
        "dispatch_dy",
        in_specs=[SMEM] + [VMEM] * 3,
        out_specs=[VMEM] * (groups + 2),
        out_shape=[
            *[shape(capacity, model)] * groups,
            shape(slots, model),
            shape(slots, tok_rows),
        ],
        scratch_shapes=[pltpu.VMEM((slots, model), BF)],
    )(where, pick, weight, out_grad)
    return list(results[:groups]), *results[groups:]


def product(left, weights):
    width = weights[0].shape[0]
    total = None
    for s, shard in enumerate(weights):
        one = jnp.dot(
            left[:, s * width : (s + 1) * width], shard[...], preferred_element_type=F32
        )
        total = one if total is None else total + one
    return total


def expert_forward(got, w_ins, w_outs):
    groups, capacity, model = got.shape
    count = len(w_ins)
    width = model // count
    double, hidden = w_ins[0].shape[1], w_outs[0].shape[1]
    slots = groups * capacity
    many = max(1, 256 // capacity)

    def kernel(got_ref, *refs):
        ins, outs, (y_ref, act_ref, inner_ref) = refs[:count], refs[count:-3], refs[-3:]
        for first in range(0, groups, many):
            theirs = slice(first, first + many)
            band = slice(first * capacity, (first + many) * capacity)
            x = got_ref[theirs].reshape(many * capacity, model)
            act_ref[band] = product(x, ins)
            act_gate = act_ref[band, :hidden]
            inner_ref[band] = (
                act_gate * jax.nn.sigmoid(act_gate) * act_ref[band, hidden:]
            ).astype(BF)
            for s in range(count):
                y = lax.dot_general(
                    inner_ref[band], outs[s][...], COLS_IN, preferred_element_type=F32
                ).astype(BF)
                y_ref[theirs, :, s * width : (s + 1) * width] = y.reshape(many, capacity, width)

    operands = (got, *w_ins, *w_outs)
    return call(
        kernel,
        "expert_forward",
        cost=work(6 * slots * model * hidden),
        in_specs=[VMEM] * len(operands),
        out_specs=[VMEM] * 3,
        out_shape=[
            shape(groups, capacity, model),
            shape(slots, double, kind=F32),
            shape(slots, hidden),
        ],
    )(*operands)


def expert_backward(where, blocks, act, w_ins, w_outs):
    groups = len(blocks)
    capacity, model = blocks[0].shape
    count = len(w_ins)
    width = model // count
    double, hidden = w_ins[0].shape[1], w_outs[0].shape[1]
    slots = groups * capacity
    rows = min(256, slots)

    def kernel(where_ref, *refs):
        got, act_ref, refs = refs[:groups], refs[groups], refs[groups + 1 :]
        ins, outs, refs = refs[:count], refs[count : 2 * count], refs[2 * count :]
        sent, (act_grad_ref, dy_ref, dx_ref) = refs[:groups], refs[groups:]
        me = where_ref[0]
        for j, block in enumerate(got):
            dy_ref[slots_of(j, me, capacity), :] = block[...]
        for first in range(0, slots, rows):
            band = slice(first, first + rows)
            inner_grad = product(dy_ref[band], outs)
            act_gate = act_ref[band, :hidden]
            act_up = act_ref[band, hidden:]
            sig = jax.nn.sigmoid(act_gate)
            act_grad_ref[band, :hidden] = (
                inner_grad * act_up * sig * (1.0 + act_gate * (1.0 - sig))
            ).astype(BF)
            act_grad_ref[band, hidden:] = (inner_grad * (act_gate * sig)).astype(BF)
            for s in range(count):
                dx_ref[band, s * width : (s + 1) * width] = lax.dot_general(
                    act_grad_ref[band], ins[s][...], COLS_IN, preferred_element_type=F32
                ).astype(BF)
        for j, block in enumerate(sent):
            block[...] = dx_ref[slots_of(j, me, capacity), :]

    operands = (where, *blocks, act, *w_ins, *w_outs)
    results = call(
        kernel,
        "expert_backward",
        cost=work(6 * slots * model * hidden),
        in_specs=[SMEM] + [VMEM] * (len(operands) - 1),
        out_specs=[VMEM] * (groups + 2),
        out_shape=[
            *[shape(capacity, model)] * groups,
            shape(slots, double),
            shape(slots, model),
        ],
        scratch_shapes=[pltpu.VMEM((slots, model), BF)],
    )(*operands)
    return list(results[:groups]), *results[groups:]


def weight_grads(shard, got, dys, inner, act_grad):
    groups, capacity, _ = got.shape
    slots, model = dys.shape
    size = model // lax.axis_size("edata")
    double, hidden = act_grad.shape[1], inner.shape[1]
    tile = min(256, size)
    steps = size // tile

    def kernel(x_ref, dy_ref, inner_ref, act_grad_ref, out_ref):
        x = x_ref[...].reshape(slots, tile)
        out_ref[:, :double] = lax.dot_general(
            x, act_grad_ref[...], ROWS_IN, preferred_element_type=F32
        ).astype(BF)
        out_ref[:, double:] = lax.dot_general(
            dy_ref[...], inner_ref[...], ROWS_IN, preferred_element_type=F32
        ).astype(BF)

    return call(
        kernel,
        "weight_grads",
        cost=work(6 * slots * size * hidden),
        grid=(steps,),
        in_specs=[
            pl.BlockSpec((groups, capacity, tile), lambda i: (0, 0, shard * steps + i)),
            pl.BlockSpec((slots, tile), lambda i: (0, shard * steps + i)),
            pl.BlockSpec((slots, hidden), lambda i: (0, 0)),
            pl.BlockSpec((slots, double), lambda i: (0, 0)),
        ],
        out_specs=pl.BlockSpec((tile, double + hidden), lambda i: (i, 0)),
        out_shape=shape(size, double + hidden),
    )(got, dys, inner, act_grad)


def combine_y(where, picks, ids_t, grad_rows, rows):
    pick, high_t, middle_t = picks
    slots, tok_rows = pick.shape
    groups, capacity, model = rows.shape
    count = lax.axis_size("edata")
    width = model // count

    def kernel(where_ref, pick_ref, high_ref, middle_ref, ids_ref, grad_ref, *refs):
        y_ref, mixed_ref, gate_grad_ref = refs
        turn = where_ref[1]
        dots = jnp.zeros((slots, 1), F32)
        for s in range(count):
            here = slice(s * width, (s + 1) * width)
            y = y_ref[:, :, here].reshape(slots, width)
            mixed_ref[:, shard_at(s, turn, count, width)] = (
                jnp.dot(high_ref[...], y, preferred_element_type=F32)
                + jnp.dot(middle_ref[...], y, preferred_element_type=F32)
            ).astype(BF)
            dots += jnp.sum(
                y.astype(F32) * grad_ref[:, here].astype(F32), axis=1, keepdims=True
            )
        by_token = pick_ref[...].astype(F32) * dots
        by_token = jnp.sum(by_token.reshape(groups, capacity, tok_rows), axis=1)
        ids = ids_ref[...]
        total = jnp.zeros(ids.shape, F32)
        for g in range(groups):
            total += jnp.where(ids == g, by_token[g : g + 1], 0.0)
        gate_grad_ref[...] = total

    return call(
        kernel,
        "combine_y",
        in_specs=[SMEM] + [VMEM] * 6,
        out_specs=[VMEM] * 2,
        out_shape=[shape(tok_rows, model), shape(*ids_t.shape, kind=F32)],
    )(where, pick, high_t, middle_t, ids_t, grad_rows, rows)


def combine_dx(where, relative_t, blocks):
    tok_rows, slots = relative_t.shape
    capacity, model = blocks[0].shape
    count = lax.axis_size("edata")
    width = model // count

    def kernel(where_ref, relative_ref, *refs):
        blocks, out_ref = refs[:-1], refs[-1]
        for s in range(count):
            here = slice(s * width, (s + 1) * width)
            dx = jnp.concatenate([block[:, here] for block in blocks], axis=0)
            out_ref[:, shard_at(s, where_ref[1], count, width)] = jnp.dot(
                relative_ref[...], dx, preferred_element_type=F32
            ).astype(BF)

    return call(
        kernel,
        "combine_dx",
        in_specs=[SMEM] + [VMEM] * (1 + len(blocks)),
        out_specs=VMEM,
        out_shape=shape(tok_rows, model),
    )(where, relative_t, *blocks)


def shards(tokens, out_grad, expert_ids, gates, w_gate_up, w_down):
    groups = lax.axis_size("node") * lax.axis_size("local")
    tok_rows = tokens.shape[0]
    capacity = tok_rows * expert_ids.shape[1] // (EXP_DEV * groups)
    queued = min(5, groups - 1)
    where = jnp.stack([lax.axis_index(("node", "local")), lax.axis_index("edata")])
    where = where.astype(jnp.int32)
    w_ins = gathered(w_gate_up[0])
    w_outs = gathered(w_down[0])
    ids_t = expert_ids.T
    sent, pick, weight = dispatch_x(where, ids_t, gates.T, tokens, groups, capacity)
    got = to_all(sent)
    blocks, grad_rows, relative = dispatch_dy(where, pick, weight, out_grad, groups, capacity)
    blocks = [blocks[0], *(after(b, *w_ins[1:], *w_outs[1:]) for b in blocks[1:])]
    dys = [blocks[0]]
    for j in range(1, groups):
        needs = (dys[j - queued],) if j > queued else ()
        dys.append(to_partner(after(blocks[j], *needs) if needs else blocks[j], j))
    held = after(got, *dys[1 : groups - queued])
    y_sent, act, inner = expert_forward(held, w_ins, w_outs)
    y_got = to_all(after(y_sent, *dys[1:]))
    dxs, act_grad, dy_rows = expert_backward(where, dys, act, w_ins, w_outs)
    backs = [dxs[0]]
    for j in range(1, groups):
        needs = (y_got, backs[j - queued]) if j > queued else ()
        backs.append(to_partner(after(dxs[j], *needs) if needs else dxs[j], j))

    parts = []
    for shard in [*range(1, len(w_ins)), 0]:
        parts.append(weight_grads(shard, got, dy_rows, inner, act_grad))
    *parts, y_got = lax.optimization_barrier((*parts, y_got))
    parts = [parts[-1]] + [from_owner(p, step) for step, p in enumerate(parts[:-1], 1)]
    double = w_gate_up.shape[2]
    sums = [
        sum(p[:, columns].astype(F32) for p in parts)
        for columns in (slice(0, double), slice(double, None))
    ]
    spread = pick.astype(F32) * after(weight, inner)
    high = lax.reduce_precision(spread, 8, 7)
    middle = (spread - high).astype(BF)
    mixed, gate_grad = combine_y(
        where, (pick, high.astype(BF).T, middle.T), ids_t, grad_rows, y_got
    )
    held = lax.optimization_barrier((*backs, *sums, mixed, gate_grad, relative.T))
    *backs, grad_in, grad_down, mixed, gate_grad, relative_t = held
    token_grad = combine_dx(where, relative_t, backs)
    return (mixed, token_grad, gate_grad.T, grad_in[None], grad_down[None])


def solution(mesh):
    rows = P(("node", "local", "edata"), None)
    weights = P(("node", "local"), "edata", None)
    return jax.shard_map(
        shards,
        mesh=mesh,
        in_specs=(rows, rows, rows, rows, weights, weights),
        out_specs=(rows, rows, rows, weights, weights),
        check_vma=False,
    )
```
